128 devices in a mesh: section: 32 (over z, x, core), dp: 4 (over y).
Axes of the slice: x: 4, y: 4, z: 4, core: 2. Of those that a mesh axis runs over, the one named last changes fastest.
Arguments:
- video_ids: int32 [32, 32], P('dp'), may hold values from 0 to 1023
- action_ids: int32 [32, 32], P('dp'), may hold values from 0 to 7
- target_ids: int32 [32, 32], P('dp'), may hold values from 0 to 1023
- live_lengths: int32 [4, 8], P('dp'), may hold values from 1 to 32, 160 in all within a row
- video_table: bfloat16 [1024, 2048], replicated, may hold values from -25 to 25
- action_table: bfloat16 [8, 2048], replicated, may hold values from -6 to 6
- layer_gain: float32 [32, 2048], P('section'), may hold values from 0.1 to 1.9
- layer_weight: bfloat16 [32, 2048, 2048], P('section', 'dp'), may hold values from -0.125 to 0.125
- out_gain: float32 [2048], replicated, may hold values from 0.1 to 1.9
- head_weight: bfloat16 [2048, 1024], replicated, may hold values from -32 to 32
Outputs:
- loss: float32 [], replicated
- weight_grad: float32 [32, 2048, 2048], P('section', 'dp')
The draws below stay inside these ranges and needn't reach their ends.
Inputs may be any that keep to these rules, and one draw needn't show every extreme that they name: Each row of live_lengths sums to 160.
All inputs are finite; a program needn't handle non-finite values.
Results may differ from the reference program's by a relative error of at most 0.015.
Values may be sent and summed in bfloat16 or wider, within the bound.
A program may use at most 128 MiB of HBM per device.

```python
import math
import jax
import jax.numpy as jnp
import numpy as np
from jax import lax

D = 2048
V = 1024
A = 8
M = 8
TOK = 32
LAYERS = 32
BATCHES = 32
N_DP = 4


def draw_video_table(key, part):
    key = jax.random.fold_in(key, 11)
    keys = jax.random.split(key, 3)
    row_scale = jnp.exp(jax.random.uniform(keys[1], (V, 1), jnp.float32, -1.15, 1.15))
    column_scale = jnp.exp(jax.random.uniform(keys[2], (1, D), jnp.float32, -1.15, 1.15))
    base_draw = jnp.clip(jax.random.normal(keys[0], (V, D), jnp.float32), -5.0, 5.0)
    return (base_draw * row_scale * column_scale * 0.5).astype(jnp.bfloat16)


def draw_head_weight(key, part):
    key = jax.random.fold_in(key, 23)
    keys = jax.random.split(key, 1)
    base_draw = jnp.clip(jax.random.normal(keys[0], (D, V), jnp.float32), -6.0, 6.0) * (3.0 * D ** (-0.5))
    return jnp.clip(base_draw, -32.0, 32.0).astype(jnp.bfloat16)


def with_ends(entries, key, least, high):
    shape = entries.shape
    spot = [jax.random.randint(jax.random.fold_in(key, axis), (), 0, shape[axis]) for axis in range(len(shape))]
    entries = entries.at[tuple(spot)].set(least)
    longest = shape.index(max(shape))
    spot[longest] = (spot[longest] + 1) % shape[longest]
    return entries.at[tuple(spot)].set(high)


def steps_of(key, dims, cuts, smallest, top_value):
    level, own = 1.0, jax.random.fold_in(key, 6)
    for dim, parts in cuts:
        heights = jnp.exp(jax.random.uniform(jax.random.fold_in(own, dim), (parts,), jnp.float32, smallest / len(cuts), top_value / len(cuts)))
        level = level * jnp.repeat(heights, dims[dim] // parts).reshape([-1 if axis == dim else 1 for axis in range(len(dims))])
    return level


def rank_table(count, lean):
    portions = [(1 << 20) // math.isqrt(grade ** lean) + 1 for grade in range(1, count + 1)]
    width = 1 + sum(portions) // (1 << 30)
    return np.cumsum(np.array([max(1, weight // width) for weight in portions]))


def ranked_ids(key, extent, count, lean):
    grid = rank_table(count, lean)
    ticket = jax.random.randint(jax.random.fold_in(key, 1), extent, 0, int(grid[count - 1]))
    standing = jnp.searchsorted(jnp.asarray(grid, jnp.int32), ticket, side="right")
    return jax.random.permutation(jax.random.fold_in(key, 2), count)[standing].astype(jnp.int32)


def length_profile(amount, total, limit, lean):
    portions = [(1 << 20) // math.isqrt(rank ** lean) + 1 for rank in range(2, amount + 1)]
    spare, holding = total - limit - (amount - 1), [1] * (amount - 1)
    while spare > 0:
        candidates = [i for i in range(amount - 1) if holding[i] < limit]
        pool, budget = sum([portions[i] for i in candidates]), spare
        for i in candidates:
            more = min(limit - holding[i], max(1, budget * portions[i] // pool), spare)
            holding[i] = holding[i] + more
            spare = spare - more
    return np.array([limit] + holding)


def ragged_sizes(stream_key, number_of, total, most, lean):
    if number_of == 2:
        one = jax.random.randint(stream_key, (), max(1, total - most), min(most, total - 1) + 1)
        return jnp.stack([one, total - one])
    sizes = jnp.asarray(length_profile(number_of, total, most, lean), jnp.int32)
    pairs = (number_of - 1) // 2
    source_of, receiver = sizes[1:1 + 2 * pairs:2], sizes[2:2 + 2 * pairs:2]
    slack = jnp.minimum(source_of - 1, most - receiver)
    passed = jax.random.randint(jax.random.fold_in(stream_key, 1), (pairs,), 0, 1 << 20) % (slack + 1)
    sizes = sizes.at[1:1 + 2 * pairs:2].set(source_of - passed).at[2:2 + 2 * pairs:2].set(receiver + passed)
    return sizes[jax.random.permutation(jax.random.fold_in(stream_key, 2), number_of)]


def normal_values(key, extent, deviation, most, shards=(), kind=jnp.bfloat16):
    values = jax.random.normal(key, extent, jnp.float32) * deviation
    if len(shards) > 0:
        values = steps_of(key, extent, shards, -0.22, 0.18) * values
    return jnp.clip(values, min=-most, max=most).astype(kind)


def setup_inputs(seed: int = 0) -> dict:
    arg_keys = jax.random.split(jax.random.key(seed), 11)
    return {
        "video_ids": with_ends(ranked_ids(arg_keys[0], (BATCHES, TOK), V, 2), jax.random.fold_in(arg_keys[0], 3), 0, V - 1).astype(jnp.int32),
        "action_ids": with_ends(jax.random.randint(arg_keys[1], (BATCHES, TOK), 0, A), jax.random.fold_in(arg_keys[1], 1), 0, A - 1).astype(jnp.int32),
        "target_ids": with_ends(ranked_ids(arg_keys[2], (BATCHES, TOK), V, 1), jax.random.fold_in(arg_keys[2], 3), 0, V - 1).astype(jnp.int32),
        "live_lengths": jax.vmap(lambda own: ragged_sizes(own, M, 5 * TOK, TOK, 2))(jax.random.split(arg_keys[3], N_DP)).reshape((N_DP, M)).astype(jnp.int32),
        "video_table": draw_video_table(jax.random.fold_in(arg_keys[10], 71), 0),
        "action_table": normal_values(arg_keys[5], (A, D), 1.0, 6.0),
        "layer_gain": jnp.clip(1.0 + 0.18 * jax.random.normal(arg_keys[6], (LAYERS, D), jnp.float32), 0.1, 1.9),
        "layer_weight": normal_values(arg_keys[7], (LAYERS, D, D), D ** -0.5, 0.125, ((0, 32), (1, 4))),
        "out_gain": jnp.clip(1.0 + 0.18 * jax.random.normal(arg_keys[8], (D,), jnp.float32), 0.1, 1.9),
        "head_weight": draw_head_weight(jax.random.fold_in(arg_keys[10], 71), 0),
    }


def norm_rows(hidden, scale_vector):
    widened = hidden.astype(jnp.float32)
    inverse = lax.rsqrt(lax.optimization_barrier(jnp.mean(widened * widened, axis=-1, keepdims=True)) + 1e-05)
    return widened * inverse * scale_vector

def contract_rows(left, right):
    return lax.dot_general(left, right, (((0,), (0,)), ((), ())), preferred_element_type=jnp.float32)

def times_transpose(left, right):
    return lax.dot_general(left, right, (((1,), (1,)), ((), ())), preferred_element_type=jnp.float32)

def layer_forward(hidden, scale_vector, weight):
    normed = norm_rows(hidden, scale_vector).astype(jnp.bfloat16)
    pre_act = jnp.dot(normed, weight, preferred_element_type=jnp.float32)
    result = (hidden.astype(jnp.float32) + jax.nn.gelu(pre_act)).astype(jnp.bfloat16)
    return (result, normed, pre_act)

def layer_backward(hidden, scale_vector, weight, pre_act, cotangent):
    widened = cotangent.astype(jnp.float32)
    _, gelu_back = jax.vjp(jax.nn.gelu, pre_act)
    d_pre = gelu_back(widened)[0].astype(jnp.bfloat16)
    d_normed = times_transpose(d_pre, weight)
    _, norm_back = jax.vjp(lambda rows_in: norm_rows(rows_in, scale_vector), hidden.astype(jnp.float32))
    d_hidden = (widened + norm_back(d_normed)[0]).astype(jnp.bfloat16)
    return (d_hidden, d_pre)

def head_terms(final_rows, out_gain, head_weight, targets, live_mask):
    normed = norm_rows(final_rows, out_gain).astype(jnp.bfloat16)
    logits = jnp.dot(normed, head_weight, preferred_element_type=jnp.float32)
    row_max = lax.optimization_barrier(jnp.max(logits, axis=-1, keepdims=True))
    exponents = jnp.exp(logits - row_max)
    denominator = lax.optimization_barrier(jnp.sum(exponents, axis=-1, keepdims=True))
    one_hot = (targets[:, None] == lax.broadcasted_iota(jnp.int32, logits.shape, 1)).astype(jnp.float32)
    picked = lax.optimization_barrier(jnp.sum(logits * one_hot, axis=-1))
    losses = (jnp.log(denominator[:, 0]) + row_max[:, 0] - picked) * live_mask
    d_logits = ((exponents / denominator - one_hot) * live_mask[:, None]).astype(jnp.bfloat16)
    d_normed = times_transpose(d_logits, head_weight)
    _, norm_back = jax.vjp(lambda rows_in: norm_rows(rows_in, out_gain), final_rows.astype(jnp.float32))
    d_final = norm_back(d_normed)[0].astype(jnp.bfloat16)
    return (jnp.sum(losses), jnp.sum(live_mask), d_final)

def reference(video_ids, action_ids, target_ids, live_lengths, video_table, action_table, layer_gain, layer_weight, out_gain, head_weight):
    embedded = (jnp.take(video_table, video_ids.reshape(-1), axis=0).astype(jnp.float32) + jnp.take(action_table, action_ids.reshape(-1), axis=0).astype(jnp.float32)).astype(jnp.bfloat16)
    positions = lax.broadcasted_iota(jnp.int32, video_ids.shape, 1)
    live_mask = (positions < live_lengths.reshape(-1)[:, None]).astype(jnp.float32).reshape(-1)

    def forward_layer(hidden, layer):
        scale_vector, weight = layer
        result, normed, pre_act = layer_forward(hidden, scale_vector, weight)
        return (result, (hidden, normed, pre_act))
    final_rows, saved = lax.scan(forward_layer, embedded, (layer_gain, layer_weight))
    loss_sum, live_count, d_final = head_terms(final_rows, out_gain, head_weight, target_ids.reshape(-1), live_mask)

    def backward_layer(cotangent, layer):
        hidden, normed, pre_act, scale_vector, weight = layer
        d_hidden, d_pre = layer_backward(hidden, scale_vector, weight, pre_act, cotangent)
        return (d_hidden, contract_rows(normed, d_pre))
    _, weight_grad = lax.scan(backward_layer, d_final, saved + (layer_gain, layer_weight), reverse=True)
    return (loss_sum / live_count, weight_grad)
```

```python
import functools

import jax
import jax.numpy as jnp
from jax import lax
from jax.experimental import pallas as pl
from jax.experimental.pallas import tpu as pltpu
from jax.sharding import PartitionSpec as P

MESH = pl.DeviceIdType.MESH
F32 = jnp.float32
BF16 = jnp.bfloat16
ROWS = 16
CUTS = 4
PRE_SCALE = 0.7978845608028654
CUBE = 0.044715


def gelu(x):
    return 0.5 * x * (1.0 + jnp.tanh(PRE_SCALE * (x + CUBE * x * x * x)))


def gelu_slope(x):
    t = jnp.tanh(PRE_SCALE * (x + CUBE * x * x * x))
    return 0.5 * (1.0 + t) + 0.5 * x * (1.0 - t * t) * (PRE_SCALE * (1.0 + 3.0 * CUBE * x * x))


def dot(left, right):
    return jnp.dot(left, right, preferred_element_type=F32)


def row_sum(x):
    return jnp.sum(x, axis=1, keepdims=True)


def kernel(
    lengths_ref,
    ids_ref,
    gains_ref,
    out_gain_ref,
    actions_ref,
    video_ref,
    weight_ref,
    head_ref,
    loss_ref,
    normed_out,
    dpre_out,
    w,
    wt,
    hw,
    ht,
    h_in,
    h_mid,
    h_out,
    pre,
    normed,
    dpre,
    g_in,
    g_out,
    dlog,
    acc,
    slope,
    inv_keep,
    picked_ids,
    loss_part,
    loss_in,
    loss_all,
    w_send,
    w_recv,
    w_fwd_send,
    w_fwd_recv,
    local_sem,
    h_send,
    h_recv,
    g_send,
    g_recv,
    peer_send,
    peer_recv,
    n_send,
    n_recv,
    d_send,
    d_recv,
    part_send,
    part_recv,
    loss_send,
    loss_recv,
):
    s = lax.axis_index("section")
    y = lax.axis_index("dp")
    planes = lax.axis_size("section") // 2
    k = s // 2
    core = s % 2
    forward = core == 1
    backward = core == 0
    first = k == 0
    last = k == planes - 1
    not_first = k > 0
    not_last = k < planes - 1

    width = w.shape[2]
    share = width // 4
    half = share // 2
    step = width // CUTS
    count = h_in.shape[0]
    vocab = hw.shape[1]

    up, down, far = (y + 1) % 4, (y + 3) % 4, (y + 2) % 4
    peer = (2 * k + 1 - core, y)
    odd = 2 * k + 1
    even = 2 * k

    def remote(src, dst, send, recv, device):
        return pltpu.make_async_remote_copy(
            src_ref=src, dst_ref=dst, send_sem=send, recv_sem=recv, device_id=device, device_id_type=MESH
        )

    barrier = pltpu.get_barrier_semaphore()
    for other in (up, down, far):
        for c in (0, 1):
            pl.semaphore_signal(barrier, inc=1, device_id=(2 * k + c, other), device_id_type=MESH)
    pl.semaphore_signal(barrier, inc=1, device_id=peer, device_id_type=MESH)

    sections = 2 * planes
    for other in ((s + 2) % sections, (s + sections - 2) % sections):
        pl.semaphore_signal(barrier, inc=1, device_id=(other, y), device_id_type=MESH)
    pl.semaphore_wait(barrier, 9)

    def rows_of(owner, part=None):
        if part is None:
            return pl.ds(pl.multiple_of(owner * share, share), share)
        return pl.ds(pl.multiple_of(owner * share + part * half, half), half)

    def direct(layer, lane, part):
        target = up if lane == 1 else down
        return remote(
            weight_ref.at[0, part * half : (part + 1) * half, :],
            w.at[layer, rows_of(y, part), :],
            w_send.at[lane, part],
            w_recv.at[layer, lane, part],
            (odd, target),
        )

    def relay(layer, part):
        owner, target = (down, up) if part == 0 else (up, down)
        block = w.at[layer, rows_of(owner, part), :]
        return remote(block, block, w_send.at[3, 2 * layer + part], w_recv.at[layer, 3, part], (odd, target))

    def to_peer(layer, lane, owner):
        block = w.at[layer, rows_of(owner), :]
        return remote(block, block, w_fwd_send.at[layer, lane], w_fwd_recv.at[layer, lane], peer)

    def own_to_peer(layer):
        return remote(
            weight_ref.at[0], w.at[layer, rows_of(y), :], w_fwd_send.at[layer, 0], w_fwd_recv.at[layer, 0], peer
        )

    def own_local(layer):
        return pltpu.make_async_copy(weight_ref.at[0], w.at[layer, rows_of(y), :], local_sem.at[0])

    def start_own(layer):
        direct(layer, 1, 0).start()
        direct(layer, 2, 1).start()
        direct(layer, 1, 1).start()
        direct(layer, 2, 0).start()
        own_to_peer(layer).start()
        own_local(layer).start()

    @pl.when(forward)
    def _():
        start_own(1)

    @pl.when(backward)
    def _():
        start_own(0)

    @pl.when(last)
    def _():
        pltpu.make_async_copy(head_ref, hw, local_sem.at[1]).start()

    @pl.when(jnp.logical_and(first, forward))
    def _():
        pltpu.make_async_copy(video_ref, ht, local_sem.at[1]).start()

    total = count * ROWS
    slots = ids_ref.shape[2]
    place = lax.broadcasted_iota(jnp.int32, (total, slots), 0)
    lane_of = lax.broadcasted_iota(jnp.int32, (total, slots), 1)
    chosen = [jnp.zeros((total, 1), jnp.int32) for _ in range(3)]
    start = jnp.int32(0)
    for b in range(ids_ref.shape[1]):
        length = lengths_ref[0, b]
        hit = jnp.logical_and(place == start + lane_of, lane_of < length)
        for kind in range(3):
            line = jnp.broadcast_to(ids_ref[kind, b : b + 1, :], (total, slots))
            chosen[kind] = chosen[kind] + row_sum(jnp.where(hit, line, 0))
        start = start + length
    picked_ids[...] = jnp.broadcast_to(chosen[2], picked_ids.shape)

    @pl.when(jnp.logical_and(first, forward))
    def _():
        pltpu.make_async_copy(video_ref, ht, local_sem.at[1]).wait()
        video_hot = (chosen[0] == lax.broadcasted_iota(jnp.int32, (total, ht.shape[0]), 1)).astype(F32).astype(BF16)
        kinds = actions_ref.shape[0]
        for j in range(CUTS):
            cols = slice(j * step, (j + 1) * step)
            rows = dot(video_hot, ht[:, cols])
            for a in range(kinds):
                rows = rows + jnp.where(chosen[1] == a, actions_ref[a : a + 1, cols].astype(F32), 0.0)
            h_in[:, :, cols] = rows.astype(BF16).reshape(count, ROWS, step)

    @pl.when(forward)
    def _():
        for layer in range(2):
            direct(layer, 1, 0).wait_recv()
            relay(layer, 0).start()
            direct(layer, 2, 1).wait_recv()
            relay(layer, 1).start()
        for layer in range(2):
            direct(layer, 1, 1).wait_recv()
            to_peer(layer, 1, down).start()
            direct(layer, 2, 0).wait_recv()
            to_peer(layer, 2, up).start()
        for layer in range(2):
            relay(layer, 0).wait_recv()
            relay(layer, 1).wait_recv()
            to_peer(layer, 3, far).start()
        own_local(1).wait()
        own_to_peer(0).wait_recv()

    @pl.when(jnp.logical_and(last, forward))
    def _():
        pltpu.make_async_copy(head_ref, hw, local_sem.at[1]).wait()

    block = min(512, width)

    def turn(layer, owner):
        def one(i, carry):
            cols = pl.ds(pl.multiple_of(i * block, block), block)
            wt[layer, cols, rows_of(owner)] = w[layer, rows_of(owner), cols].T
            return carry

        lax.fori_loop(0, width // block, one, 0)

    @pl.when(backward)
    def _():
        own_local(0).wait()
        turn(0, y)
        own_to_peer(1).wait_recv()
        turn(1, y)
        for lane, owner in ((1, down), (2, up), (3, far)):
            for layer in range(2):
                to_peer(layer, lane, owner).wait_recv()
                turn(layer, owner)

    @pl.when(jnp.logical_and(last, backward))
    def _():
        pltpu.make_async_copy(head_ref, hw, local_sem.at[1]).wait()
        for i in range(CUTS):
            ht[:, i * step : (i + 1) * step] = hw[i * step : (i + 1) * step, :].T

    def h_piece(mb, j):
        cols = pl.ds(j * step, step)
        return remote(
            h_out.at[mb, :, cols], h_in.at[mb, :, cols], h_send.at[j], h_recv.at[mb, j], (s + 2, y)
        )

    def peer_copies(mb):
        refs = [h_in, h_mid, pre.at[0], pre.at[1]]
        return [
            remote(ref.at[mb], ref.at[mb], peer_send.at[i], peer_recv.at[i, mb], peer) for i, ref in enumerate(refs)
        ]

    def head_copies(mb):
        return [
            remote(ref.at[mb], ref.at[mb], peer_send.at[4 + i], peer_recv.at[4 + i, mb], peer)
            for i, ref in enumerate([h_out, dlog])
        ]

    def inverse(squares):
        return lax.rsqrt(squares * (1.0 / width) + 1e-05)

    def cut(j):
        return slice(j * step, (j + 1) * step)

    def forward_one(mb, carry):
        squares = jnp.zeros((ROWS, 1), F32)
        for j in range(CUTS):

            @pl.when(not_first)
            def _(j=j):
                h_piece(mb, j).wait_recv()

            h = h_in[mb, :, cut(j)].astype(F32)
            squares = squares + row_sum(h * h)
            scaled = (h * gains_ref[0:1, cut(j)]).astype(BF16)
            product = dot(scaled, w[0, cut(j), :])
            if j == 0:
                acc[...] = product
            else:
                acc[...] += product
        inv = inverse(squares)
        squares = jnp.zeros((ROWS, 1), F32)
        for j in range(CUTS):
            h = h_in[mb, :, cut(j)].astype(F32)
            at = acc[:, cut(j)] * inv
            pre[0, mb, :, cut(j)] = at
            result = (h + gelu(at)).astype(BF16)
            h_mid[mb, :, cut(j)] = result
            wide = result.astype(F32)
            squares = squares + row_sum(wide * wide)
        inv_mid = inverse(squares)
        for j in range(CUTS):
            normed[1, mb, :, cut(j)] = (
                h_mid[mb, :, cut(j)].astype(F32) * inv_mid * gains_ref[1:2, cut(j)]
            ).astype(BF16)
        squares = jnp.zeros((ROWS, 1), F32)
        for j in range(CUTS):
            at = dot(normed[1, mb], w[1, :, cut(j)])
            result = (h_mid[mb, :, cut(j)].astype(F32) + gelu(at)).astype(BF16)
            h_out[mb, :, cut(j)] = result

            @pl.when(not_last)
            def _(j=j):
                h_piece(mb, j).start()

            pre[1, mb, :, cut(j)] = at
            wide = result.astype(F32)
            squares = squares + row_sum(wide * wide)
        for j in range(CUTS):
            normed[0, mb, :, cut(j)] = (
                h_in[mb, :, cut(j)].astype(F32) * inv * gains_ref[0:1, cut(j)]
            ).astype(BF16)
        for copy in peer_copies(mb):
            copy.start()

        @pl.when(last)
        def _():
            scale = inverse(squares)
            z = (h_out[mb].astype(F32) * scale * out_gain_ref[...]).astype(BF16)
            logits = dot(z, hw[...])
            top = jnp.max(logits, axis=1, keepdims=True)
            exponents = jnp.exp(logits - top)
            denominator = row_sum(exponents)
            target = picked_ids[pl.ds(pl.multiple_of(mb * ROWS, ROWS), ROWS), 0:1]
            one_hot = (target == lax.broadcasted_iota(jnp.int32, logits.shape, 1)).astype(F32)
            picked = row_sum(logits * one_hot)
            dlog[mb] = (exponents / denominator - one_hot).astype(BF16)
            for copy in head_copies(mb):
                copy.start()
            losses = jnp.sum(jnp.log(denominator) + top - picked, axis=0, keepdims=True)
            loss_part[...] += jnp.broadcast_to(losses, loss_part.shape)

        return carry

    def part_copy(lane, target):
        return remote(loss_part, loss_in.at[lane], part_send.at[lane], part_recv.at[lane], (odd, target))

    def loss_back():
        return remote(loss_all, loss_all, loss_send.at[0], loss_recv.at[0], (s - 2, y))

    def loss_peer():
        return remote(loss_all, loss_all, loss_send.at[1], loss_recv.at[1], peer)

    def n_copy(layer, owner, lane):
        src = normed.at[layer, :, :, pl.ds(pl.multiple_of(owner * share, share), share)]
        return remote(src, normed_out.at[y], n_send.at[layer, lane], n_recv.at[lane], (2 * k + layer, owner))

    def n_local(layer):
        src = normed.at[layer, :, :, pl.ds(pl.multiple_of(y * share, share), share)]
        return pltpu.make_async_copy(src, normed_out.at[y], local_sem.at[0])

    def n_wait(lane, owner):
        src = normed.at[0, :, :, pl.ds(0, share)]
        return remote(src, normed_out.at[owner], n_send.at[0, lane], n_recv.at[lane], peer)

    def d_copy(layer, owner, lane, mb):
        return remote(
            dpre.at[layer, mb], dpre_out.at[y, mb], d_send.at[layer, lane], d_recv.at[lane], (2 * k + layer, owner)
        )

    def d_local(layer, mb):
        return pltpu.make_async_copy(dpre.at[layer, mb], dpre_out.at[y, mb], local_sem.at[1])

    def d_wait(lane, owner):
        return remote(dpre.at[0], dpre_out.at[owner], d_send.at[0, lane], d_recv.at[lane], peer)

    lanes = ((1, up), (2, down), (3, far))
    arrivals = ((1, down), (2, up), (3, far))

    @pl.when(forward)
    def _():
        loss_part[...] = jnp.zeros_like(loss_part)
        lax.fori_loop(0, count, forward_one, 0)
        for layer in range(2):
            for lane, owner in lanes:
                n_copy(layer, owner, lane).start()
        n_copy(0, y, 0).start()
        n_local(1).start()

        @pl.when(last)
        def _():
            for lane, owner in lanes:
                part_copy(lane, owner).start()
            for lane, owner in lanes:
                part_copy(lane, owner).wait_recv()
            loss_all[...] = loss_part[...] + loss_in[1] + loss_in[2] + loss_in[3]

        @pl.when(not_last)
        def _():
            loss_back().wait_recv()

        @pl.when(not_first)
        def _():
            loss_back().start()

        loss_peer().start()

    def g_piece(mb, j):
        cols = pl.ds(j * step, step)
        return remote(
            g_out.at[mb, :, cols], g_in.at[mb, :, cols], g_send.at[j], g_recv.at[mb, j], (s - 2, y)
        )

    def prepare(mb):
        for copy in peer_copies(mb):
            copy.wait_recv()
        for layer, rows in ((0, h_in), (1, h_mid)):
            squares = jnp.zeros((ROWS, 1), F32)
            for j in range(CUTS):
                h = rows[mb, :, cut(j)].astype(F32)
                squares = squares + row_sum(h * h)
                slope[layer, :, cut(j)] = gelu_slope(pre[layer, mb, :, cut(j)])
            inv_keep[layer] = jnp.broadcast_to(inverse(squares), inv_keep.shape[1:])

    def backward_one(mb, carry):
        @pl.when(last)
        def _():
            for copy in head_copies(mb):
                copy.wait_recv()
            back = dot(dlog[mb], ht[...]) * out_gain_ref[...]
            h = h_out[mb].astype(F32)
            scale = inverse(row_sum(h * h))
            inner = row_sum(back * h)
            g_in[mb] = (scale * back - h * (scale * scale * scale * (1.0 / width) * inner)).astype(BF16)

        for j in range(CUTS):

            @pl.when(not_last)
            def _(j=j):
                g_piece(mb, j).wait_recv()

            d = (g_in[mb, :, cut(j)].astype(F32) * slope[1, :, cut(j)]).astype(BF16)
            dpre[1, mb, :, cut(j)] = d
            product = dot(d, wt[1, cut(j), :])
            if j == 0:
                acc[...] = product
            else:
                acc[...] += product
        inv = inv_keep[1, :, 0:1]
        inner = jnp.zeros((ROWS, 1), F32)
        for j in range(CUTS):
            inner = inner + row_sum(acc[:, cut(j)] * gains_ref[1:2, cut(j)] * h_mid[mb, :, cut(j)].astype(F32))
        pull = inv * inv * inv * (1.0 / width) * inner
        dots = jnp.zeros((ROWS, 1), F32)
        for j in range(CUTS):
            back = acc[:, cut(j)] * gains_ref[1:2, cut(j)]
            g = (
                g_in[mb, :, cut(j)].astype(F32) + (inv * back - h_mid[mb, :, cut(j)].astype(F32) * pull)
            ).astype(BF16)
            acc[:, cut(j)] = g.astype(F32)
            d = (g.astype(F32) * slope[0, :, cut(j)]).astype(BF16)
            dpre[0, mb, :, cut(j)] = d
            dots = dots + row_sum(d.astype(F32) * pre[0, mb, :, cut(j)])

        @pl.when(not_first)
        def _():
            inv = inv_keep[0, :, 0:1]
            pull = inv * inv * (1.0 / width) * dots
            for j in range(CUTS):
                back = dot(dpre[0, mb], wt[0, :, cut(j)]) * gains_ref[0:1, cut(j)]
                g_out[mb, :, cut(j)] = (
                    acc[:, cut(j)] + (inv * back - h_in[mb, :, cut(j)].astype(F32) * pull)
                ).astype(BF16)
                g_piece(mb, j).start()

        for layer in range(2):
            for lane, owner in lanes:
                d_copy(layer, owner, lane, mb).start()
        d_copy(1, y, 0, mb).start()
        d_local(0, mb).start()

        @pl.when(mb < count - 1)
        def _():
            prepare(mb + 1)

        return carry

    @pl.when(backward)
    def _():
        prepare(0)
        lax.fori_loop(0, count, backward_one, 0)
        loss_peer().wait_recv()

    loss_ref[...] = loss_all[...]
    for lane, owner in arrivals:
        n_wait(lane, owner).wait_recv()
        d_wait(lane, owner).wait_recv()

    def sent(ref, sem):
        pltpu.make_async_copy(ref, ref, sem).wait()

    for lane in (1, 2):
        for part in (0, 1):
            sent(w.at[0, 0:half, :], w_send.at[lane, part])

    @pl.when(forward)
    def _():
        for i in range(4):
            sent(w.at[0, 0:half, :], w_send.at[3, i])
        sent(w.at[0, 0:share, :], w_fwd_send.at[1, 0])
        for layer in range(2):
            for lane in (1, 2, 3):
                sent(w.at[0, 0:share, :], w_fwd_send.at[layer, lane])
                sent(normed.at[0, :, :, 0:share], n_send.at[layer, lane])
        sent(normed.at[0, :, :, 0:share], n_send.at[0, 0])
        n_local(1).wait()
        for copy in [remote(ref, ref, peer_send.at[i], peer_recv.at[i, 0], peer) for i, ref in enumerate([h_in, h_mid, pre.at[0], pre.at[1]])]:
            copy.wait_send()

        @pl.when(not_last)
        def _():
            for j in range(CUTS):
                sent(h_out.at[:, :, cut(j)], h_send.at[j])

        @pl.when(last)
        def _():
            sent(h_out, peer_send.at[4])
            sent(dlog, peer_send.at[5])
            for lane in (1, 2, 3):
                sent(loss_part, part_send.at[lane])

        @pl.when(not_first)
        def _():
            sent(loss_all, loss_send.at[0])

        sent(loss_all, loss_send.at[1])
        d_wait(0, y).wait_recv()

    @pl.when(backward)
    def _():
        sent(w.at[0, 0:share, :], w_fwd_send.at[0, 0])
        for layer in range(2):
            for lane in (1, 2, 3):
                sent(dpre.at[0], d_send.at[layer, lane])
        sent(dpre.at[0], d_send.at[1, 0])
        sent(dpre.at[0], local_sem.at[1])

        @pl.when(not_first)
        def _():
            for j in range(CUTS):
                sent(g_out.at[:, :, cut(j)], g_send.at[j])

        n_wait(0, y).wait_recv()


def shards(
    video_ids,
    action_ids,
    target_ids,
    live_lengths,
    video_table,
    action_table,
    layer_gain,
    layer_weight,
    out_gain,
    head_weight,
    live_rows,
):
    width, vocab = head_weight.shape
    share = width // 4
    count = live_rows // ROWS
    ids = jnp.stack([video_ids, action_ids, target_ids])
    other = lax.ppermute(
        layer_gain, "section", [(i, i ^ 1) for i in range(lax.axis_size("section"))]
    )
    odd = lax.axis_index("section") % 2 == 1
    gains = jnp.where(odd, jnp.concatenate([other, layer_gain]), jnp.concatenate([layer_gain, other]))

    vmem = pl.BlockSpec(memory_space=pltpu.VMEM)
    smem = pl.BlockSpec(memory_space=pltpu.SMEM)
    hbm = pl.BlockSpec(memory_space=pl.ANY)
    dma = pltpu.SemaphoreType.DMA
    rows = lambda kind: pltpu.VMEM((count, ROWS, width), kind)
    pair = lambda kind: pltpu.VMEM((2, count, ROWS, width), kind)
    loss, normed, dpre = pl.pallas_call(
        kernel,
        name="stack",
        out_shape=(
            jax.ShapeDtypeStruct((8, 128), F32),
            jax.ShapeDtypeStruct((4, count, ROWS, share), BF16),
            jax.ShapeDtypeStruct((4, count, ROWS, width), BF16),
        ),
        in_specs=[smem, vmem, vmem, vmem, vmem, hbm, hbm, hbm],
        out_specs=(vmem, hbm, hbm),
        scratch_shapes=[
            pltpu.VMEM((2, width, width), BF16),
            pltpu.VMEM((2, width, width), BF16),
            pltpu.VMEM((width, vocab), BF16),
            pltpu.VMEM((vocab, width), BF16),
            rows(BF16),
            rows(BF16),
            rows(BF16),
            pair(F32),
            pair(BF16),
            pair(BF16),
            rows(BF16),
            rows(BF16),
            pltpu.VMEM((count, ROWS, vocab), BF16),
            pltpu.VMEM((ROWS, width), F32),
            pltpu.VMEM((2, ROWS, width), F32),
            pltpu.VMEM((2, ROWS, 128), F32),
            pltpu.VMEM((live_rows, 128), jnp.int32),
            pltpu.VMEM((8, 128), F32),
            pltpu.VMEM((4, 8, 128), F32),
            pltpu.VMEM((8, 128), F32),
            dma((4, 4)),
            dma((2, 4, 2)),
            dma((2, 4)),
            dma((2, 4)),
            dma((2,)),
            dma((CUTS,)),
            dma((count, CUTS)),
            dma((CUTS,)),
            dma((count, CUTS)),
            dma((6,)),
            dma((6, count)),
            dma((2, 4)),
            dma((4,)),
            dma((2, 4)),
            dma((4,)),
            dma((4,)),
            dma((4,)),
            dma((2,)),
            dma((2,)),
        ],
        compiler_params=pltpu.CompilerParams(
            collective_id=0, has_side_effects=True, vmem_limit_bytes=60 * 1024 * 1024
        ),
        cost_estimate=pl.CostEstimate(flops=10**10, bytes_accessed=2 * 10**7, transcendentals=0),
    )(live_lengths, ids, gains, out_gain[None], action_table, video_table, layer_weight, head_weight)
    grad = lax.dot_general(
        normed.reshape(4 * live_rows, share),
        dpre.reshape(4 * live_rows, width),
        (((0,), (0,)), ((), ())),
        preferred_element_type=F32,
    )
    live_count = (jnp.sum(live_lengths) * lax.axis_size("dp")).astype(F32)
    return (loss[0, 0] / live_count, grad[None])


def solution(mesh, live_rows=160):
    in_specs = (
        P("dp", None),
        P("dp", None),
        P("dp", None),
        P("dp", None),
        P(),
        P(),
        P("section", None),
        P("section", "dp", None),
        P(),
        P(),
    )
    out_specs = (P(), P("section", "dp", None))
    return jax.shard_map(
        functools.partial(shards, live_rows=live_rows),
        mesh=mesh,
        in_specs=in_specs,
        out_specs=out_specs,
        check_vma=False,
    )
```

```python
import functools

import jax
import jax.numpy as jnp
from jax import lax
from jax.experimental import pallas as pl
from jax.experimental.pallas import tpu as pltpu
from jax.sharding import PartitionSpec as P

MESH = pl.DeviceIdType.MESH
F32 = jnp.float32
BF16 = jnp.bfloat16
ROWS = 16
CUTS = 4
PRE_SCALE = 0.7978845608028654
CUBE = 0.044715


def gelu(x):
    return 0.5 * x * (1.0 + jnp.tanh(PRE_SCALE * (x + CUBE * x * x * x)))


def gelu_slope(x):
    t = jnp.tanh(PRE_SCALE * (x + CUBE * x * x * x))
    return 0.5 * (1.0 + t) + 0.5 * x * (1.0 - t * t) * (PRE_SCALE * (1.0 + 3.0 * CUBE * x * x))


def dot(left, right):
    return jnp.dot(left, right, preferred_element_type=F32)


def row_sum(x):
    return jnp.sum(x, axis=1, keepdims=True)


def kernel(
    lengths_ref,
    video_ids_ref,
    action_ids_ref,
    target_ids_ref,
    gain_ref,
    out_gain_ref,
    actions_ref,
    video_ref,
    weight_ref,
    head_ref,
    loss_ref,
    normed_out,
    dpre_out,
    w,
    wt,
    hw,
    ht,
    h_in,
    h_mid,
    h_out,
    pre,
    normed,
    dpre,
    g_in,
    g_out,
    dlog,
    acc,
    slope,
    inv_keep,
    gains,
    picked_ids,
    loss_part,
    loss_in,
    loss_all,
    w_send,
    w_recv,
    w_fwd_send,
    w_fwd_recv,
    local_sem,
    h_send,
    h_recv,
    g_send,
    g_recv,
    peer_send,
    peer_recv,
    n_send,
    n_recv,
    d_send,
    d_recv,
    part_send,
    part_recv,
    loss_send,
    loss_recv,
    gain_send,
    gain_recv,
):
    s = lax.axis_index("section")
    y = lax.axis_index("dp")
    planes = lax.axis_size("section") // 2
    k = s // 2
    core = s % 2
    turning = planes - max(1, planes * 3 // 16)
    late = k >= turning
    early = k < turning
    odd_core = core == 1
    even_core = core == 0
    forward = odd_core
    backward = jnp.logical_or(jnp.logical_and(early, odd_core), jnp.logical_and(late, even_core))
    back_target = 2 * (k - 1) + jnp.where(k - 1 < turning, 1, 0)
    first = k == 0
    last = k == planes - 1
    not_first = k > 0
    not_last = k < planes - 1

    width = w.shape[2]
    share = width // 4
    half = share // 2
    step = width // CUTS
    count = h_in.shape[0]
    vocab = hw.shape[1]

    up, down, far = (y + 1) % 4, (y + 3) % 4, (y + 2) % 4
    peer = (2 * k + 1 - core, y)
    odd = 2 * k + 1
    even = 2 * k

    def remote(src, dst, send, recv, device):
        return pltpu.make_async_remote_copy(
            src_ref=src, dst_ref=dst, send_sem=send, recv_sem=recv, device_id=device, device_id_type=MESH
        )

    barrier = pltpu.get_barrier_semaphore()
    for other in (up, down, far):
        for c in (0, 1):
            pl.semaphore_signal(barrier, inc=1, device_id=(2 * k + c, other), device_id_type=MESH)
    pl.semaphore_signal(barrier, inc=1, device_id=peer, device_id_type=MESH)

    for plane in ((k + 1) % planes, (k + planes - 1) % planes):
        for c in (0, 1):
            pl.semaphore_signal(barrier, inc=1, device_id=(2 * plane + c, y), device_id_type=MESH)
    pl.semaphore_wait(barrier, 11)

    def rows_of(owner, part=None):
        if part is None:
            return pl.ds(pl.multiple_of(owner * share, share), share)
        return pl.ds(pl.multiple_of(owner * share + part * half, half), half)

    def direct(layer, lane, part):
        target = up if lane == 1 else down
        return remote(
            weight_ref.at[0, part * half : (part + 1) * half, :],
            w.at[layer, rows_of(y, part), :],
            w_send.at[lane, part],
            w_recv.at[layer, lane, part],
            (odd, target),
        )

    def relay(layer, part):
        owner, target = (down, up) if part == 0 else (up, down)
        block = w.at[layer, rows_of(owner, part), :]
        return remote(block, block, w_send.at[3, 2 * layer + part], w_recv.at[layer, 3, part], (odd, target))

    def to_peer(layer, lane, owner):
        block = w.at[layer, rows_of(owner), :]
        return remote(block, block, w_fwd_send.at[layer, lane], w_fwd_recv.at[layer, lane], peer)

    def own_to_peer(layer):
        return remote(
            weight_ref.at[0], w.at[layer, rows_of(y), :], w_fwd_send.at[layer, 0], w_fwd_recv.at[layer, 0], peer
        )

    def own_local(layer):
        return pltpu.make_async_copy(weight_ref.at[0], w.at[layer, rows_of(y), :], local_sem.at[0])

    def start_own(layer):
        direct(layer, 1, 0).start()
        direct(layer, 2, 1).start()
        direct(layer, 1, 1).start()
        direct(layer, 2, 0).start()
        gain_peer(layer).start()
        gains[layer] = gain_ref[...]

    def gain_peer(layer):
        return remote(gain_ref, gains.at[layer], gain_send.at[0], gain_recv.at[0], peer)

    @pl.when(odd_core)
    def _():
        start_own(1)
        own_local(1).start()

        @pl.when(late)
        def _():
            own_to_peer(1).start()

    @pl.when(even_core)
    def _():
        start_own(0)
        own_to_peer(0).start()

        @pl.when(late)
        def _():
            own_local(0).start()

    @pl.when(last)
    def _():
        pltpu.make_async_copy(head_ref, hw, local_sem.at[1]).start()

    @pl.when(jnp.logical_and(first, forward))
    def _():
        pltpu.make_async_copy(video_ref, ht, local_sem.at[1]).start()

    total = count * ROWS
    slots = video_ids_ref.shape[1]
    place = lax.broadcasted_iota(jnp.int32, (total, slots), 0)
    lane_of = lax.broadcasted_iota(jnp.int32, (total, slots), 1)
    chosen = [jnp.zeros((total, 1), jnp.int32) for _ in range(3)]
    start = jnp.int32(0)
    for b in range(video_ids_ref.shape[0]):
        length = lengths_ref[0, b]
        hit = jnp.logical_and(place == start + lane_of, lane_of < length)
        for kind, ids_ref in enumerate((video_ids_ref, action_ids_ref, target_ids_ref)):
            line = jnp.broadcast_to(ids_ref[b : b + 1, :], (total, slots))
            chosen[kind] = chosen[kind] + row_sum(jnp.where(hit, line, 0))
        start = start + length
    picked_ids[...] = jnp.broadcast_to(chosen[2], picked_ids.shape)

    @pl.when(jnp.logical_and(first, forward))
    def _():
        pltpu.make_async_copy(video_ref, ht, local_sem.at[1]).wait()
        video_hot = (chosen[0] == lax.broadcasted_iota(jnp.int32, (total, ht.shape[0]), 1)).astype(F32).astype(BF16)
        kinds = actions_ref.shape[0]
        for j in range(CUTS):
            cols = slice(j * step, (j + 1) * step)
            rows = dot(video_hot, ht[:, cols])
            for a in range(kinds):
                rows = rows + jnp.where(chosen[1] == a, actions_ref[a : a + 1, cols].astype(F32), 0.0)
            h_in[:, :, cols] = rows.astype(BF16).reshape(count, ROWS, step)

    block = min(512, width)

    def turn(layer, owner):
        def one(i, carry):
            cols = pl.ds(pl.multiple_of(i * block, block), block)
            wt[layer, cols, rows_of(owner)] = w[layer, rows_of(owner), cols].T
            return carry

        lax.fori_loop(0, width // block, one, 0)

    gain_peer(0).wait_recv()

    @pl.when(odd_core)
    def _():
        for layer in range(2):
            direct(layer, 1, 0).wait_recv()
            relay(layer, 0).start()
            direct(layer, 2, 1).wait_recv()
            relay(layer, 1).start()
        own_local(1).wait()
        own_to_peer(0).wait_recv()
        for layer in range(2):
            direct(layer, 1, 1).wait_recv()
            direct(layer, 2, 0).wait_recv()

        @pl.when(late)
        def _():
            for layer in range(2):
                to_peer(layer, 1, down).start()
                to_peer(layer, 2, up).start()

        @pl.when(early)
        def _():
            for layer in range(2):
                for owner in (y, down, up):
                    turn(layer, owner)

        for layer in range(2):
            relay(layer, 0).wait_recv()
            relay(layer, 1).wait_recv()

        @pl.when(late)
        def _():
            for layer in range(2):
                to_peer(layer, 3, far).start()

    @pl.when(jnp.logical_and(last, forward))
    def _():
        pltpu.make_async_copy(head_ref, hw, local_sem.at[1]).wait()

    @pl.when(jnp.logical_and(late, even_core))
    def _():
        own_local(0).wait()
        turn(0, y)
        own_to_peer(1).wait_recv()
        turn(1, y)
        for lane, owner in ((1, down), (2, up), (3, far)):
            for layer in range(2):
                to_peer(layer, lane, owner).wait_recv()
                turn(layer, owner)

    @pl.when(jnp.logical_and(last, backward))
    def _():
        pltpu.make_async_copy(head_ref, hw, local_sem.at[1]).wait()
        for i in range(CUTS):
            ht[:, i * step : (i + 1) * step] = hw[i * step : (i + 1) * step, :].T

    def h_piece(mb, j):
        cols = pl.ds(j * step, step)
        return remote(
            h_out.at[mb, :, cols], h_in.at[mb, :, cols], h_send.at[j], h_recv.at[mb, j], (s + 2, y)
        )

    def peer_copies(mb):
        refs = [h_in, h_mid, pre.at[0], pre.at[1]]
        return [
            remote(ref.at[mb], ref.at[mb], peer_send.at[i], peer_recv.at[i, mb], peer) for i, ref in enumerate(refs)
        ]

    def head_copies(mb):
        return [
            remote(ref.at[mb], ref.at[mb], peer_send.at[4 + i], peer_recv.at[4 + i, mb], peer)
            for i, ref in enumerate([h_out, dlog])
        ]

    def inverse(squares):
        return lax.rsqrt(squares * (1.0 / width) + 1e-05)

    def cut(j):
        return slice(j * step, (j + 1) * step)

    def forward_one(mb, carry):
        squares = jnp.zeros((ROWS, 1), F32)
        for j in range(CUTS):

            @pl.when(not_first)
            def _(j=j):
                h_piece(mb, j).wait_recv()

            h = h_in[mb, :, cut(j)].astype(F32)
            squares = squares + row_sum(h * h)
            scaled = (h * gains[0, :, cut(j)]).astype(BF16)
            product = dot(scaled, w[0, cut(j), :])
            if j == 0:
                acc[...] = product
            else:
                acc[...] += product
        inv = inverse(squares)
        squares = jnp.zeros((ROWS, 1), F32)
        for j in range(CUTS):
            h = h_in[mb, :, cut(j)].astype(F32)
            at = acc[:, cut(j)] * inv
            pre[0, mb, :, cut(j)] = at
            result = (h + gelu(at)).astype(BF16)
            h_mid[mb, :, cut(j)] = result
            wide = result.astype(F32)
            squares = squares + row_sum(wide * wide)
        inv_mid = inverse(squares)
        for j in range(CUTS):
            normed[1, mb, :, cut(j)] = (
                h_mid[mb, :, cut(j)].astype(F32) * inv_mid * gains[1, :, cut(j)]
            ).astype(BF16)
        squares = jnp.zeros((ROWS, 1), F32)
        for j in range(CUTS):
            at = dot(normed[1, mb], w[1, :, cut(j)])
            result = (h_mid[mb, :, cut(j)].astype(F32) + gelu(at)).astype(BF16)
            h_out[mb, :, cut(j)] = result

            @pl.when(not_last)
            def _(j=j):
                h_piece(mb, j).start()

            pre[1, mb, :, cut(j)] = at
            wide = result.astype(F32)
            squares = squares + row_sum(wide * wide)
        for j in range(CUTS):
            normed[0, mb, :, cut(j)] = (
                h_in[mb, :, cut(j)].astype(F32) * inv * gains[0, :, cut(j)]
            ).astype(BF16)

        @pl.when(late)
        def _():
            for copy in peer_copies(mb):
                copy.start()

        @pl.when(last)
        def _():
            scale = inverse(squares)
            z = (h_out[mb].astype(F32) * scale * out_gain_ref[...]).astype(BF16)
            logits = dot(z, hw[...])
            top = jnp.max(logits, axis=1, keepdims=True)
            exponents = jnp.exp(logits - top)
            denominator = row_sum(exponents)
            target = picked_ids[pl.ds(pl.multiple_of(mb * ROWS, ROWS), ROWS), 0:1]
            one_hot = (target == lax.broadcasted_iota(jnp.int32, logits.shape, 1)).astype(F32)
            picked = row_sum(logits * one_hot)
            dlog[mb] = (exponents / denominator - one_hot).astype(BF16)
            for copy in head_copies(mb):
                copy.start()
            losses = jnp.sum(jnp.log(denominator) + top - picked, axis=0, keepdims=True)
            loss_part[...] += jnp.broadcast_to(losses, loss_part.shape)

        return carry

    def part_copy(lane, target):
        return remote(loss_part, loss_in.at[lane], part_send.at[lane], part_recv.at[lane], (odd, target))

    def loss_back():
        return remote(loss_all, loss_all, loss_send.at[0], loss_recv.at[0], (s - 2, y))

    def loss_peer():
        return remote(loss_all, loss_all, loss_send.at[1], loss_recv.at[1], peer)

    def n_copy(layer, owner, lane):
        src = normed.at[layer, :, :, pl.ds(pl.multiple_of(owner * share, share), share)]
        return remote(src, normed_out.at[y], n_send.at[layer, lane], n_recv.at[lane], (2 * k + layer, owner))

    def n_local(layer):
        src = normed.at[layer, :, :, pl.ds(pl.multiple_of(y * share, share), share)]
        return pltpu.make_async_copy(src, normed_out.at[y], local_sem.at[0])

    def n_wait(lane, owner):
        src = normed.at[0, :, :, pl.ds(0, share)]
        return remote(src, normed_out.at[owner], n_send.at[0, lane], n_recv.at[lane], peer)

    def d_copy(layer, owner, lane, mb):
        return remote(
            dpre.at[layer, mb], dpre_out.at[y, mb], d_send.at[layer, lane], d_recv.at[lane], (2 * k + layer, owner)
        )

    def send_dpre(layer, mb):
        for lane, owner in lanes:
            d_copy(layer, owner, lane, mb).start()
        here = early if layer == 1 else late

        @pl.when(here)
        def _():
            d_local(layer, mb).start()

        @pl.when(jnp.logical_not(here))
        def _():
            d_copy(layer, y, 0, mb).start()

    def d_local(layer, mb):
        return pltpu.make_async_copy(dpre.at[layer, mb], dpre_out.at[y, mb], local_sem.at[1])

    def d_wait(lane, owner):
        return remote(dpre.at[0], dpre_out.at[owner], d_send.at[0, lane], d_recv.at[lane], peer)

    lanes = ((1, up), (2, down), (3, far))
    arrivals = ((1, down), (2, up), (3, far))

    @pl.when(forward)
    def _():
        loss_part[...] = jnp.zeros_like(loss_part)
        lax.fori_loop(0, count, forward_one, 0)
        for layer in range(2):
            for lane, owner in lanes:
                n_copy(layer, owner, lane).start()
        n_copy(0, y, 0).start()
        n_local(1).start()

        @pl.when(early)
        def _():
            for layer in range(2):
                turn(layer, far)

    def g_piece(mb, j):
        cols = pl.ds(j * step, step)
        return remote(
            g_out.at[mb, :, cols], g_in.at[mb, :, cols], g_send.at[j], g_recv.at[mb, j], (back_target, y)
        )

    def prepare(mb):
        @pl.when(late)
        def _():
            for copy in peer_copies(mb):
                copy.wait_recv()

        for layer, rows in ((0, h_in), (1, h_mid)):
            squares = jnp.zeros((ROWS, 1), F32)
            for j in range(CUTS):
                h = rows[mb, :, cut(j)].astype(F32)
                squares = squares + row_sum(h * h)
                slope[layer, :, cut(j)] = gelu_slope(pre[layer, mb, :, cut(j)])
            inv_keep[layer] = jnp.broadcast_to(inverse(squares), inv_keep.shape[1:])

    def backward_one(mb, carry):
        @pl.when(last)
        def _():
            for copy in head_copies(mb):
                copy.wait_recv()
            back = dot(dlog[mb], ht[...]) * out_gain_ref[...]
            h = h_out[mb].astype(F32)
            scale = inverse(row_sum(h * h))
            inner = row_sum(back * h)
            g_in[mb] = (scale * back - h * (scale * scale * scale * (1.0 / width) * inner)).astype(BF16)

        for j in range(CUTS):

            @pl.when(not_last)
            def _(j=j):
                g_piece(mb, j).wait_recv()

            d = (g_in[mb, :, cut(j)].astype(F32) * slope[1, :, cut(j)]).astype(BF16)
            dpre[1, mb, :, cut(j)] = d
            product = dot(d, wt[1, cut(j), :])
            if j == 0:
                acc[...] = product
            else:
                acc[...] += product
        inv = inv_keep[1, :, 0:1]
        inner = jnp.zeros((ROWS, 1), F32)
        for j in range(CUTS):
            inner = inner + row_sum(acc[:, cut(j)] * gains[1, :, cut(j)] * h_mid[mb, :, cut(j)].astype(F32))
        pull = inv * inv * inv * (1.0 / width) * inner
        dots = jnp.zeros((ROWS, 1), F32)
        for j in range(CUTS):
            back = acc[:, cut(j)] * gains[1, :, cut(j)]
            g = (
                g_in[mb, :, cut(j)].astype(F32) + (inv * back - h_mid[mb, :, cut(j)].astype(F32) * pull)
            ).astype(BF16)
            acc[:, cut(j)] = g.astype(F32)
            d = (g.astype(F32) * slope[0, :, cut(j)]).astype(BF16)
            dpre[0, mb, :, cut(j)] = d
            dots = dots + row_sum(d.astype(F32) * pre[0, mb, :, cut(j)])

        @pl.when(not_first)
        def _():
            inv = inv_keep[0, :, 0:1]
            pull = inv * inv * (1.0 / width) * dots
            for j in range(CUTS):
                back = dot(dpre[0, mb], wt[0, :, cut(j)]) * gains[0, :, cut(j)]
                g_out[mb, :, cut(j)] = (
                    acc[:, cut(j)] + (inv * back - h_in[mb, :, cut(j)].astype(F32) * pull)
                ).astype(BF16)
                g_piece(mb, j).start()

        send_dpre(0, mb)
        send_dpre(1, mb)

        @pl.when(mb < count - 1)
        def _():
            prepare(mb + 1)

        return carry

    @pl.when(backward)
    def _():
        prepare(0)
        lax.fori_loop(0, count, backward_one, 0)

    @pl.when(odd_core)
    def _():
        @pl.when(last)
        def _():
            for lane, owner in lanes:
                part_copy(lane, owner).start()
            for lane, owner in lanes:
                part_copy(lane, owner).wait_recv()
            loss_all[...] = loss_part[...] + loss_in[1] + loss_in[2] + loss_in[3]

        @pl.when(not_last)
        def _():
            loss_back().wait_recv()

        @pl.when(not_first)
        def _():
            loss_back().start()

        loss_peer().start()

    @pl.when(even_core)
    def _():
        loss_peer().wait_recv()

    live_count = (start * lax.axis_size("dp")).astype(F32)
    loss_ref[0, 0] = loss_all[0, 0] / live_count
    for lane, owner in arrivals:
        n_wait(lane, owner).wait_recv()
        d_wait(lane, owner).wait_recv()

    def sent(ref, sem):
        pltpu.make_async_copy(ref, ref, sem).wait()

    sent(gain_ref, gain_send.at[0])
    for lane in (1, 2):
        for part in (0, 1):
            sent(w.at[0, 0:half, :], w_send.at[lane, part])

    @pl.when(odd_core)
    def _():
        for i in range(4):
            sent(w.at[0, 0:half, :], w_send.at[3, i])
        for layer in range(2):
            for lane in (1, 2, 3):
                sent(normed.at[0, :, :, 0:share], n_send.at[layer, lane])
        sent(normed.at[0, :, :, 0:share], n_send.at[0, 0])
        n_local(1).wait()

        @pl.when(late)
        def _():
            sent(w.at[0, 0:share, :], w_fwd_send.at[1, 0])
            for layer in range(2):
                for lane in (1, 2, 3):
                    sent(w.at[0, 0:share, :], w_fwd_send.at[layer, lane])
            for i, ref in enumerate([h_in, h_mid, pre.at[0], pre.at[1]]):
                sent(ref, peer_send.at[i])
            d_wait(0, y).wait_recv()

        @pl.when(not_last)
        def _():
            for j in range(CUTS):
                sent(h_out.at[:, :, cut(j)], h_send.at[j])

        @pl.when(last)
        def _():
            sent(h_out, peer_send.at[4])
            sent(dlog, peer_send.at[5])
            for lane in (1, 2, 3):
                sent(loss_part, part_send.at[lane])

        @pl.when(not_first)
        def _():
            sent(loss_all, loss_send.at[0])

        sent(loss_all, loss_send.at[1])

    @pl.when(even_core)
    def _():
        sent(w.at[0, 0:share, :], w_fwd_send.at[0, 0])
        n_wait(0, y).wait_recv()

        @pl.when(early)
        def _():
            d_wait(0, y).wait_recv()

    @pl.when(backward)
    def _():
        for layer in range(2):
            for lane in (1, 2, 3):
                sent(dpre.at[0], d_send.at[layer, lane])
        sent(dpre.at[0], local_sem.at[1])

        @pl.when(early)
        def _():
            sent(dpre.at[0], d_send.at[0, 0])

        @pl.when(late)
        def _():
            sent(dpre.at[0], d_send.at[1, 0])

        @pl.when(not_first)
        def _():
            for j in range(CUTS):
                sent(g_out.at[:, :, cut(j)], g_send.at[j])


def product_kernel(normed_ref, dpre_ref, out_ref, turned):
    @pl.when(pl.program_id(0) == 0)
    def _():
        turned[...] = normed_ref[...].T

    out_ref[0] = dot(turned[...], dpre_ref[...])


def product(normed, dpre):
    rows, share = normed.shape
    width = dpre.shape[1]
    step = min(512, width)
    return pl.pallas_call(
        product_kernel,
        name="weight_grad",
        grid=(width // step,),
        out_shape=jax.ShapeDtypeStruct((1, share, width), F32),
        in_specs=[
            pl.BlockSpec((rows, share), lambda i: (0, 0)),
            pl.BlockSpec((rows, step), lambda i: (0, i)),
        ],
        out_specs=pl.BlockSpec((1, share, step), lambda i: (0, 0, i)),
        scratch_shapes=[pltpu.VMEM((share, rows), BF16)],
        compiler_params=pltpu.CompilerParams(vmem_limit_bytes=32 * 1024 * 1024),
        cost_estimate=pl.CostEstimate(
            flops=2 * rows * share * width, bytes_accessed=6 * share * width, transcendentals=0
        ),
    )(normed, dpre)


def shards(
    video_ids,
    action_ids,
    target_ids,
    live_lengths,
    video_table,
    action_table,
    layer_gain,
    layer_weight,
    out_gain,
    head_weight,
    live_rows,
):
    width, vocab = head_weight.shape
    share = width // 4
    count = live_rows // ROWS

    vmem = pl.BlockSpec(memory_space=pltpu.VMEM)
    smem = pl.BlockSpec(memory_space=pltpu.SMEM)
    hbm = pl.BlockSpec(memory_space=pl.ANY)
    dma = pltpu.SemaphoreType.DMA
    rows = lambda kind: pltpu.VMEM((count, ROWS, width), kind)
    pair = lambda kind: pltpu.VMEM((2, count, ROWS, width), kind)
    loss, normed, dpre = pl.pallas_call(
        kernel,
        name="stack",
        out_shape=(
            jax.ShapeDtypeStruct((1, 1), F32),
            jax.ShapeDtypeStruct((4, count, ROWS, share), BF16),
            jax.ShapeDtypeStruct((4, count, ROWS, width), BF16),
        ),
        in_specs=[smem, vmem, vmem, vmem, vmem, vmem, vmem, hbm, hbm, hbm],
        out_specs=(smem, hbm, hbm),
        scratch_shapes=[
            pltpu.VMEM((2, width, width), BF16),
            pltpu.VMEM((2, width, width), BF16),
            pltpu.VMEM((width, vocab), BF16),
            pltpu.VMEM((vocab, width), BF16),
            rows(BF16),
            rows(BF16),
            rows(BF16),
            pair(F32),
            pair(BF16),
            pair(BF16),
            rows(BF16),
            rows(BF16),
            pltpu.VMEM((count, ROWS, vocab), BF16),
            pltpu.VMEM((ROWS, width), F32),
            pltpu.VMEM((2, ROWS, width), F32),
            pltpu.VMEM((2, ROWS, 128), F32),
            pltpu.VMEM((2, 1, width), F32),
            pltpu.VMEM((live_rows, 128), jnp.int32),
            pltpu.VMEM((8, 128), F32),
            pltpu.VMEM((4, 8, 128), F32),
            pltpu.VMEM((8, 128), F32),
            dma((4, 4)),
            dma((2, 4, 2)),
            dma((2, 4)),
            dma((2, 4)),
            dma((2,)),
            dma((CUTS,)),
            dma((count, CUTS)),
            dma((CUTS,)),
            dma((count, CUTS)),
            dma((6,)),
            dma((6, count)),
            dma((2, 4)),
            dma((4,)),
            dma((2, 4)),
            dma((4,)),
            dma((4,)),
            dma((4,)),
            dma((2,)),
            dma((2,)),
            dma((1,)),
            dma((1,)),
        ],
        compiler_params=pltpu.CompilerParams(
            collective_id=0, has_side_effects=True, vmem_limit_bytes=60 * 1024 * 1024
        ),
        cost_estimate=pl.CostEstimate(flops=10**10, bytes_accessed=2 * 10**7, transcendentals=0),
    )(
        live_lengths,
        video_ids,
        action_ids,
        target_ids,
        layer_gain,
        out_gain[None],
        action_table,
        video_table,
        layer_weight,
        head_weight,
    )
    grad = product(normed.reshape(4 * live_rows, share), dpre.reshape(4 * live_rows, width))
    return (loss[0, 0], grad)


def solution(mesh, live_rows=160):
    in_specs = (
        P("dp", None),
        P("dp", None),
        P("dp", None),
        P("dp", None),
        P(),
        P(),
        P("section", None),
        P("section", "dp", None),
        P(),
        P(),
    )
    out_specs = (P(), P("section", "dp", None))
    return jax.shard_map(
        functools.partial(shards, live_rows=live_rows),
        mesh=mesh,
        in_specs=in_specs,
        out_specs=out_specs,
        check_vma=False,
    )
```

```python
import functools

import jax
import jax.numpy as jnp
from jax import lax
from jax.experimental import pallas as pl
from jax.experimental.pallas import tpu as pltpu
from jax.sharding import PartitionSpec as P

MESH = pl.DeviceIdType.MESH
F32 = jnp.float32
BF16 = jnp.bfloat16
ROWS = 16
CUTS = 4
PRE_SCALE = 0.7978845608028654
CUBE = 0.044715


def gelu(x):
    return 0.5 * x * (1.0 + jnp.tanh(PRE_SCALE * (x + CUBE * x * x * x)))


def gelu_slope(x):
    t = jnp.tanh(PRE_SCALE * (x + CUBE * x * x * x))
    return 0.5 * (1.0 + t) + 0.5 * x * (1.0 - t * t) * (PRE_SCALE * (1.0 + 3.0 * CUBE * x * x))


def dot(left, right):
    return jnp.dot(left, right, preferred_element_type=F32)


def row_sum(x):
    return jnp.sum(x, axis=1, keepdims=True)


def kernel(
    lengths_ref,
    video_ids_ref,
    action_ids_ref,
    target_ids_ref,
    gain_ref,
    out_gain_ref,
    actions_ref,
    video_ref,
    weight_ref,
    head_ref,
    loss_ref,
    normed_out,
    dpre_out,
    w,
    wt,
    hw,
    ht,
    h_in,
    h_mid,
    h_out,
    pre,
    normed,
    dpre,
    g_in,
    g_out,
    dlog,
    acc,
    raw,
    slope,
    inv_keep,
    gains,
    picked_ids,
    loss_part,
    loss_in,
    loss_all,
    w_send,
    w_recv,
    w_fwd_send,
    w_fwd_recv,
    local_sem,
    h_send,
    h_recv,
    g_send,
    g_recv,
    peer_send,
    peer_recv,
    n_send,
    n_recv,
    d_send,
    d_recv,
    part_send,
    part_recv,
    loss_send,
    loss_recv,
    gain_send,
    gain_recv,
    held,
    held_send,
    held_recv,
    back_send,
    back_recv,
    go_sem,
):
    s = lax.axis_index("section")
    y = lax.axis_index("dp")
    planes = lax.axis_size("section") // 2
    k = s // 2
    core = s % 2
    turning = planes - max(1, planes * 3 // 16)
    late = k >= turning
    early = k < turning
    odd_core = core == 1
    even_core = core == 0
    forward = odd_core
    backward = jnp.logical_or(jnp.logical_and(early, odd_core), jnp.logical_and(late, even_core))
    back_target = 2 * (k - 1) + jnp.where(k - 1 < turning, 1, 0)
    first = k == 0
    last = k == planes - 1
    not_first = k > 0
    not_last = k < planes - 1

    width = w.shape[2]
    share = width // 4
    halves = (share * 3 // 8, share // 8)
    main = 2 * halves[0]
    step = width // CUTS
    count = h_in.shape[0]
    vocab = hw.shape[1]

    up, down, far = (y + 1) % 4, (y + 3) % 4, (y + 2) % 4
    peer = (2 * k + 1 - core, y)
    odd = 2 * k + 1
    even = 2 * k

    def remote(src, dst, send, recv, device):
        return pltpu.make_async_remote_copy(
            src_ref=src, dst_ref=dst, send_sem=send, recv_sem=recv, device_id=device, device_id_type=MESH
        )

    barrier = pltpu.get_barrier_semaphore()
    for other in (up, down, far):
        for c in (0, 1):
            pl.semaphore_signal(barrier, inc=1, device_id=(2 * k + c, other), device_id_type=MESH)
    pl.semaphore_signal(barrier, inc=1, device_id=peer, device_id_type=MESH)

    for plane in ((k + 1) % planes, (k + planes - 1) % planes):
        for c in (0, 1):
            pl.semaphore_signal(barrier, inc=1, device_id=(2 * plane + c, y), device_id_type=MESH)

    group = planes // 4
    helped = k < group
    helper = k >= planes - group
    friend = jnp.where(helped, k + planes - group, k - planes + group)

    @pl.when(jnp.logical_or(helped, helper))
    def _():
        for c in (0, 1):
            pl.semaphore_signal(barrier, inc=1, device_id=(2 * friend + c, y), device_id_type=MESH)

    pl.semaphore_wait(barrier, 11 + jnp.where(jnp.logical_or(helped, helper), 2, 0))

    def rows_of(owner):
        return pl.ds(pl.multiple_of(owner * share, share), share)

    def piece(kind, part):
        return kind * main + part * halves[kind], halves[kind]

    def piece_of(owner, kind, part):
        offset, size = piece(kind, part)
        return pl.ds(pl.multiple_of(owner * share + offset, 16), size)

    def direct(layer, lane, kind, part):
        offset, size = piece(kind, part)
        return remote(
            weight_ref.at[0, offset : offset + size, :],
            w.at[layer, piece_of(y, kind, part), :],
            w_send.at[lane, 2 * kind + part],
            w_recv.at[layer, lane, 2 * kind + part],
            (odd, up if lane == 1 else down),
        )

    def relay(layer, kind, part):
        owner, target = (down, up) if part == 0 else (up, down)
        block = w.at[layer, piece_of(owner, kind, part), :]
        return remote(
            block, block, w_send.at[3 + layer, 2 * kind + part], w_recv.at[layer, 3, 2 * kind + part], (odd, target)
        )

    friend_odd = 2 * friend + 1

    def to_helper(layer, part):
        offset, size = piece(1, part)
        return remote(
            weight_ref.at[0, offset : offset + size, :],
            held.at[layer, y, part],
            held_send.at[0, part],
            held_recv.at[layer, 0, part],
            (friend_odd, y),
        )

    def held_direct(layer, lane, part):
        block = held.at[layer, y, part]
        return remote(
            block,
            block,
            held_send.at[1 + 2 * layer + (lane - 1), part],
            held_recv.at[layer, lane, part],
            (odd, up if lane == 1 else down),
        )

    def held_relay(layer, part):
        owner, target = (down, up) if part == 0 else (up, down)
        block = held.at[layer, owner, part]
        return remote(block, block, held_send.at[5 + layer, part], held_recv.at[layer, 3, part], (odd, target))

    owners = {1: down, 2: up, 3: far}

    def hand_back(layer, lane, part):
        return remote(
            held.at[layer, owners[lane], part],
            w.at[layer, piece_of(owners[lane], 1, part), :],
            back_send.at[layer, lane, part],
            back_recv.at[layer, lane, part],
            (friend_odd, y),
        )

    def to_peer(layer, lane, owner):
        block = w.at[layer, rows_of(owner), :]
        return remote(block, block, w_fwd_send.at[layer, lane], w_fwd_recv.at[layer, lane], peer)

    def own_to_peer(layer):
        return remote(
            weight_ref.at[0], w.at[layer, rows_of(y), :], w_fwd_send.at[layer, 0], w_fwd_recv.at[layer, 0], peer
        )

    def own_local(layer):
        return pltpu.make_async_copy(weight_ref.at[0], w.at[layer, rows_of(y), :], local_sem.at[0])

    def start_own(layer):
        @pl.when(helped)
        def _():
            to_helper(layer, 0).start()
            to_helper(layer, 1).start()

        for kind in (0, 1):

            def one_kind(kind=kind):
                direct(layer, 1, kind, 0).start()
                direct(layer, 2, kind, 1).start()
                direct(layer, 1, kind, 1).start()
                direct(layer, 2, kind, 0).start()

            if kind == 0:
                one_kind()
            else:
                pl.when(jnp.logical_not(helped))(one_kind)

    def gain_peer(layer):
        return remote(gain_ref, gains.at[layer], gain_send.at[0], gain_recv.at[0], peer)

    def exchange_gain(layer):
        gain_peer(layer).start()
        gains[layer] = gain_ref[...]

    @pl.when(odd_core)
    def _():
        exchange_gain(1)

        @pl.when(helper)
        def _():
            for part in (0, 1):
                for layer in (0, 1):
                    to_helper(layer, part).wait_recv()
                    held_direct(layer, 1 + part, part).start()
                    held_direct(layer, 2 - part, part).start()
            pl.semaphore_signal(go_sem, inc=1, device_id=peer, device_id_type=MESH)

        @pl.when(helper)
        def _():
            for part in (0, 1):
                for layer in (0, 1):
                    held_direct(layer, 1 + part, part).wait_recv()
                    held_relay(layer, part).start()
                    hand_back(layer, 1 + part, part).start()
                    held_direct(layer, 2 - part, part).wait_recv()
                    hand_back(layer, 2 - part, part).start()
            for part in (0, 1):
                for layer in (0, 1):
                    held_relay(layer, part).wait_recv()
                    hand_back(layer, 3, part).start()

        start_own(1)
        own_local(1).start()

        @pl.when(late)
        def _():
            own_to_peer(1).start()

    @pl.when(even_core)
    def _():
        exchange_gain(0)
        own_to_peer(0).start()

        @pl.when(helper)
        def _():
            pl.semaphore_wait(go_sem, 1)

        start_own(0)

        @pl.when(late)
        def _():
            own_local(0).start()

    @pl.when(last)
    def _():
        pltpu.make_async_copy(head_ref, hw, local_sem.at[1]).start()

    @pl.when(jnp.logical_and(first, forward))
    def _():
        pltpu.make_async_copy(video_ref, ht, local_sem.at[1]).start()

    total = count * ROWS
    slots = video_ids_ref.shape[1]
    place = lax.broadcasted_iota(jnp.int32, (total, slots), 0)
    lane_of = lax.broadcasted_iota(jnp.int32, (total, slots), 1)
    chosen = [jnp.zeros((total, 1), jnp.int32) for _ in range(3)]
    start = jnp.int32(0)
    for b in range(video_ids_ref.shape[0]):
        length = lengths_ref[0, b]
        hit = jnp.logical_and(place == start + lane_of, lane_of < length)
        for kind, ids_ref in enumerate((video_ids_ref, action_ids_ref, target_ids_ref)):
            line = jnp.broadcast_to(ids_ref[b : b + 1, :], (total, slots))
            chosen[kind] = chosen[kind] + row_sum(jnp.where(hit, line, 0))
        start = start + length
    picked_ids[...] = jnp.broadcast_to(chosen[2], picked_ids.shape)

    @pl.when(jnp.logical_and(first, forward))
    def _():
        pltpu.make_async_copy(video_ref, ht, local_sem.at[1]).wait()
        video_hot = (chosen[0] == lax.broadcasted_iota(jnp.int32, (total, ht.shape[0]), 1)).astype(F32).astype(BF16)
        kinds = actions_ref.shape[0]
        for j in range(CUTS):
            cols = slice(j * step, (j + 1) * step)
            rows = dot(video_hot, ht[:, cols])
            for a in range(kinds):
                rows = rows + jnp.where(chosen[1] == a, actions_ref[a : a + 1, cols].astype(F32), 0.0)
            h_in[:, :, cols] = rows.astype(BF16).reshape(count, ROWS, step)

    block = min(512, width)

    def turn(layer, owner):
        def one(i, carry):
            cols = pl.ds(pl.multiple_of(i * block, block), block)
            wt[layer, cols, rows_of(owner)] = w[layer, rows_of(owner), cols].T
            return carry

        lax.fori_loop(0, width // block, one, 0)

    gain_peer(0).wait_recv()

    def ring(kind):
        for layer in range(2):
            direct(layer, 1, kind, 0).wait_recv()
            relay(layer, kind, 0).start()
            direct(layer, 2, kind, 1).wait_recv()
            relay(layer, kind, 1).start()

    def ring_rest(kind):
        for layer in range(2):
            direct(layer, 1, kind, 1).wait_recv()
            direct(layer, 2, kind, 0).wait_recv()

    def ring_far(kind):
        for layer in range(2):
            relay(layer, kind, 0).wait_recv()
            relay(layer, kind, 1).wait_recv()

    @pl.when(odd_core)
    def _():
        ring(0)
        own_local(1).wait()
        own_to_peer(0).wait_recv()

        @pl.when(helped)
        def _():
            ring_rest(0)
            ring_far(0)
            for layer in range(2):
                for lane in (1, 2, 3):
                    for part in (0, 1):
                        hand_back(layer, lane, part).wait_recv()

        @pl.when(jnp.logical_not(helped))
        def _():
            ring(1)
            ring_rest(0)
            ring_rest(1)

            @pl.when(late)
            def _():
                for layer in range(2):
                    to_peer(layer, 1, down).start()
                    to_peer(layer, 2, up).start()

            @pl.when(early)
            def _():
                for layer in range(2):
                    for owner in (y, down, up):
                        turn(layer, owner)

            ring_far(0)
            ring_far(1)

            @pl.when(late)
            def _():
                for layer in range(2):
                    to_peer(layer, 3, far).start()

    @pl.when(jnp.logical_and(last, forward))
    def _():
        pltpu.make_async_copy(head_ref, hw, local_sem.at[1]).wait()

    @pl.when(jnp.logical_and(late, even_core))
    def _():
        own_local(0).wait()
        turn(0, y)
        own_to_peer(1).wait_recv()
        turn(1, y)
        for lane, owner in ((1, down), (2, up), (3, far)):
            for layer in range(2):
                to_peer(layer, lane, owner).wait_recv()
                turn(layer, owner)

    @pl.when(jnp.logical_and(last, backward))
    def _():
        pltpu.make_async_copy(head_ref, hw, local_sem.at[1]).wait()
        for i in range(CUTS):
            ht[:, i * step : (i + 1) * step] = hw[i * step : (i + 1) * step, :].T

    def sent(ref, sem):
        pltpu.make_async_copy(ref, ref, sem).wait()

    def gather_sent():
        sent(gain_ref, gain_send.at[0])

        def parts_sent(send, kind):
            for part in (0, 1):
                sent(w.at[0, 0 : halves[kind], :], send.at[2 * kind + part])

        for lane in (1, 2):
            parts_sent(w_send.at[lane], 0)

        @pl.when(jnp.logical_not(helped))
        def _():
            for lane in (1, 2):
                parts_sent(w_send.at[lane], 1)

        @pl.when(helped)
        def _():
            for part in (0, 1):
                sent(held.at[0, 0, 0], held_send.at[0, part])

        @pl.when(odd_core)
        def _():
            for layer in (0, 1):
                parts_sent(w_send.at[3 + layer], 0)

            @pl.when(jnp.logical_not(helped))
            def _():
                for layer in (0, 1):
                    parts_sent(w_send.at[3 + layer], 1)

            @pl.when(helper)
            def _():
                for part in (0, 1):
                    for i in range(1, 7):
                        sent(held.at[0, 0, 0], held_send.at[i, part])
                    for layer in (0, 1):
                        for lane in (1, 2, 3):
                            sent(held.at[0, 0, 0], back_send.at[layer, lane, part])

            @pl.when(late)
            def _():
                sent(w.at[0, 0:share, :], w_fwd_send.at[1, 0])
                for layer in range(2):
                    for lane in (1, 2, 3):
                        sent(w.at[0, 0:share, :], w_fwd_send.at[layer, lane])

        @pl.when(even_core)
        def _():
            sent(w.at[0, 0:share, :], w_fwd_send.at[0, 0])

    def h_piece(mb, j):
        cols = pl.ds(j * step, step)
        return remote(
            h_out.at[mb, :, cols], h_in.at[mb, :, cols], h_send.at[j], h_recv.at[mb, j], (s + 2, y)
        )

    def peer_copies(mb):
        refs = [h_in, h_mid, pre.at[0], pre.at[1]]
        return [
            remote(ref.at[mb], ref.at[mb], peer_send.at[i], peer_recv.at[i, mb], peer) for i, ref in enumerate(refs)
        ]

    def head_copies(mb):
        return [
            remote(ref.at[mb], ref.at[mb], peer_send.at[4 + i], peer_recv.at[4 + i, mb], peer)
            for i, ref in enumerate([h_out, dlog])
        ]

    def inverse(squares):
        return lax.rsqrt(squares * (1.0 / width) + 1e-05)

    def cut(j):
        return slice(j * step, (j + 1) * step)

    def fold(x):
        return sum(x[:, i : i + 128] for i in range(0, x.shape[1], 128))

    def forward_one(mb, carry, is_first, is_last):
        squares = jnp.zeros((ROWS, 128), F32)
        for j in range(CUTS):
            if not is_first:
                h_piece(mb, j).wait_recv()
            h = h_in[mb, :, cut(j)].astype(F32)
            squares = squares + fold(h * h)
            product = dot((h * gains[0, :, cut(j)]).astype(BF16), w[0, cut(j), :])
            if j == 0:
                acc[...] = product
            else:
                acc[...] += product
        inv = inverse(row_sum(squares))
        squares = jnp.zeros((ROWS, 128), F32)
        opening = None
        for j in range(CUTS):
            h = h_in[mb, :, cut(j)].astype(F32)
            at = acc[:, cut(j)] * inv
            pre[0, mb, :, cut(j)] = at
            result = (h + gelu(at)).astype(BF16)
            h_mid[mb, :, cut(j)] = result
            wide = result.astype(F32)
            squares = squares + fold(wide * wide)
            scaled = (wide * gains[1, :, cut(j)]).astype(BF16)
            raw[:, cut(j)] = scaled
            part = dot(scaled, w[1, cut(j), cut(0)])
            opening = part if opening is None else opening + part
        inv_mid = inverse(row_sum(squares))
        squares = jnp.zeros((ROWS, 128), F32)
        for j in range(CUTS):
            at = (opening if j == 0 else dot(raw[...], w[1, :, cut(j)])) * inv_mid
            result = (h_mid[mb, :, cut(j)].astype(F32) + gelu(at)).astype(BF16)
            h_out[mb, :, cut(j)] = result
            if not is_last:
                h_piece(mb, j).start()
            pre[1, mb, :, cut(j)] = at
            wide = result.astype(F32)
            squares = squares + fold(wide * wide)
        for j in range(CUTS):
            normed[0, mb, :, cut(j)] = (
                h_in[mb, :, cut(j)].astype(F32) * inv * gains[0, :, cut(j)]
            ).astype(BF16)
            normed[1, mb, :, cut(j)] = (
                h_mid[mb, :, cut(j)].astype(F32) * inv_mid * gains[1, :, cut(j)]
            ).astype(BF16)

        @pl.when(late)
        def _():
            for copy in peer_copies(mb):
                copy.start()

        if is_last:
            scale = inverse(row_sum(squares))
            z = (h_out[mb].astype(F32) * scale * out_gain_ref[...]).astype(BF16)
            logits = dot(z, hw[...])
            top = jnp.max(logits, axis=1, keepdims=True)
            exponents = jnp.exp(logits - top)
            denominator = row_sum(exponents)
            target = picked_ids[pl.ds(pl.multiple_of(mb * ROWS, ROWS), ROWS), 0:1]
            one_hot = (target == lax.broadcasted_iota(jnp.int32, logits.shape, 1)).astype(F32)
            picked = row_sum(logits * one_hot)
            dlog[mb] = (exponents / denominator - one_hot).astype(BF16)
            for copy in head_copies(mb):
                copy.start()
            losses = jnp.sum(jnp.log(denominator) + top - picked, axis=0, keepdims=True)
            loss_part[...] += jnp.broadcast_to(losses, loss_part.shape)

        return carry

    def part_copy(lane, target):
        return remote(loss_part, loss_in.at[lane], part_send.at[lane], part_recv.at[lane], (odd, target))

    def loss_back():
        return remote(loss_all, loss_all, loss_send.at[0], loss_recv.at[0], (s - 2, y))

    def loss_peer():
        return remote(loss_all, loss_all, loss_send.at[1], loss_recv.at[1], peer)

    def n_copy(layer, owner, lane):
        src = normed.at[layer, :, :, pl.ds(pl.multiple_of(owner * share, share), share)]
        return remote(src, normed_out.at[y], n_send.at[layer, lane], n_recv.at[lane], (2 * k + layer, owner))

    def n_local(layer):
        src = normed.at[layer, :, :, pl.ds(pl.multiple_of(y * share, share), share)]
        return pltpu.make_async_copy(src, normed_out.at[y], local_sem.at[0])

    def n_wait(lane, owner):
        src = normed.at[0, :, :, pl.ds(0, share)]
        return remote(src, normed_out.at[owner], n_send.at[0, lane], n_recv.at[lane], peer)

    def d_copy(layer, owner, lane, mb):
        return remote(
            dpre.at[layer, mb], dpre_out.at[y, mb], d_send.at[layer, lane], d_recv.at[lane], (2 * k + layer, owner)
        )

    def send_dpre(layer, mb):
        for lane, owner in lanes:
            d_copy(layer, owner, lane, mb).start()
        here = early if layer == 1 else late

        @pl.when(here)
        def _():
            d_local(layer, mb).start()

        @pl.when(jnp.logical_not(here))
        def _():
            d_copy(layer, y, 0, mb).start()

    def d_local(layer, mb):
        return pltpu.make_async_copy(dpre.at[layer, mb], dpre_out.at[y, mb], local_sem.at[1])

    def d_wait(lane, owner):
        return remote(dpre.at[0], dpre_out.at[owner], d_send.at[0, lane], d_recv.at[lane], peer)

    lanes = ((1, up), (2, down), (3, far))
    arrivals = ((1, down), (2, up), (3, far))

    @pl.when(forward)
    def _():
        loss_part[...] = jnp.zeros_like(loss_part)

        @pl.when(first)
        def _():
            lax.fori_loop(0, count, functools.partial(forward_one, is_first=True, is_last=False), 0)

        @pl.when(jnp.logical_and(not_first, not_last))
        def _():
            lax.fori_loop(0, count, functools.partial(forward_one, is_first=False, is_last=False), 0)

        @pl.when(last)
        def _():
            lax.fori_loop(0, count, functools.partial(forward_one, is_first=False, is_last=True), 0)

        for layer in range(2):
            for lane, owner in lanes:
                n_copy(layer, owner, lane).start()
        n_copy(0, y, 0).start()
        n_local(1).start()

        @pl.when(early)
        def _():
            for layer in range(2):
                turn(layer, far)

        @pl.when(helped)
        def _():
            for layer in range(2):
                for owner in (y, down, up):
                    turn(layer, owner)

    def g_piece(mb, j):
        cols = pl.ds(j * step, step)
        return remote(
            g_out.at[mb, :, cols], g_in.at[mb, :, cols], g_send.at[j], g_recv.at[mb, j], (back_target, y)
        )

    def prepare(mb):
        @pl.when(late)
        def _():
            for copy in peer_copies(mb):
                copy.wait_recv()

        for layer, rows in ((0, h_in), (1, h_mid)):
            squares = jnp.zeros((ROWS, 1), F32)
            for j in range(CUTS):
                h = rows[mb, :, cut(j)].astype(F32)
                squares = squares + row_sum(h * h)
                slope[layer, :, cut(j)] = gelu_slope(pre[layer, mb, :, cut(j)])
            inv_keep[layer] = jnp.broadcast_to(inverse(squares), inv_keep.shape[1:])

    def backward_one(mb, carry, is_first, is_last):
        if is_last:
            for copy in head_copies(mb):
                copy.wait_recv()
            back = dot(dlog[mb], ht[...]) * out_gain_ref[...]
            h = h_out[mb].astype(F32)
            scale = inverse(row_sum(h * h))
            inner = row_sum(back * h)
            g_in[mb] = (scale * back - h * (scale * scale * scale * (1.0 / width) * inner)).astype(BF16)

        dots = jnp.zeros((ROWS, 128), F32)
        for j in range(CUTS):
            if not is_last:
                g_piece(mb, j).wait_recv()
            d = (g_in[mb, :, cut(j)].astype(F32) * slope[1, :, cut(j)]).astype(BF16)
            dpre[1, mb, :, cut(j)] = d
            dots = dots + fold(d.astype(F32) * pre[1, mb, :, cut(j)])
            product = dot(d, wt[1, cut(j), :])
            if j == 0:
                acc[...] = product
            else:
                acc[...] += product
        if is_first:
            send_dpre(1, mb)
        inv = inv_keep[1, :, 0:1]
        pull = inv * inv * (1.0 / width) * row_sum(dots)
        dots = jnp.zeros((ROWS, 128), F32)
        opening = None
        for j in range(CUTS):
            back = acc[:, cut(j)] * gains[1, :, cut(j)]
            g = (
                g_in[mb, :, cut(j)].astype(F32) + (inv * back - h_mid[mb, :, cut(j)].astype(F32) * pull)
            ).astype(BF16).astype(F32)
            d = (g * slope[0, :, cut(j)]).astype(BF16)
            dpre[0, mb, :, cut(j)] = d
            if not is_first:
                acc[:, cut(j)] = g
                dots = dots + fold(d.astype(F32) * pre[0, mb, :, cut(j)])
                part = dot(d, wt[0, cut(j), cut(0)])
                opening = part if opening is None else opening + part
        if not is_first:
            inv = inv_keep[0, :, 0:1]
            pull = inv * inv * (1.0 / width) * row_sum(dots)
            for j in range(CUTS):
                back = (opening if j == 0 else dot(dpre[0, mb], wt[0, :, cut(j)])) * gains[0, :, cut(j)]
                g_out[mb, :, cut(j)] = (
                    acc[:, cut(j)] + (inv * back - h_in[mb, :, cut(j)].astype(F32) * pull)
                ).astype(BF16)
                g_piece(mb, j).start()

        send_dpre(0, mb)
        if not is_first:
            send_dpre(1, mb)

        @pl.when(mb < count - 1)
        def _():
            prepare(mb + 1)

        return carry

    @pl.when(backward)
    def _():
        prepare(0)

        @pl.when(first)
        def _():
            lax.fori_loop(0, count, functools.partial(backward_one, is_first=True, is_last=False), 0)

        @pl.when(jnp.logical_and(not_first, not_last))
        def _():
            lax.fori_loop(0, count, functools.partial(backward_one, is_first=False, is_last=False), 0)

        @pl.when(last)
        def _():
            lax.fori_loop(0, count, functools.partial(backward_one, is_first=False, is_last=True), 0)


    @pl.when(odd_core)
    def _():
        @pl.when(last)
        def _():
            for lane, owner in lanes:
                part_copy(lane, owner).start()
            for lane, owner in lanes:
                part_copy(lane, owner).wait_recv()
            loss_all[...] = loss_part[...] + loss_in[1] + loss_in[2] + loss_in[3]

        @pl.when(not_last)
        def _():
            loss_back().wait_recv()

        @pl.when(not_first)
        def _():
            loss_back().start()

        loss_peer().start()

    @pl.when(even_core)
    def _():
        loss_peer().wait_recv()

    live_count = (start * lax.axis_size("dp")).astype(F32)
    loss_ref[0, 0] = loss_all[0, 0] / live_count
    for lane, owner in arrivals:
        n_wait(lane, owner).wait_recv()
        d_wait(lane, owner).wait_recv()

    gather_sent()

    @pl.when(odd_core)
    def _():
        for layer in range(2):
            for lane in (1, 2, 3):
                sent(normed.at[0, :, :, 0:share], n_send.at[layer, lane])
        sent(normed.at[0, :, :, 0:share], n_send.at[0, 0])
        n_local(1).wait()

        @pl.when(late)
        def _():
            for i, ref in enumerate([h_in, h_mid, pre.at[0], pre.at[1]]):
                sent(ref, peer_send.at[i])
            d_wait(0, y).wait_recv()

        @pl.when(not_last)
        def _():
            for j in range(CUTS):
                sent(h_out.at[:, :, cut(j)], h_send.at[j])

        @pl.when(last)
        def _():
            sent(h_out, peer_send.at[4])
            sent(dlog, peer_send.at[5])
            for lane in (1, 2, 3):
                sent(loss_part, part_send.at[lane])

        @pl.when(not_first)
        def _():
            sent(loss_all, loss_send.at[0])

        sent(loss_all, loss_send.at[1])

    @pl.when(even_core)
    def _():
        n_wait(0, y).wait_recv()

        @pl.when(early)
        def _():
            d_wait(0, y).wait_recv()

    @pl.when(backward)
    def _():
        for layer in range(2):
            for lane in (1, 2, 3):
                sent(dpre.at[0], d_send.at[layer, lane])
        sent(dpre.at[0], local_sem.at[1])

        @pl.when(early)
        def _():
            sent(dpre.at[0], d_send.at[0, 0])

        @pl.when(late)
        def _():
            sent(dpre.at[0], d_send.at[1, 0])

        @pl.when(not_first)
        def _():
            for j in range(CUTS):
                sent(g_out.at[:, :, cut(j)], g_send.at[j])


def product_kernel(normed_ref, dpre_ref, out_ref, turned):
    @pl.when(pl.program_id(0) == 0)
    def _():
        turned[...] = normed_ref[...].T

    out_ref[0] = dot(turned[...], dpre_ref[...])


def product(normed, dpre):
    rows, share = normed.shape
    width = dpre.shape[1]
    step = min(512, width)
    return pl.pallas_call(
        product_kernel,
        name="weight_grad",
        grid=(width // step,),
        out_shape=jax.ShapeDtypeStruct((1, share, width), F32),
        in_specs=[
            pl.BlockSpec((rows, share), lambda i: (0, 0)),
            pl.BlockSpec((rows, step), lambda i: (0, i)),
        ],
        out_specs=pl.BlockSpec((1, share, step), lambda i: (0, 0, i)),
        scratch_shapes=[pltpu.VMEM((share, rows), BF16)],
        compiler_params=pltpu.CompilerParams(vmem_limit_bytes=60 * 1024 * 1024),
        cost_estimate=pl.CostEstimate(
            flops=2 * rows * share * width, bytes_accessed=6 * share * width, transcendentals=0
        ),
    )(normed, dpre)


def shards(
    video_ids,
    action_ids,
    target_ids,
    live_lengths,
    video_table,
    action_table,
    layer_gain,
    layer_weight,
    out_gain,
    head_weight,
    live_rows,
):
    width, vocab = head_weight.shape
    share = width // 4
    count = live_rows // ROWS

    vmem = pl.BlockSpec(memory_space=pltpu.VMEM)
    smem = pl.BlockSpec(memory_space=pltpu.SMEM)
    hbm = pl.BlockSpec(memory_space=pl.ANY)
    dma = pltpu.SemaphoreType.DMA
    rows = lambda kind: pltpu.VMEM((count, ROWS, width), kind)
    pair = lambda kind: pltpu.VMEM((2, count, ROWS, width), kind)
    loss, normed, dpre = pl.pallas_call(
        kernel,
        name="stack",
        out_shape=(
            jax.ShapeDtypeStruct((1, 1), F32),
            jax.ShapeDtypeStruct((4, count, ROWS, share), BF16),
            jax.ShapeDtypeStruct((4, count, ROWS, width), BF16),
        ),
        in_specs=[smem, vmem, vmem, vmem, vmem, vmem, vmem, hbm, hbm, hbm],
        out_specs=(smem, hbm, hbm),
        scratch_shapes=[
            pltpu.VMEM((2, width, width), BF16),
            pltpu.VMEM((2, width, width), BF16),
            pltpu.VMEM((width, vocab), BF16),
            pltpu.VMEM((vocab, width), BF16),
            rows(BF16),
            rows(BF16),
            rows(BF16),
            pair(F32),
            pair(BF16),
            pair(BF16),
            rows(BF16),
            rows(BF16),
            pltpu.VMEM((count, ROWS, vocab), BF16),
            pltpu.VMEM((ROWS, width), F32),
            pltpu.VMEM((ROWS, width), BF16),
            pltpu.VMEM((2, ROWS, width), F32),
            pltpu.VMEM((2, ROWS, 128), F32),
            pltpu.VMEM((2, 1, width), F32),
            pltpu.VMEM((live_rows, 128), jnp.int32),
            pltpu.VMEM((8, 128), F32),
            pltpu.VMEM((4, 8, 128), F32),
            pltpu.VMEM((8, 128), F32),
            dma((5, 4)),
            dma((2, 4, 4)),
            dma((2, 4)),
            dma((2, 4)),
            dma((2,)),
            dma((CUTS,)),
            dma((count, CUTS)),
            dma((CUTS,)),
            dma((count, CUTS)),
            dma((6,)),
            dma((6, count)),
            dma((2, 4)),
            dma((4,)),
            dma((2, 4)),
            dma((4,)),
            dma((4,)),
            dma((4,)),
            dma((2,)),
            dma((2,)),
            dma((1,)),
            dma((1,)),
            pltpu.VMEM((2, 4, 2, share // 8, width), BF16),
            dma((7, 2)),
            dma((2, 4, 2)),
            dma((2, 4, 2)),
            dma((2, 4, 2)),
            pltpu.SemaphoreType.REGULAR,
        ],
        compiler_params=pltpu.CompilerParams(
            collective_id=0, has_side_effects=True, vmem_limit_bytes=60 * 1024 * 1024
        ),
        cost_estimate=pl.CostEstimate(flops=10**10, bytes_accessed=2 * 10**7, transcendentals=0),
    )(
        live_lengths,
        video_ids,
        action_ids,
        target_ids,
        layer_gain,
        out_gain[None],
        action_table,
        video_table,
        layer_weight,
        head_weight,
    )
    grad = product(normed.reshape(4 * live_rows, share), dpre.reshape(4 * live_rows, width))
    return (loss[0, 0], grad)


def solution(mesh, live_rows=160):
    in_specs = (
        P("dp", None),
        P("dp", None),
        P("dp", None),
        P("dp", None),
        P(),
        P(),
        P("section", None),
        P("section", "dp", None),
        P(),
        P(),
    )
    out_specs = (P(), P("section", "dp", None))
    return jax.shard_map(
        functools.partial(shards, live_rows=live_rows),
        mesh=mesh,
        in_specs=in_specs,
        out_specs=out_specs,
        check_vma=False,
    )
```

```python
import functools

import jax
import jax.numpy as jnp
from jax import lax
from jax.experimental import pallas as pl
from jax.experimental.pallas import tpu as pltpu
from jax.sharding import PartitionSpec as P

MESH = pl.DeviceIdType.MESH
F32 = jnp.float32
BF16 = jnp.bfloat16
ROWS = 16
PIECES = (2, 2, 2, 2)
CUTS = len(PIECES)
PRE_SCALE = 0.7978845608028654
CUBE = 0.044715


def gelu(x):
    return 0.5 * x * (1.0 + jnp.tanh(PRE_SCALE * (x + CUBE * x * x * x)))


def gelu_slope(x):
    t = jnp.tanh(PRE_SCALE * (x + CUBE * x * x * x))
    return 0.5 * (1.0 + t) + 0.5 * x * (1.0 - t * t) * (PRE_SCALE * (1.0 + 3.0 * CUBE * x * x))


def dot(left, right):
    return jnp.dot(left, right, preferred_element_type=F32)


def row_sum(x):
    return jnp.sum(x, axis=1, keepdims=True)


def kernel(
    lengths_ref,
    video_ids_ref,
    action_ids_ref,
    target_ids_ref,
    gain_ref,
    out_gain_ref,
    actions_ref,
    video_ref,
    weight_ref,
    head_ref,
    loss_ref,
    normed_out,
    dpre_out,
    w,
    wt,
    hw,
    ht,
    h_in,
    h_mid,
    h_out,
    pre,
    normed,
    dpre,
    g_in,
    g_out,
    dlog,
    stats,
    acc,
    raw,
    slope,
    inv_keep,
    gains,
    picked_ids,
    loss_part,
    loss_in,
    loss_all,
    w_send,
    w_recv,
    w_fwd_send,
    w_fwd_recv,
    local_sem,
    h_send,
    h_recv,
    g_send,
    g_recv,
    peer_send,
    peer_recv,
    n_send,
    n_recv,
    d_send,
    d_recv,
    part_send,
    part_recv,
    loss_send,
    loss_recv,
    gain_send,
    gain_recv,
    held,
    held_send,
    held_recv,
    back_send,
    back_recv,
    go_sem,
):
    s = lax.axis_index("section")
    y = lax.axis_index("dp")
    planes = lax.axis_size("section") // 2
    k = s // 2
    core = s % 2
    turning = planes - max(1, planes * 3 // 16)
    late = k >= turning
    early = k < turning
    odd_core = core == 1
    even_core = core == 0
    forward = odd_core
    backward = jnp.logical_or(jnp.logical_and(early, odd_core), jnp.logical_and(late, even_core))
    back_target = 2 * (k - 1) + jnp.where(k - 1 < turning, 1, 0)
    first = k == 0
    last = k == planes - 1
    not_first = k > 0
    not_last = k < planes - 1

    width = w.shape[2]
    share = width // 4
    halves = (share * 3 // 8, share // 8)
    main = 2 * halves[0]
    edges = [width * sum(PIECES[:j]) // sum(PIECES) for j in range(CUTS + 1)]
    count = h_in.shape[0]
    vocab = hw.shape[1]

    up, down, far = (y + 1) % 4, (y + 3) % 4, (y + 2) % 4
    peer = (2 * k + 1 - core, y)
    odd = 2 * k + 1
    even = 2 * k

    def remote(src, dst, send, recv, device):
        return pltpu.make_async_remote_copy(
            src_ref=src, dst_ref=dst, send_sem=send, recv_sem=recv, device_id=device, device_id_type=MESH
        )

    def cut(j):
        return slice(edges[j], edges[j + 1])

    def window(j):
        return pl.ds(edges[j], edges[j + 1] - edges[j])

    barrier = pltpu.get_barrier_semaphore()
    for other in (up, down, far):
        for c in (0, 1):
            pl.semaphore_signal(barrier, inc=1, device_id=(2 * k + c, other), device_id_type=MESH)
    pl.semaphore_signal(barrier, inc=1, device_id=peer, device_id_type=MESH)

    for plane in ((k + 1) % planes, (k + planes - 1) % planes):
        for c in (0, 1):
            pl.semaphore_signal(barrier, inc=1, device_id=(2 * plane + c, y), device_id_type=MESH)

    group = planes // 4
    helped = k < group
    helper = k >= planes - group
    friend = jnp.where(helped, k + planes - group, k - planes + group)

    @pl.when(jnp.logical_or(helped, helper))
    def _():
        for c in (0, 1):
            pl.semaphore_signal(barrier, inc=1, device_id=(2 * friend + c, y), device_id_type=MESH)

    pl.semaphore_wait(barrier, 11 + jnp.where(jnp.logical_or(helped, helper), 2, 0))

    def rows_of(owner):
        return pl.ds(pl.multiple_of(owner * share, share), share)

    def piece(kind, part):
        return kind * main + part * halves[kind], halves[kind]

    def piece_of(owner, kind, part):
        offset, size = piece(kind, part)
        return pl.ds(pl.multiple_of(owner * share + offset, 16), size)

    def direct(layer, lane, kind, part):
        offset, size = piece(kind, part)
        return remote(
            weight_ref.at[0, offset : offset + size, :],
            w.at[layer, piece_of(y, kind, part), :],
            w_send.at[lane, 2 * kind + part],
            w_recv.at[layer, lane, 2 * kind + part],
            (odd, up if lane == 1 else down),
        )

    def relay(layer, kind, part):
        owner, target = (down, up) if part == 0 else (up, down)
        block = w.at[layer, piece_of(owner, kind, part), :]
        return remote(
            block, block, w_send.at[3 + layer, 2 * kind + part], w_recv.at[layer, 3, 2 * kind + part], (odd, target)
        )

    friend_odd = 2 * friend + 1

    def to_helper(layer, part):
        offset, size = piece(1, part)
        return remote(
            weight_ref.at[0, offset : offset + size, :],
            held.at[layer, y, part],
            held_send.at[0, part],
            held_recv.at[layer, 0, part],
            (friend_odd, y),
        )

    def held_direct(layer, lane, part):
        block = held.at[layer, y, part]
        return remote(
            block,
            block,
            held_send.at[1 + 2 * layer + (lane - 1), part],
            held_recv.at[layer, lane, part],
            (odd, up if lane == 1 else down),
        )

    def held_relay(layer, part):
        owner, target = (down, up) if part == 0 else (up, down)
        block = held.at[layer, owner, part]
        return remote(block, block, held_send.at[5 + layer, part], held_recv.at[layer, 3, part], (odd, target))

    owners = {1: down, 2: up, 3: far}

    def hand_back(layer, lane, part):
        return remote(
            held.at[layer, owners[lane], part],
            w.at[layer, piece_of(owners[lane], 1, part), :],
            back_send.at[layer, lane, part],
            back_recv.at[layer, lane, part],
            (friend_odd, y),
        )

    def to_peer(layer, lane, owner):
        block = w.at[layer, rows_of(owner), :]
        return remote(block, block, w_fwd_send.at[layer, lane], w_fwd_recv.at[layer, lane], peer)

    def own_to_peer(layer):
        return remote(
            weight_ref.at[0], w.at[layer, rows_of(y), :], w_fwd_send.at[layer, 0], w_fwd_recv.at[layer, 0], peer
        )

    def own_local(layer):
        return pltpu.make_async_copy(weight_ref.at[0], w.at[layer, rows_of(y), :], local_sem.at[0])

    def start_own(layer):
        @pl.when(helped)
        def _():
            to_helper(layer, 0).start()
            to_helper(layer, 1).start()

        for kind in (0, 1):

            def one_kind(kind=kind):
                direct(layer, 1, kind, 0).start()
                direct(layer, 2, kind, 1).start()
                direct(layer, 1, kind, 1).start()
                direct(layer, 2, kind, 0).start()

            if kind == 0:
                one_kind()
            else:
                pl.when(jnp.logical_not(helped))(one_kind)

    def gain_peer(layer):
        return remote(gain_ref, gains.at[layer], gain_send.at[0], gain_recv.at[0], peer)

    def exchange_gain(layer):
        gain_peer(layer).start()
        gains[layer] = gain_ref[...]

    @pl.when(odd_core)
    def _():
        exchange_gain(1)

        @pl.when(helper)
        def _():
            for part in (0, 1):
                for layer in (0, 1):
                    to_helper(layer, part).wait_recv()
                    held_direct(layer, 1 + part, part).start()
                    held_direct(layer, 2 - part, part).start()
            pl.semaphore_signal(go_sem, inc=1, device_id=peer, device_id_type=MESH)

        @pl.when(helper)
        def _():
            for part in (0, 1):
                for layer in (0, 1):
                    held_direct(layer, 1 + part, part).wait_recv()
                    held_relay(layer, part).start()
                    hand_back(layer, 1 + part, part).start()
                    held_direct(layer, 2 - part, part).wait_recv()
                    hand_back(layer, 2 - part, part).start()
            for part in (0, 1):
                for layer in (0, 1):
                    held_relay(layer, part).wait_recv()
                    hand_back(layer, 3, part).start()

        start_own(1)
        own_local(1).start()

        @pl.when(late)
        def _():
            own_to_peer(1).start()

    @pl.when(even_core)
    def _():
        exchange_gain(0)
        own_to_peer(0).start()

        @pl.when(helper)
        def _():
            pl.semaphore_wait(go_sem, 1)

        start_own(0)

        @pl.when(late)
        def _():
            own_local(0).start()

    @pl.when(last)
    def _():
        pltpu.make_async_copy(head_ref, hw, local_sem.at[1]).start()

    @pl.when(jnp.logical_and(first, forward))
    def _():
        pltpu.make_async_copy(video_ref, ht, local_sem.at[1]).start()

    total = count * ROWS
    slots = video_ids_ref.shape[1]
    place = lax.broadcasted_iota(jnp.int32, (total, slots), 0)
    lane_of = lax.broadcasted_iota(jnp.int32, (total, slots), 1)
    chosen = [jnp.zeros((total, 1), jnp.int32) for _ in range(3)]
    start = jnp.int32(0)
    for b in range(video_ids_ref.shape[0]):
        length = lengths_ref[0, b]
        hit = jnp.logical_and(place == start + lane_of, lane_of < length)
        for kind, ids_ref in enumerate((video_ids_ref, action_ids_ref, target_ids_ref)):
            line = jnp.broadcast_to(ids_ref[b : b + 1, :], (total, slots))
            chosen[kind] = chosen[kind] + row_sum(jnp.where(hit, line, 0))
        start = start + length
    picked_ids[...] = jnp.broadcast_to(chosen[2], picked_ids.shape)

    @pl.when(jnp.logical_and(first, forward))
    def _():
        pltpu.make_async_copy(video_ref, ht, local_sem.at[1]).wait()
        video_hot = (chosen[0] == lax.broadcasted_iota(jnp.int32, (total, ht.shape[0]), 1)).astype(F32).astype(BF16)
        kinds = actions_ref.shape[0]
        for j in range(CUTS):
            cols = cut(j)
            rows = dot(video_hot, ht[:, cols])
            for a in range(kinds):
                rows = rows + jnp.where(chosen[1] == a, actions_ref[a : a + 1, cols].astype(F32), 0.0)
            h_in[:, :, cols] = rows.astype(BF16).reshape(count, ROWS, -1)

    block = min(512, width)

    def turn(layer, owner):
        def one(i, carry):
            cols = pl.ds(pl.multiple_of(i * block, block), block)
            wt[layer, cols, rows_of(owner)] = w[layer, rows_of(owner), cols].T
            return carry

        lax.fori_loop(0, width // block, one, 0)

    gain_peer(0).wait_recv()

    def ring(kind):
        for layer in range(2):
            direct(layer, 1, kind, 0).wait_recv()
            relay(layer, kind, 0).start()
            direct(layer, 2, kind, 1).wait_recv()
            relay(layer, kind, 1).start()

    def ring_rest(kind):
        for layer in range(2):
            direct(layer, 1, kind, 1).wait_recv()
            direct(layer, 2, kind, 0).wait_recv()

    def ring_far(kind):
        for layer in range(2):
            relay(layer, kind, 0).wait_recv()
            relay(layer, kind, 1).wait_recv()

    @pl.when(odd_core)
    def _():
        ring(0)
        own_local(1).wait()
        own_to_peer(0).wait_recv()

        @pl.when(helped)
        def _():
            ring_rest(0)
            ring_far(0)
            for layer in range(2):
                for lane in (1, 2, 3):
                    for part in (0, 1):
                        hand_back(layer, lane, part).wait_recv()

        @pl.when(jnp.logical_not(helped))
        def _():
            ring(1)
            ring_rest(0)
            ring_rest(1)

            @pl.when(late)
            def _():
                for layer in range(2):
                    to_peer(layer, 1, down).start()
                    to_peer(layer, 2, up).start()

            @pl.when(early)
            def _():
                for layer in range(2):
                    for owner in (y, down, up):
                        turn(layer, owner)

            ring_far(0)
            ring_far(1)

            @pl.when(late)
            def _():
                for layer in range(2):
                    to_peer(layer, 3, far).start()

    @pl.when(jnp.logical_and(last, forward))
    def _():
        pltpu.make_async_copy(head_ref, hw, local_sem.at[1]).wait()

    @pl.when(jnp.logical_and(late, even_core))
    def _():
        own_local(0).wait()
        turn(0, y)
        own_to_peer(1).wait_recv()
        turn(1, y)
        for lane, owner in ((1, down), (2, up), (3, far)):
            for layer in range(2):
                to_peer(layer, lane, owner).wait_recv()
                turn(layer, owner)

    @pl.when(jnp.logical_and(last, backward))
    def _():
        pltpu.make_async_copy(head_ref, hw, local_sem.at[1]).wait()
        for i in range(CUTS):
            ht[:, cut(i)] = hw[cut(i), :].T

    def sent(ref, sem):
        pltpu.make_async_copy(ref, ref, sem).wait()

    def gather_sent():
        sent(gain_ref, gain_send.at[0])

        def parts_sent(send, kind):
            for part in (0, 1):
                sent(w.at[0, 0 : halves[kind], :], send.at[2 * kind + part])

        for lane in (1, 2):
            parts_sent(w_send.at[lane], 0)

        @pl.when(jnp.logical_not(helped))
        def _():
            for lane in (1, 2):
                parts_sent(w_send.at[lane], 1)

        @pl.when(helped)
        def _():
            for part in (0, 1):
                sent(held.at[0, 0, 0], held_send.at[0, part])

        @pl.when(odd_core)
        def _():
            for layer in (0, 1):
                parts_sent(w_send.at[3 + layer], 0)

            @pl.when(jnp.logical_not(helped))
            def _():
                for layer in (0, 1):
                    parts_sent(w_send.at[3 + layer], 1)

            @pl.when(helper)
            def _():
                for part in (0, 1):
                    for i in range(1, 7):
                        sent(held.at[0, 0, 0], held_send.at[i, part])
                    for layer in (0, 1):
                        for lane in (1, 2, 3):
                            sent(held.at[0, 0, 0], back_send.at[layer, lane, part])

            @pl.when(late)
            def _():
                sent(w.at[0, 0:share, :], w_fwd_send.at[1, 0])
                for layer in range(2):
                    for lane in (1, 2, 3):
                        sent(w.at[0, 0:share, :], w_fwd_send.at[layer, lane])

        @pl.when(even_core)
        def _():
            sent(w.at[0, 0:share, :], w_fwd_send.at[0, 0])

    def h_piece(mb, j):
        cols = window(j)
        return remote(
            h_out.at[mb, :, cols], h_in.at[mb, :, cols], h_send.at[j], h_recv.at[mb, j], (s + 2, y)
        )

    def peer_copies(mb):
        refs = [h_in, h_mid, pre.at[0], pre.at[1]]
        return [
            remote(ref.at[mb], ref.at[mb], peer_send.at[i], peer_recv.at[i, mb], peer) for i, ref in enumerate(refs)
        ]

    def head_copies(mb):
        return [
            remote(ref.at[mb], ref.at[mb], peer_send.at[4 + i], peer_recv.at[4 + i, mb], peer)
            for i, ref in enumerate([h_out, dlog, stats])
        ]

    def inverse(squares):
        return lax.rsqrt(squares * (1.0 / width) + 1e-05)

    def fold(x):
        return sum(x[:, i : i + 128] for i in range(0, x.shape[1], 128))

    def forward_one(mb, carry, is_first, is_last):
        squares = jnp.zeros((ROWS, 128), F32)
        for j in range(CUTS):
            if not is_first:
                h_piece(mb, j).wait_recv()
            h = h_in[mb, :, cut(j)].astype(F32)
            squares = squares + fold(h * h)
            product = dot((h * gains[0, :, cut(j)]).astype(BF16), w[0, cut(j), :])
            if j == 0:
                acc[...] = product
            else:
                acc[...] += product
        inv = inverse(row_sum(squares))
        squares = jnp.zeros((ROWS, 128), F32)
        opening = None
        for j in range(CUTS):
            h = h_in[mb, :, cut(j)].astype(F32)
            at = acc[:, cut(j)] * inv
            pre[0, mb, :, cut(j)] = at
            result = (h + gelu(at)).astype(BF16)
            h_mid[mb, :, cut(j)] = result
            wide = result.astype(F32)
            squares = squares + fold(wide * wide)
            scaled = (wide * gains[1, :, cut(j)]).astype(BF16)
            raw[:, cut(j)] = scaled
            part = dot(scaled, w[1, cut(j), cut(0)])
            opening = part if opening is None else opening + part
        inv_mid = inverse(row_sum(squares))
        squares = jnp.zeros((ROWS, 128), F32)
        for j in range(CUTS):
            at = (opening if j == 0 else dot(raw[...], w[1, :, cut(j)])) * inv_mid
            result = (h_mid[mb, :, cut(j)].astype(F32) + gelu(at)).astype(BF16)
            h_out[mb, :, cut(j)] = result
            if not is_last:
                h_piece(mb, j).start()
            pre[1, mb, :, cut(j)] = at
            wide = result.astype(F32)
            squares = squares + fold(wide * wide)
        for j in range(CUTS):
            normed[0, mb, :, cut(j)] = (
                h_in[mb, :, cut(j)].astype(F32) * inv * gains[0, :, cut(j)]
            ).astype(BF16)
            normed[1, mb, :, cut(j)] = (
                h_mid[mb, :, cut(j)].astype(F32) * inv_mid * gains[1, :, cut(j)]
            ).astype(BF16)

        @pl.when(late)
        def _():
            for copy in peer_copies(mb):
                copy.start()

        if is_last:
            scale = inverse(row_sum(squares))
            z = (h_out[mb].astype(F32) * scale * out_gain_ref[...]).astype(BF16)
            logits = dot(z, hw[...])
            top = jnp.max(logits, axis=1, keepdims=True)
            exponents = jnp.exp(logits - top)
            denominator = row_sum(exponents)
            target = picked_ids[pl.ds(pl.multiple_of(mb * ROWS, ROWS), ROWS), 0:1]
            one_hot = (target == lax.broadcasted_iota(jnp.int32, logits.shape, 1)).astype(F32)
            picked = row_sum(logits * one_hot)
            d = (exponents / denominator - one_hot).astype(BF16)
            dlog[mb] = d
            pull = scale * scale * (1.0 / width) * row_sum(d.astype(F32) * logits)
            stats[mb, 0] = jnp.broadcast_to(scale, stats.shape[2:])
            stats[mb, 1] = jnp.broadcast_to(pull, stats.shape[2:])
            for copy in head_copies(mb):
                copy.start()
            losses = jnp.sum(jnp.log(denominator) + top - picked, axis=0, keepdims=True)
            loss_part[...] += jnp.broadcast_to(losses, loss_part.shape)

        return carry

    def part_copy(lane, target):
        return remote(loss_part, loss_in.at[lane], part_send.at[lane], part_recv.at[lane], (odd, target))

    def loss_back():
        return remote(loss_all, loss_all, loss_send.at[0], loss_recv.at[0], (s - 2, y))

    def loss_peer():
        return remote(loss_all, loss_all, loss_send.at[1], loss_recv.at[1], peer)

    def n_copy(layer, owner, lane):
        src = normed.at[layer, :, :, pl.ds(pl.multiple_of(owner * share, share), share)]
        return remote(src, normed_out.at[y], n_send.at[layer, lane], n_recv.at[lane], (2 * k + layer, owner))

    def n_local(layer):
        src = normed.at[layer, :, :, pl.ds(pl.multiple_of(y * share, share), share)]
        return pltpu.make_async_copy(src, normed_out.at[y], local_sem.at[0])

    def n_wait(lane, owner):
        src = normed.at[0, :, :, pl.ds(0, share)]
        return remote(src, normed_out.at[owner], n_send.at[0, lane], n_recv.at[lane], peer)

    def d_copy(layer, owner, lane, mb):
        return remote(
            dpre.at[layer, mb], dpre_out.at[y, mb], d_send.at[layer, lane], d_recv.at[lane], (2 * k + layer, owner)
        )

    def send_dpre(layer, mb):
        for lane, owner in lanes:
            d_copy(layer, owner, lane, mb).start()
        here = early if layer == 1 else late

        @pl.when(here)
        def _():
            d_local(layer, mb).start()

        @pl.when(jnp.logical_not(here))
        def _():
            d_copy(layer, y, 0, mb).start()

    def d_local(layer, mb):
        return pltpu.make_async_copy(dpre.at[layer, mb], dpre_out.at[y, mb], local_sem.at[1])

    def d_wait(lane, owner):
        return remote(dpre.at[0], dpre_out.at[owner], d_send.at[0, lane], d_recv.at[lane], peer)

    lanes = ((1, up), (2, down), (3, far))
    arrivals = ((1, down), (2, up), (3, far))

    @pl.when(forward)
    def _():
        loss_part[...] = jnp.zeros_like(loss_part)

        @pl.when(first)
        def _():
            lax.fori_loop(0, count, functools.partial(forward_one, is_first=True, is_last=False), 0)

        @pl.when(jnp.logical_and(not_first, not_last))
        def _():
            lax.fori_loop(0, count, functools.partial(forward_one, is_first=False, is_last=False), 0)

        @pl.when(last)
        def _():
            lax.fori_loop(0, count, functools.partial(forward_one, is_first=False, is_last=True), 0)

        for layer in range(2):
            for lane, owner in lanes:
                n_copy(layer, owner, lane).start()
        n_copy(0, y, 0).start()
        n_local(1).start()

        @pl.when(early)
        def _():
            for layer in range(2):
                turn(layer, far)

        @pl.when(helped)
        def _():
            for layer in range(2):
                for owner in (y, down, up):
                    turn(layer, owner)

    def g_piece(mb, j):
        cols = window(j)
        return remote(
            g_out.at[mb, :, cols], g_in.at[mb, :, cols], g_send.at[j], g_recv.at[mb, j], (back_target, y)
        )

    def prepare(mb):
        @pl.when(late)
        def _():
            for copy in peer_copies(mb):
                copy.wait_recv()

        for layer, rows in ((0, h_in), (1, h_mid)):
            squares = jnp.zeros((ROWS, 1), F32)
            for j in range(CUTS):
                h = rows[mb, :, cut(j)].astype(F32)
                squares = squares + row_sum(h * h)
                slope[layer, :, cut(j)] = gelu_slope(pre[layer, mb, :, cut(j)])
            inv_keep[layer] = jnp.broadcast_to(inverse(squares), inv_keep.shape[1:])

    def backward_one(mb, carry, is_first, is_last):
        if is_last:
            for copy in head_copies(mb):
                copy.wait_recv()
            scale, pull = stats[mb, 0, :, 0:1], stats[mb, 1, :, 0:1]
            ahead = dot(dlog[mb], ht[:, cut(0)])

        dots = jnp.zeros((ROWS, 128), F32)
        for j in range(CUTS):
            if not is_last:
                g_piece(mb, j).wait_recv()
            else:
                back = ahead * out_gain_ref[:, cut(j)]
                if j + 1 < CUTS:
                    ahead = dot(dlog[mb], ht[:, cut(j + 1)])
                g_in[mb, :, cut(j)] = (scale * back - h_out[mb, :, cut(j)].astype(F32) * pull).astype(BF16)
            d = (g_in[mb, :, cut(j)].astype(F32) * slope[1, :, cut(j)]).astype(BF16)
            dpre[1, mb, :, cut(j)] = d
            dots = dots + fold(d.astype(F32) * pre[1, mb, :, cut(j)])
            product = dot(d, wt[1, cut(j), :])
            if j == 0:
                acc[...] = product
            else:
                acc[...] += product
        if is_first:
            send_dpre(1, mb)
        inv = inv_keep[1, :, 0:1]
        pull = inv * inv * (1.0 / width) * row_sum(dots)
        dots = jnp.zeros((ROWS, 128), F32)
        opening = None
        for j in range(CUTS):
            back = acc[:, cut(j)] * gains[1, :, cut(j)]
            g = (
                g_in[mb, :, cut(j)].astype(F32) + (inv * back - h_mid[mb, :, cut(j)].astype(F32) * pull)
            ).astype(BF16).astype(F32)
            d = (g * slope[0, :, cut(j)]).astype(BF16)
            dpre[0, mb, :, cut(j)] = d
            if not is_first:
                acc[:, cut(j)] = g
                dots = dots + fold(d.astype(F32) * pre[0, mb, :, cut(j)])
                part = dot(d, wt[0, cut(j), cut(0)])
                opening = part if opening is None else opening + part
        if not is_first:
            inv = inv_keep[0, :, 0:1]
            pull = inv * inv * (1.0 / width) * row_sum(dots)
            for j in range(CUTS):
                back = (opening if j == 0 else dot(dpre[0, mb], wt[0, :, cut(j)])) * gains[0, :, cut(j)]
                g_out[mb, :, cut(j)] = (
                    acc[:, cut(j)] + (inv * back - h_in[mb, :, cut(j)].astype(F32) * pull)
                ).astype(BF16)
                g_piece(mb, j).start()

        send_dpre(0, mb)
        if not is_first:
            send_dpre(1, mb)

        @pl.when(mb < count - 1)
        def _():
            prepare(mb + 1)

        return carry

    @pl.when(backward)
    def _():
        prepare(0)

        @pl.when(first)
        def _():
            lax.fori_loop(0, count, functools.partial(backward_one, is_first=True, is_last=False), 0)

        @pl.when(jnp.logical_and(not_first, not_last))
        def _():
            lax.fori_loop(0, count, functools.partial(backward_one, is_first=False, is_last=False), 0)

        @pl.when(last)
        def _():
            lax.fori_loop(0, count, functools.partial(backward_one, is_first=False, is_last=True), 0)


    @pl.when(odd_core)
    def _():
        @pl.when(last)
        def _():
            for lane, owner in lanes:
                part_copy(lane, owner).start()
            for lane, owner in lanes:
                part_copy(lane, owner).wait_recv()
            loss_all[...] = loss_part[...] + loss_in[1] + loss_in[2] + loss_in[3]

        @pl.when(not_last)
        def _():
            loss_back().wait_recv()

        @pl.when(not_first)
        def _():
            loss_back().start()

        loss_peer().start()

    @pl.when(even_core)
    def _():
        loss_peer().wait_recv()

    live_count = (start * lax.axis_size("dp")).astype(F32)
    loss_ref[0, 0] = loss_all[0, 0] / live_count
    for lane, owner in arrivals:
        n_wait(lane, owner).wait_recv()
        d_wait(lane, owner).wait_recv()

    gather_sent()

    @pl.when(odd_core)
    def _():
        for layer in range(2):
            for lane in (1, 2, 3):
                sent(normed.at[0, :, :, 0:share], n_send.at[layer, lane])
        sent(normed.at[0, :, :, 0:share], n_send.at[0, 0])
        n_local(1).wait()

        @pl.when(late)
        def _():
            for i, ref in enumerate([h_in, h_mid, pre.at[0], pre.at[1]]):
                sent(ref, peer_send.at[i])
            d_wait(0, y).wait_recv()

        @pl.when(not_last)
        def _():
            for j in range(CUTS):
                sent(h_out.at[:, :, cut(j)], h_send.at[j])

        @pl.when(last)
        def _():
            sent(h_out, peer_send.at[4])
            sent(dlog, peer_send.at[5])
            sent(stats, peer_send.at[6])
            for lane in (1, 2, 3):
                sent(loss_part, part_send.at[lane])

        @pl.when(not_first)
        def _():
            sent(loss_all, loss_send.at[0])

        sent(loss_all, loss_send.at[1])

    @pl.when(even_core)
    def _():
        n_wait(0, y).wait_recv()

        @pl.when(early)
        def _():
            d_wait(0, y).wait_recv()

    @pl.when(backward)
    def _():
        for layer in range(2):
            for lane in (1, 2, 3):
                sent(dpre.at[0], d_send.at[layer, lane])
        sent(dpre.at[0], local_sem.at[1])

        @pl.when(early)
        def _():
            sent(dpre.at[0], d_send.at[0, 0])

        @pl.when(late)
        def _():
            sent(dpre.at[0], d_send.at[1, 0])

        @pl.when(not_first)
        def _():
            for j in range(CUTS):
                sent(g_out.at[:, :, cut(j)], g_send.at[j])


def product_kernel(normed_ref, dpre_ref, out_ref, turned):
    @pl.when(pl.program_id(0) == 0)
    def _():
        turned[...] = normed_ref[...].T

    out_ref[0] = dot(turned[...], dpre_ref[...])


def product(normed, dpre):
    rows, share = normed.shape
    width = dpre.shape[1]
    step = min(512, width)
    return pl.pallas_call(
        product_kernel,
        name="weight_grad",
        grid=(width // step,),
        out_shape=jax.ShapeDtypeStruct((1, share, width), F32),
        in_specs=[
            pl.BlockSpec((rows, share), lambda i: (0, 0)),
            pl.BlockSpec((rows, step), lambda i: (0, i)),
        ],
        out_specs=pl.BlockSpec((1, share, step), lambda i: (0, 0, i)),
        scratch_shapes=[pltpu.VMEM((share, rows), BF16)],
        compiler_params=pltpu.CompilerParams(vmem_limit_bytes=60 * 1024 * 1024),
        cost_estimate=pl.CostEstimate(
            flops=2 * rows * share * width, bytes_accessed=6 * share * width, transcendentals=0
        ),
    )(normed, dpre)


def shards(
    video_ids,
    action_ids,
    target_ids,
    live_lengths,
    video_table,
    action_table,
    layer_gain,
    layer_weight,
    out_gain,
    head_weight,
    live_rows,
):
    width, vocab = head_weight.shape
    share = width // 4
    count = live_rows // ROWS

    vmem = pl.BlockSpec(memory_space=pltpu.VMEM)
    smem = pl.BlockSpec(memory_space=pltpu.SMEM)
    hbm = pl.BlockSpec(memory_space=pl.ANY)
    dma = pltpu.SemaphoreType.DMA
    rows = lambda kind: pltpu.VMEM((count, ROWS, width), kind)
    pair = lambda kind: pltpu.VMEM((2, count, ROWS, width), kind)
    loss, normed, dpre = pl.pallas_call(
        kernel,
        name="stack",
        out_shape=(
            jax.ShapeDtypeStruct((1, 1), F32),
            jax.ShapeDtypeStruct((4, count, ROWS, share), BF16),
            jax.ShapeDtypeStruct((4, count, ROWS, width), BF16),
        ),
        in_specs=[smem, vmem, vmem, vmem, vmem, vmem, vmem, hbm, hbm, hbm],
        out_specs=(smem, hbm, hbm),
        scratch_shapes=[
            pltpu.VMEM((2, width, width), BF16),
            pltpu.VMEM((2, width, width), BF16),
            pltpu.VMEM((width, vocab), BF16),
            pltpu.VMEM((vocab, width), BF16),
            rows(BF16),
            rows(BF16),
            rows(BF16),
            pair(F32),
            pair(BF16),
            pair(BF16),
            rows(BF16),
            rows(BF16),
            pltpu.VMEM((count, ROWS, vocab), BF16),
            pltpu.VMEM((count, 2, ROWS, 128), F32),
            pltpu.VMEM((ROWS, width), F32),
            pltpu.VMEM((ROWS, width), BF16),
            pltpu.VMEM((2, ROWS, width), F32),
            pltpu.VMEM((2, ROWS, 128), F32),
            pltpu.VMEM((2, 1, width), F32),
            pltpu.VMEM((live_rows, 128), jnp.int32),
            pltpu.VMEM((8, 128), F32),
            pltpu.VMEM((4, 8, 128), F32),
            pltpu.VMEM((8, 128), F32),
            dma((5, 4)),
            dma((2, 4, 4)),
            dma((2, 4)),
            dma((2, 4)),
            dma((2,)),
            dma((CUTS,)),
            dma((count, CUTS)),
            dma((CUTS,)),
            dma((count, CUTS)),
            dma((7,)),
            dma((7, count)),
            dma((2, 4)),
            dma((4,)),
            dma((2, 4)),
            dma((4,)),
            dma((4,)),
            dma((4,)),
            dma((2,)),
            dma((2,)),
            dma((1,)),
            dma((1,)),
            pltpu.VMEM((2, 4, 2, share // 8, width), BF16),
            dma((7, 2)),
            dma((2, 4, 2)),
            dma((2, 4, 2)),
            dma((2, 4, 2)),
            pltpu.SemaphoreType.REGULAR,
        ],
        compiler_params=pltpu.CompilerParams(
            collective_id=0, has_side_effects=True, vmem_limit_bytes=60 * 1024 * 1024
        ),
        cost_estimate=pl.CostEstimate(flops=10**10, bytes_accessed=2 * 10**7, transcendentals=0),
    )(
        live_lengths,
        video_ids,
        action_ids,
        target_ids,
        layer_gain,
        out_gain[None],
        action_table,
        video_table,
        layer_weight,
        head_weight,
    )
    grad = product(normed.reshape(4 * live_rows, share), dpre.reshape(4 * live_rows, width))
    return (loss[0, 0], grad)


def solution(mesh, live_rows=160):
    in_specs = (
        P("dp", None),
        P("dp", None),
        P("dp", None),
        P("dp", None),
        P(),
        P(),
        P("section", None),
        P("section", "dp", None),
        P(),
        P(),
    )
    out_specs = (P(), P("section", "dp", None))
    return jax.shard_map(
        functools.partial(shards, live_rows=live_rows),
        mesh=mesh,
        in_specs=in_specs,
        out_specs=out_specs,
        check_vma=False,
    )
```

```python
import functools

import jax
import jax.numpy as jnp
from jax import lax
from jax.experimental import pallas as pl
from jax.experimental.pallas import tpu as pltpu
from jax.sharding import PartitionSpec as P

MESH = pl.DeviceIdType.MESH
F32 = jnp.float32
BF16 = jnp.bfloat16
ROWS = 16
PIECES = (2, 2, 2, 2)
CUTS = len(PIECES)
PRE_SCALE = 0.7978845608028654
CUBE = 0.044715


def gelu(x):
    return 0.5 * x * (1.0 + jnp.tanh(PRE_SCALE * (x + CUBE * x * x * x)))


def gelu_slope(x):
    t = jnp.tanh(PRE_SCALE * (x + CUBE * x * x * x))
    return 0.5 * (1.0 + t) + 0.5 * x * (1.0 - t * t) * (PRE_SCALE * (1.0 + 3.0 * CUBE * x * x))


def dot(left, right):
    return jnp.dot(left, right, preferred_element_type=F32)


def row_sum(x):
    return jnp.sum(x, axis=1, keepdims=True)


def kernel(
    lengths_ref,
    video_ids_ref,
    action_ids_ref,
    target_ids_ref,
    gain_ref,
    out_gain_ref,
    actions_ref,
    video_ref,
    weight_ref,
    head_ref,
    loss_ref,
    normed_out,
    dpre_out,
    w,
    wt,
    hw,
    ht,
    h_in,
    h_mid,
    h_out,
    pre,
    normed,
    dpre,
    g_in,
    g_out,
    dlog,
    stats,
    acc,
    raw,
    slope,
    inv_keep,
    gains,
    picked_ids,
    loss_part,
    loss_in,
    loss_all,
    w_send,
    w_recv,
    w_fwd_send,
    w_fwd_recv,
    local_sem,
    h_send,
    h_recv,
    g_send,
    g_recv,
    peer_send,
    peer_recv,
    n_send,
    n_recv,
    d_send,
    d_recv,
    part_send,
    part_recv,
    loss_send,
    loss_recv,
    gain_send,
    gain_recv,
    held,
    held_send,
    held_recv,
    back_send,
    back_recv,
    go_sem,
):
    s = lax.axis_index("section")
    y = lax.axis_index("dp")
    planes = lax.axis_size("section") // 2
    k = s // 2
    core = s % 2
    turning = planes - max(1, planes * 3 // 16)
    late = k >= turning
    early = k < turning
    odd_core = core == 1
    even_core = core == 0
    forward = odd_core
    backward = jnp.logical_or(jnp.logical_and(early, odd_core), jnp.logical_and(late, even_core))
    back_target = 2 * (k - 1) + jnp.where(k - 1 < turning, 1, 0)
    first = k == 0
    last = k == planes - 1
    not_first = k > 0
    not_last = k < planes - 1

    width = w.shape[2]
    share = width // 4
    halves = (share * 3 // 8, share // 8)
    main = 2 * halves[0]
    edges = [width * sum(PIECES[:j]) // sum(PIECES) for j in range(CUTS + 1)]
    count = h_in.shape[0]
    vocab = hw.shape[1]

    up, down, far = (y + 1) % 4, (y + 3) % 4, (y + 2) % 4
    peer = (2 * k + 1 - core, y)
    odd = 2 * k + 1
    even = 2 * k

    def remote(src, dst, send, recv, device):
        return pltpu.make_async_remote_copy(
            src_ref=src, dst_ref=dst, send_sem=send, recv_sem=recv, device_id=device, device_id_type=MESH
        )

    def cut(j):
        return slice(edges[j], edges[j + 1])

    def window(j):
        return pl.ds(edges[j], edges[j + 1] - edges[j])

    barrier = pltpu.get_barrier_semaphore()
    for other in (up, down, far):
        for c in (0, 1):
            pl.semaphore_signal(barrier, inc=1, device_id=(2 * k + c, other), device_id_type=MESH)
    pl.semaphore_signal(barrier, inc=1, device_id=peer, device_id_type=MESH)

    for plane in ((k + 1) % planes, (k + planes - 1) % planes):
        for c in (0, 1):
            pl.semaphore_signal(barrier, inc=1, device_id=(2 * plane + c, y), device_id_type=MESH)

    group = planes // 4
    helped = k < group
    helper = k >= planes - group
    friend = jnp.where(helped, k + planes - group, k - planes + group)

    @pl.when(jnp.logical_or(helped, helper))
    def _():
        for c in (0, 1):
            pl.semaphore_signal(barrier, inc=1, device_id=(2 * friend + c, y), device_id_type=MESH)

    pl.semaphore_wait(barrier, 11 + jnp.where(jnp.logical_or(helped, helper), 2, 0))

    def rows_of(owner):
        return pl.ds(pl.multiple_of(owner * share, share), share)

    def piece(kind, part):
        return kind * main + part * halves[kind], halves[kind]

    def piece_of(owner, kind, part):
        offset, size = piece(kind, part)
        return pl.ds(pl.multiple_of(owner * share + offset, 16), size)

    def direct(layer, lane, kind, part):
        offset, size = piece(kind, part)
        return remote(
            weight_ref.at[0, offset : offset + size, :],
            w.at[layer, piece_of(y, kind, part), :],
            w_send.at[lane, 2 * kind + part],
            w_recv.at[layer, lane, 2 * kind + part],
            (odd, up if lane == 1 else down),
        )

    def relay(layer, kind, part):
        owner, target = (down, up) if part == 0 else (up, down)
        block = w.at[layer, piece_of(owner, kind, part), :]
        return remote(
            block, block, w_send.at[3 + layer, 2 * kind + part], w_recv.at[layer, 3, 2 * kind + part], (odd, target)
        )

    friend_odd = 2 * friend + 1

    def to_helper(layer, part):
        offset, size = piece(1, part)
        return remote(
            weight_ref.at[0, offset : offset + size, :],
            held.at[layer, y, part],
            held_send.at[0, part],
            held_recv.at[layer, 0, part],
            (friend_odd, y),
        )

    def held_direct(layer, lane, part):
        block = held.at[layer, y, part]
        return remote(
            block,
            block,
            held_send.at[1 + 2 * layer + (lane - 1), part],
            held_recv.at[layer, lane, part],
            (odd, up if lane == 1 else down),
        )

    def held_relay(layer, part):
        owner, target = (down, up) if part == 0 else (up, down)
        block = held.at[layer, owner, part]
        return remote(block, block, held_send.at[5 + layer, part], held_recv.at[layer, 3, part], (odd, target))

    owners = {1: down, 2: up, 3: far}

    def hand_back(layer, lane, part):
        return remote(
            held.at[layer, owners[lane], part],
            w.at[layer, piece_of(owners[lane], 1, part), :],
            back_send.at[layer, lane, part],
            back_recv.at[layer, lane, part],
            (friend_odd, y),
        )

    def to_peer(layer, lane, owner):
        block = w.at[layer, rows_of(owner), :]
        return remote(block, block, w_fwd_send.at[layer, lane], w_fwd_recv.at[layer, lane], peer)

    def own_to_peer(layer):
        return remote(
            weight_ref.at[0], w.at[layer, rows_of(y), :], w_fwd_send.at[layer, 0], w_fwd_recv.at[layer, 0], peer
        )

    def own_local(layer):
        return pltpu.make_async_copy(weight_ref.at[0], w.at[layer, rows_of(y), :], local_sem.at[0])

    def start_own(layer):
        @pl.when(helped)
        def _():
            to_helper(layer, 0).start()
            to_helper(layer, 1).start()

        for kind in (0, 1):

            def one_kind(kind=kind):
                direct(layer, 1, kind, 0).start()
                direct(layer, 2, kind, 1).start()
                direct(layer, 1, kind, 1).start()
                direct(layer, 2, kind, 0).start()

            if kind == 0:
                one_kind()
            else:
                pl.when(jnp.logical_not(helped))(one_kind)

    def gain_peer(layer):
        return remote(gain_ref, gains.at[layer], gain_send.at[0], gain_recv.at[0], peer)

    def exchange_gain(layer):
        gain_peer(layer).start()
        gains[layer] = gain_ref[...]

    @pl.when(odd_core)
    def _():
        exchange_gain(1)

        @pl.when(helper)
        def _():
            for part in (0, 1):
                for layer in (0, 1):
                    to_helper(layer, part).wait_recv()
                    held_direct(layer, 1 + part, part).start()
                    held_direct(layer, 2 - part, part).start()
            pl.semaphore_signal(go_sem, inc=1, device_id=peer, device_id_type=MESH)

        @pl.when(helper)
        def _():
            for part in (0, 1):
                for layer in (0, 1):
                    held_direct(layer, 1 + part, part).wait_recv()
                    held_relay(layer, part).start()
                    hand_back(layer, 1 + part, part).start()
                    held_direct(layer, 2 - part, part).wait_recv()
                    hand_back(layer, 2 - part, part).start()
            for part in (0, 1):
                for layer in (0, 1):
                    held_relay(layer, part).wait_recv()
                    hand_back(layer, 3, part).start()

        start_own(1)
        own_local(1).start()

        @pl.when(late)
        def _():
            own_to_peer(1).start()

    @pl.when(even_core)
    def _():
        exchange_gain(0)
        own_to_peer(0).start()

        @pl.when(helper)
        def _():
            pl.semaphore_wait(go_sem, 1)

        start_own(0)

        @pl.when(late)
        def _():
            own_local(0).start()

    @pl.when(last)
    def _():
        pltpu.make_async_copy(head_ref, hw, local_sem.at[1]).start()

    @pl.when(jnp.logical_and(first, forward))
    def _():
        pltpu.make_async_copy(video_ref, ht, local_sem.at[1]).start()

    total = count * ROWS
    slots = video_ids_ref.shape[1]
    place = lax.broadcasted_iota(jnp.int32, (total, slots), 0)
    lane_of = lax.broadcasted_iota(jnp.int32, (total, slots), 1)
    chosen = [jnp.zeros((total, 1), jnp.int32) for _ in range(3)]
    start = jnp.int32(0)
    for b in range(video_ids_ref.shape[0]):
        length = lengths_ref[0, b]
        hit = jnp.logical_and(place == start + lane_of, lane_of < length)
        for kind, ids_ref in enumerate((video_ids_ref, action_ids_ref, target_ids_ref)):
            line = jnp.broadcast_to(ids_ref[b : b + 1, :], (total, slots))
            chosen[kind] = chosen[kind] + row_sum(jnp.where(hit, line, 0))
        start = start + length
    picked_ids[...] = jnp.broadcast_to(chosen[2], picked_ids.shape)

    @pl.when(jnp.logical_and(first, forward))
    def _():
        pltpu.make_async_copy(video_ref, ht, local_sem.at[1]).wait()
        video_hot = (chosen[0] == lax.broadcasted_iota(jnp.int32, (total, ht.shape[0]), 1)).astype(F32).astype(BF16)
        kinds = actions_ref.shape[0]
        for j in range(CUTS):
            cols = cut(j)
            rows = dot(video_hot, ht[:, cols])
            for a in range(kinds):
                rows = rows + jnp.where(chosen[1] == a, actions_ref[a : a + 1, cols].astype(F32), 0.0)
            h_in[:, :, cols] = rows.astype(BF16).reshape(count, ROWS, -1)

    block = min(512, width)

    def turn(layer, owner):
        def one(i, carry):
            cols = pl.ds(pl.multiple_of(i * block, block), block)
            wt[layer, cols, rows_of(owner)] = w[layer, rows_of(owner), cols].T
            return carry

        lax.fori_loop(0, width // block, one, 0)

    gain_peer(0).wait_recv()

    def ring(kind):
        for layer in range(2):
            direct(layer, 1, kind, 0).wait_recv()
            relay(layer, kind, 0).start()
            direct(layer, 2, kind, 1).wait_recv()
            relay(layer, kind, 1).start()

    def ring_rest(kind):
        for layer in range(2):
            direct(layer, 1, kind, 1).wait_recv()
            direct(layer, 2, kind, 0).wait_recv()

    def ring_far(kind):
        for layer in range(2):
            relay(layer, kind, 0).wait_recv()
            relay(layer, kind, 1).wait_recv()

    @pl.when(odd_core)
    def _():
        ring(0)
        own_local(1).wait()
        own_to_peer(0).wait_recv()

        @pl.when(helped)
        def _():
            ring_rest(0)
            ring_far(0)
            for layer in range(2):
                for lane in (1, 2, 3):
                    for part in (0, 1):
                        hand_back(layer, lane, part).wait_recv()

        @pl.when(jnp.logical_not(helped))
        def _():
            ring(1)
            ring_rest(0)
            ring_rest(1)

            @pl.when(late)
            def _():
                for layer in range(2):
                    to_peer(layer, 1, down).start()
                    to_peer(layer, 2, up).start()

            @pl.when(early)
            def _():
                for layer in range(2):
                    for owner in (y, down, up):
                        turn(layer, owner)

            ring_far(0)
            ring_far(1)

            @pl.when(late)
            def _():
                for layer in range(2):
                    to_peer(layer, 3, far).start()

    @pl.when(jnp.logical_and(last, forward))
    def _():
        pltpu.make_async_copy(head_ref, hw, local_sem.at[1]).wait()

    @pl.when(jnp.logical_and(late, even_core))
    def _():
        own_local(0).wait()
        turn(0, y)
        own_to_peer(1).wait_recv()
        turn(1, y)
        for lane, owner in ((1, down), (2, up), (3, far)):
            for layer in range(2):
                to_peer(layer, lane, owner).wait_recv()
                turn(layer, owner)

    @pl.when(jnp.logical_and(last, backward))
    def _():
        pltpu.make_async_copy(head_ref, hw, local_sem.at[1]).wait()
        for i in range(CUTS):
            ht[:, cut(i)] = hw[cut(i), :].T

    def sent(ref, sem):
        pltpu.make_async_copy(ref, ref, sem).wait()

    def gather_sent():
        sent(gain_ref, gain_send.at[0])

        def parts_sent(send, kind):
            for part in (0, 1):
                sent(w.at[0, 0 : halves[kind], :], send.at[2 * kind + part])

        for lane in (1, 2):
            parts_sent(w_send.at[lane], 0)

        @pl.when(jnp.logical_not(helped))
        def _():
            for lane in (1, 2):
                parts_sent(w_send.at[lane], 1)

        @pl.when(helped)
        def _():
            for part in (0, 1):
                sent(held.at[0, 0, 0], held_send.at[0, part])

        @pl.when(odd_core)
        def _():
            for layer in (0, 1):
                parts_sent(w_send.at[3 + layer], 0)

            @pl.when(jnp.logical_not(helped))
            def _():
                for layer in (0, 1):
                    parts_sent(w_send.at[3 + layer], 1)

            @pl.when(helper)
            def _():
                for part in (0, 1):
                    for i in range(1, 7):
                        sent(held.at[0, 0, 0], held_send.at[i, part])
                    for layer in (0, 1):
                        for lane in (1, 2, 3):
                            sent(held.at[0, 0, 0], back_send.at[layer, lane, part])

            @pl.when(late)
            def _():
                sent(w.at[0, 0:share, :], w_fwd_send.at[1, 0])
                for layer in range(2):
                    for lane in (1, 2, 3):
                        sent(w.at[0, 0:share, :], w_fwd_send.at[layer, lane])

        @pl.when(even_core)
        def _():
            sent(w.at[0, 0:share, :], w_fwd_send.at[0, 0])

    def h_piece(mb, j):
        cols = window(j)
        return remote(
            h_out.at[mb, :, cols], h_in.at[mb, :, cols], h_send.at[j], h_recv.at[mb, j], (s + 2, y)
        )

    def peer_copies(mb):
        refs = [h_in, h_mid, pre.at[0], pre.at[1]]
        return [
            remote(ref.at[mb], ref.at[mb], peer_send.at[i], peer_recv.at[i, mb], peer) for i, ref in enumerate(refs)
        ]

    def head_copies(mb):
        return [
            remote(ref.at[mb], ref.at[mb], peer_send.at[4 + i], peer_recv.at[4 + i, mb], peer)
            for i, ref in enumerate([h_out, dlog, stats])
        ]

    def inverse(squares):
        return lax.rsqrt(squares * (1.0 / width) + 1e-05)

    def fold(x):
        return sum(x[:, i : i + 128] for i in range(0, x.shape[1], 128))

    def forward_one(mb, carry, is_first, is_last):
        squares = jnp.zeros((ROWS, 128), F32)
        for j in range(CUTS):
            if not is_first:
                h_piece(mb, j).wait_recv()
            h = h_in[mb, :, cut(j)].astype(F32)
            squares = squares + fold(h * h)
            product = dot((h * gains[0, :, cut(j)]).astype(BF16), w[0, cut(j), :])
            if j == 0:
                acc[...] = product
            else:
                acc[...] += product
        inv = inverse(row_sum(squares))
        squares = jnp.zeros((ROWS, 128), F32)
        opening = None
        for j in range(CUTS):
            h = h_in[mb, :, cut(j)].astype(F32)
            at = acc[:, cut(j)] * inv
            pre[0, mb, :, cut(j)] = at
            result = (h + gelu(at)).astype(BF16)
            h_mid[mb, :, cut(j)] = result
            wide = result.astype(F32)
            squares = squares + fold(wide * wide)
            scaled = (wide * gains[1, :, cut(j)]).astype(BF16)
            raw[:, cut(j)] = scaled
            part = dot(scaled, w[1, cut(j), cut(0)])
            opening = part if opening is None else opening + part
        inv_mid = inverse(row_sum(squares))
        squares = jnp.zeros((ROWS, 128), F32)
        for j in range(CUTS):
            at = opening * inv_mid
            if j + 1 < CUTS:
                opening = dot(raw[...], w[1, :, cut(j + 1)])
            result = (h_mid[mb, :, cut(j)].astype(F32) + gelu(at)).astype(BF16)
            h_out[mb, :, cut(j)] = result
            if not is_last:
                h_piece(mb, j).start()
            pre[1, mb, :, cut(j)] = at
            wide = result.astype(F32)
            squares = squares + fold(wide * wide)
        for j in range(CUTS):
            normed[0, mb, :, cut(j)] = (
                h_in[mb, :, cut(j)].astype(F32) * inv * gains[0, :, cut(j)]
            ).astype(BF16)
            normed[1, mb, :, cut(j)] = (
                h_mid[mb, :, cut(j)].astype(F32) * inv_mid * gains[1, :, cut(j)]
            ).astype(BF16)

        @pl.when(late)
        def _():
            for copy in peer_copies(mb):
                copy.start()

        if is_last:
            scale = inverse(row_sum(squares))
            z = (h_out[mb].astype(F32) * scale * out_gain_ref[...]).astype(BF16)
            logits = dot(z, hw[...])
            top = jnp.max(logits, axis=1, keepdims=True)
            exponents = jnp.exp(logits - top)
            denominator = row_sum(exponents)
            target = picked_ids[pl.ds(pl.multiple_of(mb * ROWS, ROWS), ROWS), 0:1]
            one_hot = (target == lax.broadcasted_iota(jnp.int32, logits.shape, 1)).astype(F32)
            picked = row_sum(logits * one_hot)
            d = (exponents / denominator - one_hot).astype(BF16)
            dlog[mb] = d
            pull = scale * scale * (1.0 / width) * row_sum(d.astype(F32) * logits)
            stats[mb, 0] = jnp.broadcast_to(scale, stats.shape[2:])
            stats[mb, 1] = jnp.broadcast_to(pull, stats.shape[2:])
            for copy in head_copies(mb):
                copy.start()
            losses = jnp.sum(jnp.log(denominator) + top - picked, axis=0, keepdims=True)
            loss_part[...] += jnp.broadcast_to(losses, loss_part.shape)

        return carry

    def part_copy(lane, target):
        return remote(loss_part, loss_in.at[lane], part_send.at[lane], part_recv.at[lane], (odd, target))

    def loss_back():
        return remote(loss_all, loss_all, loss_send.at[0], loss_recv.at[0], (s - 2, y))

    def loss_peer():
        return remote(loss_all, loss_all, loss_send.at[1], loss_recv.at[1], peer)

    def n_copy(layer, owner, lane):
        src = normed.at[layer, :, :, pl.ds(pl.multiple_of(owner * share, share), share)]
        return remote(src, normed_out.at[y], n_send.at[layer, lane], n_recv.at[lane], (2 * k + layer, owner))

    def n_local(layer):
        src = normed.at[layer, :, :, pl.ds(pl.multiple_of(y * share, share), share)]
        return pltpu.make_async_copy(src, normed_out.at[y], local_sem.at[0])

    def n_wait(lane, owner):
        src = normed.at[0, :, :, pl.ds(0, share)]
        return remote(src, normed_out.at[owner], n_send.at[0, lane], n_recv.at[lane], peer)

    def d_copy(layer, owner, lane, mb):
        return remote(
            dpre.at[layer, mb], dpre_out.at[y, mb], d_send.at[layer, lane], d_recv.at[lane], (2 * k + layer, owner)
        )

    def send_dpre(layer, mb):
        for lane, owner in lanes:
            d_copy(layer, owner, lane, mb).start()
        here = early if layer == 1 else late

        @pl.when(here)
        def _():
            d_local(layer, mb).start()

        @pl.when(jnp.logical_not(here))
        def _():
            d_copy(layer, y, 0, mb).start()

    def d_local(layer, mb):
        return pltpu.make_async_copy(dpre.at[layer, mb], dpre_out.at[y, mb], local_sem.at[1])

    def d_wait(lane, owner):
        return remote(dpre.at[0], dpre_out.at[owner], d_send.at[0, lane], d_recv.at[lane], peer)

    lanes = ((1, up), (2, down), (3, far))
    arrivals = ((1, down), (2, up), (3, far))

    @pl.when(forward)
    def _():
        loss_part[...] = jnp.zeros_like(loss_part)

        @pl.when(first)
        def _():
            lax.fori_loop(0, count, functools.partial(forward_one, is_first=True, is_last=False), 0)

        @pl.when(jnp.logical_and(not_first, not_last))
        def _():
            lax.fori_loop(0, count, functools.partial(forward_one, is_first=False, is_last=False), 0)

        @pl.when(last)
        def _():
            lax.fori_loop(0, count, functools.partial(forward_one, is_first=False, is_last=True), 0)

        for layer in range(2):
            for lane, owner in lanes:
                n_copy(layer, owner, lane).start()
        n_copy(0, y, 0).start()
        n_local(1).start()

        @pl.when(early)
        def _():
            for layer in range(2):
                turn(layer, far)

        @pl.when(helped)
        def _():
            for layer in range(2):
                for owner in (y, down, up):
                    turn(layer, owner)

    def g_piece(mb, j):
        cols = window(j)
        return remote(
            g_out.at[mb, :, cols], g_in.at[mb, :, cols], g_send.at[j], g_recv.at[mb, j], (back_target, y)
        )

    def prepare(mb):
        @pl.when(late)
        def _():
            for copy in peer_copies(mb):
                copy.wait_recv()

        for layer, rows in ((0, h_in), (1, h_mid)):
            squares = jnp.zeros((ROWS, 1), F32)
            for j in range(CUTS):
                h = rows[mb, :, cut(j)].astype(F32)
                squares = squares + row_sum(h * h)
                slope[layer, :, cut(j)] = gelu_slope(pre[layer, mb, :, cut(j)])
            inv_keep[layer] = jnp.broadcast_to(inverse(squares), inv_keep.shape[1:])

    def backward_one(mb, carry, is_first, is_last):
        if is_last:
            for copy in head_copies(mb):
                copy.wait_recv()
            scale, pull = stats[mb, 0, :, 0:1], stats[mb, 1, :, 0:1]
            ahead = dot(dlog[mb], ht[:, cut(0)])

        dots = jnp.zeros((ROWS, 128), F32)
        for j in range(CUTS):
            if not is_last:
                g_piece(mb, j).wait_recv()
            else:
                back = ahead * out_gain_ref[:, cut(j)]
                if j + 1 < CUTS:
                    ahead = dot(dlog[mb], ht[:, cut(j + 1)])
                g_in[mb, :, cut(j)] = (scale * back - h_out[mb, :, cut(j)].astype(F32) * pull).astype(BF16)
            d = (g_in[mb, :, cut(j)].astype(F32) * slope[1, :, cut(j)]).astype(BF16)
            dpre[1, mb, :, cut(j)] = d
            dots = dots + fold(d.astype(F32) * pre[1, mb, :, cut(j)])
            product = dot(d, wt[1, cut(j), :])
            if j == 0:
                acc[...] = product
            else:
                acc[...] += product
        if is_first:
            send_dpre(1, mb)
        inv = inv_keep[1, :, 0:1]
        pull = inv * inv * (1.0 / width) * row_sum(dots)
        dots = jnp.zeros((ROWS, 128), F32)
        opening = None
        for j in range(CUTS):
            back = acc[:, cut(j)] * gains[1, :, cut(j)]
            g = (
                g_in[mb, :, cut(j)].astype(F32) + (inv * back - h_mid[mb, :, cut(j)].astype(F32) * pull)
            ).astype(BF16).astype(F32)
            d = (g * slope[0, :, cut(j)]).astype(BF16)
            dpre[0, mb, :, cut(j)] = d
            if not is_first:
                acc[:, cut(j)] = g
                dots = dots + fold(d.astype(F32) * pre[0, mb, :, cut(j)])
                part = dot(d, wt[0, cut(j), cut(0)])
                opening = part if opening is None else opening + part
        if not is_first:
            inv = inv_keep[0, :, 0:1]
            pull = inv * inv * (1.0 / width) * row_sum(dots)
            for j in range(CUTS):
                back = opening * gains[0, :, cut(j)]
                if j + 1 < CUTS:
                    opening = dot(dpre[0, mb], wt[0, :, cut(j + 1)])
                g_out[mb, :, cut(j)] = (
                    acc[:, cut(j)] + (inv * back - h_in[mb, :, cut(j)].astype(F32) * pull)
                ).astype(BF16)
                g_piece(mb, j).start()

        send_dpre(0, mb)
        if not is_first:
            send_dpre(1, mb)

        @pl.when(mb < count - 1)
        def _():
            prepare(mb + 1)

        return carry

    @pl.when(backward)
    def _():
        prepare(0)

        @pl.when(first)
        def _():
            lax.fori_loop(0, count, functools.partial(backward_one, is_first=True, is_last=False), 0)

        @pl.when(jnp.logical_and(not_first, not_last))
        def _():
            lax.fori_loop(0, count, functools.partial(backward_one, is_first=False, is_last=False), 0)

        @pl.when(last)
        def _():
            lax.fori_loop(0, count, functools.partial(backward_one, is_first=False, is_last=True), 0)


    @pl.when(odd_core)
    def _():
        @pl.when(last)
        def _():
            for lane, owner in lanes:
                part_copy(lane, owner).start()
            for lane, owner in lanes:
                part_copy(lane, owner).wait_recv()
            loss_all[...] = loss_part[...] + loss_in[1] + loss_in[2] + loss_in[3]

        @pl.when(not_last)
        def _():
            loss_back().wait_recv()

        @pl.when(not_first)
        def _():
            loss_back().start()

        loss_peer().start()

    @pl.when(even_core)
    def _():
        loss_peer().wait_recv()

    live_count = (start * lax.axis_size("dp")).astype(F32)
    loss_ref[0, 0] = loss_all[0, 0] / live_count
    for lane, owner in arrivals:
        n_wait(lane, owner).wait_recv()
        d_wait(lane, owner).wait_recv()

    gather_sent()

    @pl.when(odd_core)
    def _():
        for layer in range(2):
            for lane in (1, 2, 3):
                sent(normed.at[0, :, :, 0:share], n_send.at[layer, lane])
        sent(normed.at[0, :, :, 0:share], n_send.at[0, 0])
        n_local(1).wait()

        @pl.when(late)
        def _():
            for i, ref in enumerate([h_in, h_mid, pre.at[0], pre.at[1]]):
                sent(ref, peer_send.at[i])
            d_wait(0, y).wait_recv()

        @pl.when(not_last)
        def _():
            for j in range(CUTS):
                sent(h_out.at[:, :, cut(j)], h_send.at[j])

        @pl.when(last)
        def _():
            sent(h_out, peer_send.at[4])
            sent(dlog, peer_send.at[5])
            sent(stats, peer_send.at[6])
            for lane in (1, 2, 3):
                sent(loss_part, part_send.at[lane])

        @pl.when(not_first)
        def _():
            sent(loss_all, loss_send.at[0])

        sent(loss_all, loss_send.at[1])

    @pl.when(even_core)
    def _():
        n_wait(0, y).wait_recv()

        @pl.when(early)
        def _():
            d_wait(0, y).wait_recv()

    @pl.when(backward)
    def _():
        for layer in range(2):
            for lane in (1, 2, 3):
                sent(dpre.at[0], d_send.at[layer, lane])
        sent(dpre.at[0], local_sem.at[1])

        @pl.when(early)
        def _():
            sent(dpre.at[0], d_send.at[0, 0])

        @pl.when(late)
        def _():
            sent(dpre.at[0], d_send.at[1, 0])

        @pl.when(not_first)
        def _():
            for j in range(CUTS):
                sent(g_out.at[:, :, cut(j)], g_send.at[j])


def product_kernel(normed_ref, dpre_ref, out_ref, turned):
    @pl.when(pl.program_id(0) == 0)
    def _():
        turned[...] = normed_ref[...].T

    out_ref[0] = dot(turned[...], dpre_ref[...])


def product(normed, dpre):
    rows, share = normed.shape
    width = dpre.shape[1]
    step = min(512, width)
    return pl.pallas_call(
        product_kernel,
        name="weight_grad",
        grid=(width // step,),
        out_shape=jax.ShapeDtypeStruct((1, share, width), F32),
        in_specs=[
            pl.BlockSpec((rows, share), lambda i: (0, 0)),
            pl.BlockSpec((rows, step), lambda i: (0, i)),
        ],
        out_specs=pl.BlockSpec((1, share, step), lambda i: (0, 0, i)),
        scratch_shapes=[pltpu.VMEM((share, rows), BF16)],
        compiler_params=pltpu.CompilerParams(vmem_limit_bytes=60 * 1024 * 1024),
        cost_estimate=pl.CostEstimate(
            flops=2 * rows * share * width, bytes_accessed=6 * share * width, transcendentals=0
        ),
    )(normed, dpre)


def shards(
    video_ids,
    action_ids,
    target_ids,
    live_lengths,
    video_table,
    action_table,
    layer_gain,
    layer_weight,
    out_gain,
    head_weight,
    live_rows,
):
    width, vocab = head_weight.shape
    share = width // 4
    count = live_rows // ROWS

    vmem = pl.BlockSpec(memory_space=pltpu.VMEM)
    smem = pl.BlockSpec(memory_space=pltpu.SMEM)
    hbm = pl.BlockSpec(memory_space=pl.ANY)
    dma = pltpu.SemaphoreType.DMA
    rows = lambda kind: pltpu.VMEM((count, ROWS, width), kind)
    pair = lambda kind: pltpu.VMEM((2, count, ROWS, width), kind)
    loss, normed, dpre = pl.pallas_call(
        kernel,
        name="stack",
        out_shape=(
            jax.ShapeDtypeStruct((1, 1), F32),
            jax.ShapeDtypeStruct((4, count, ROWS, share), BF16),
            jax.ShapeDtypeStruct((4, count, ROWS, width), BF16),
        ),
        in_specs=[smem, vmem, vmem, vmem, vmem, vmem, vmem, hbm, hbm, hbm],
        out_specs=(smem, hbm, hbm),
        scratch_shapes=[
            pltpu.VMEM((2, width, width), BF16),
            pltpu.VMEM((2, width, width), BF16),
            pltpu.VMEM((width, vocab), BF16),
            pltpu.VMEM((vocab, width), BF16),
            rows(BF16),
            rows(BF16),
            rows(BF16),
            pair(F32),
            pair(BF16),
            pair(BF16),
            rows(BF16),
            rows(BF16),
            pltpu.VMEM((count, ROWS, vocab), BF16),
            pltpu.VMEM((count, 2, ROWS, 128), F32),
            pltpu.VMEM((ROWS, width), F32),
            pltpu.VMEM((ROWS, width), BF16),
            pltpu.VMEM((2, ROWS, width), F32),
            pltpu.VMEM((2, ROWS, 128), F32),
            pltpu.VMEM((2, 1, width), F32),
            pltpu.VMEM((live_rows, 128), jnp.int32),
            pltpu.VMEM((8, 128), F32),
            pltpu.VMEM((4, 8, 128), F32),
            pltpu.VMEM((8, 128), F32),
            dma((5, 4)),
            dma((2, 4, 4)),
            dma((2, 4)),
            dma((2, 4)),
            dma((2,)),
            dma((CUTS,)),
            dma((count, CUTS)),
            dma((CUTS,)),
            dma((count, CUTS)),
            dma((7,)),
            dma((7, count)),
            dma((2, 4)),
            dma((4,)),
            dma((2, 4)),
            dma((4,)),
            dma((4,)),
            dma((4,)),
            dma((2,)),
            dma((2,)),
            dma((1,)),
            dma((1,)),
            pltpu.VMEM((2, 4, 2, share // 8, width), BF16),
            dma((7, 2)),
            dma((2, 4, 2)),
            dma((2, 4, 2)),
            dma((2, 4, 2)),
            pltpu.SemaphoreType.REGULAR,
        ],
        compiler_params=pltpu.CompilerParams(
            collective_id=0, has_side_effects=True, vmem_limit_bytes=60 * 1024 * 1024
        ),
        cost_estimate=pl.CostEstimate(flops=10**10, bytes_accessed=2 * 10**7, transcendentals=0),
    )(
        live_lengths,
        video_ids,
        action_ids,
        target_ids,
        layer_gain,
        out_gain[None],
        action_table,
        video_table,
        layer_weight,
        head_weight,
    )
    grad = product(normed.reshape(4 * live_rows, share), dpre.reshape(4 * live_rows, width))
    return (loss[0, 0], grad)


def solution(mesh, live_rows=160):
    in_specs = (
        P("dp", None),
        P("dp", None),
        P("dp", None),
        P("dp", None),
        P(),
        P(),
        P("section", None),
        P("section", "dp", None),
        P(),
        P(),
    )
    out_specs = (P(), P("section", "dp", None))
    return jax.shard_map(
        functools.partial(shards, live_rows=live_rows),
        mesh=mesh,
        in_specs=in_specs,
        out_specs=out_specs,
        check_vma=False,
    )
```

```python
import functools

import jax
import jax.numpy as jnp
from jax import lax
from jax.experimental import pallas as pl
from jax.experimental.pallas import tpu as pltpu
from jax.sharding import PartitionSpec as P

MESH = pl.DeviceIdType.MESH
F32 = jnp.float32
BF16 = jnp.bfloat16
ROWS = 16
PIECES = (2, 2, 2, 2)
CUTS = len(PIECES)
PRE_SCALE = 0.7978845608028654
CUBE = 0.044715


def gelu(x):
    return 0.5 * x * (1.0 + jnp.tanh(PRE_SCALE * (x + CUBE * x * x * x)))


def gelu_slope(x):
    t = jnp.tanh(PRE_SCALE * (x + CUBE * x * x * x))
    return 0.5 * (1.0 + t) + 0.5 * x * (1.0 - t * t) * (PRE_SCALE * (1.0 + 3.0 * CUBE * x * x))


def dot(left, right):
    return jnp.dot(left, right, preferred_element_type=F32)


def row_sum(x):
    return jnp.sum(x, axis=1, keepdims=True)


def kernel(
    lengths_ref,
    video_ids_ref,
    action_ids_ref,
    target_ids_ref,
    gain_ref,
    out_gain_ref,
    actions_ref,
    video_ref,
    weight_ref,
    head_ref,
    loss_ref,
    normed_out,
    dpre_out,
    w,
    wt,
    hw,
    ht,
    h_in,
    h_mid,
    h_out,
    pre,
    normed,
    dpre,
    g_in,
    g_out,
    dlog,
    stats,
    acc,
    raw,
    slope,
    inv_keep,
    gains,
    picked_ids,
    loss_part,
    loss_in,
    loss_all,
    w_send,
    w_recv,
    w_fwd_send,
    w_fwd_recv,
    local_sem,
    h_send,
    h_recv,
    g_send,
    g_recv,
    peer_send,
    peer_recv,
    n_send,
    n_recv,
    d_send,
    d_recv,
    part_send,
    part_recv,
    loss_send,
    loss_recv,
    gain_send,
    gain_recv,
    held,
    held_send,
    held_recv,
    back_send,
    back_recv,
    go_sem,
):
    s = lax.axis_index("section")
    y = lax.axis_index("dp")
    planes = lax.axis_size("section") // 2
    k = s // 2
    core = s % 2
    turning = planes - max(1, planes * 3 // 16)
    late = k >= turning
    early = k < turning
    odd_core = core == 1
    even_core = core == 0
    forward = odd_core
    backward = jnp.logical_or(jnp.logical_and(early, odd_core), jnp.logical_and(late, even_core))
    back_target = 2 * (k - 1) + jnp.where(k - 1 < turning, 1, 0)
    first = k == 0
    last = k == planes - 1
    not_first = k > 0
    not_last = k < planes - 1

    width = w.shape[2]
    share = width // 4
    halves = (share * 3 // 8, share // 8)
    main = 2 * halves[0]
    edges = [width * sum(PIECES[:j]) // sum(PIECES) for j in range(CUTS + 1)]
    count = h_in.shape[0]
    vocab = hw.shape[1]

    up, down, far = (y + 1) % 4, (y + 3) % 4, (y + 2) % 4
    peer = (2 * k + 1 - core, y)
    odd = 2 * k + 1
    even = 2 * k

    def remote(src, dst, send, recv, device):
        return pltpu.make_async_remote_copy(
            src_ref=src, dst_ref=dst, send_sem=send, recv_sem=recv, device_id=device, device_id_type=MESH
        )

    def cut(j):
        return slice(edges[j], edges[j + 1])

    def window(j):
        return pl.ds(edges[j], edges[j + 1] - edges[j])

    barrier = pltpu.get_barrier_semaphore()
    for other in (up, down, far):
        for c in (0, 1):
            pl.semaphore_signal(barrier, inc=1, device_id=(2 * k + c, other), device_id_type=MESH)
    pl.semaphore_signal(barrier, inc=1, device_id=peer, device_id_type=MESH)

    for plane in ((k + 1) % planes, (k + planes - 1) % planes):
        for c in (0, 1):
            pl.semaphore_signal(barrier, inc=1, device_id=(2 * plane + c, y), device_id_type=MESH)

    group = planes // 4
    helped = k < group
    helper = k >= planes - group
    friend = jnp.where(helped, k + planes - group, k - planes + group)

    @pl.when(jnp.logical_or(helped, helper))
    def _():
        for c in (0, 1):
            pl.semaphore_signal(barrier, inc=1, device_id=(2 * friend + c, y), device_id_type=MESH)

    pl.semaphore_wait(barrier, 11 + jnp.where(jnp.logical_or(helped, helper), 2, 0))

    def rows_of(owner):
        return pl.ds(pl.multiple_of(owner * share, share), share)

    def piece(kind, part):
        return kind * main + part * halves[kind], halves[kind]

    def piece_of(owner, kind, part):
        offset, size = piece(kind, part)
        return pl.ds(pl.multiple_of(owner * share + offset, 16), size)

    def direct(layer, lane, kind, part):
        offset, size = piece(kind, part)
        return remote(
            weight_ref.at[0, offset : offset + size, :],
            w.at[layer, piece_of(y, kind, part), :],
            w_send.at[lane, 2 * kind + part],
            w_recv.at[layer, lane, 2 * kind + part],
            (odd, up if lane == 1 else down),
        )

    def relay(layer, kind, part):
        owner, target = (down, up) if part == 0 else (up, down)
        block = w.at[layer, piece_of(owner, kind, part), :]
        return remote(
            block, block, w_send.at[3 + layer, 2 * kind + part], w_recv.at[layer, 3, 2 * kind + part], (odd, target)
        )

    friend_odd = 2 * friend + 1

    def to_helper(layer, part):
        offset, size = piece(1, part)
        return remote(
            weight_ref.at[0, offset : offset + size, :],
            held.at[layer, y, part],
            held_send.at[0, part],
            held_recv.at[layer, 0, part],
            (friend_odd, y),
        )

    def held_direct(layer, lane, part):
        block = held.at[layer, y, part]
        return remote(
            block,
            block,
            held_send.at[1 + 2 * layer + (lane - 1), part],
            held_recv.at[layer, lane, part],
            (odd, up if lane == 1 else down),
        )

    def held_relay(layer, part):
        owner, target = (down, up) if part == 0 else (up, down)
        block = held.at[layer, owner, part]
        return remote(block, block, held_send.at[5 + layer, part], held_recv.at[layer, 3, part], (odd, target))

    owners = {1: down, 2: up, 3: far}

    def hand_back(layer, lane, part):
        return remote(
            held.at[layer, owners[lane], part],
            w.at[layer, piece_of(owners[lane], 1, part), :],
            back_send.at[layer, lane, part],
            back_recv.at[layer, lane, part],
            (friend_odd, y),
        )

    def to_peer(layer, lane, owner):
        block = w.at[layer, rows_of(owner), :]
        return remote(block, block, w_fwd_send.at[layer, lane], w_fwd_recv.at[layer, lane], peer)

    def own_to_peer(layer):
        return remote(
            weight_ref.at[0], w.at[layer, rows_of(y), :], w_fwd_send.at[layer, 0], w_fwd_recv.at[layer, 0], peer
        )

    def own_local(layer):
        return pltpu.make_async_copy(weight_ref.at[0], w.at[layer, rows_of(y), :], local_sem.at[0])

    def start_own(layer):
        @pl.when(helped)
        def _():
            to_helper(layer, 0).start()
            to_helper(layer, 1).start()

        for kind in (0, 1):

            def one_kind(kind=kind):
                direct(layer, 1, kind, 0).start()
                direct(layer, 2, kind, 1).start()
                direct(layer, 1, kind, 1).start()
                direct(layer, 2, kind, 0).start()

            if kind == 0:
                one_kind()
            else:
                pl.when(jnp.logical_not(helped))(one_kind)

    def gain_peer(layer):
        return remote(gain_ref, gains.at[layer], gain_send.at[0], gain_recv.at[0], peer)

    def exchange_gain(layer):
        gain_peer(layer).start()
        gains[layer] = gain_ref[...]

    @pl.when(odd_core)
    def _():
        exchange_gain(1)

        @pl.when(helper)
        def _():
            for part in (0, 1):
                for layer in (0, 1):
                    to_helper(layer, part).wait_recv()
                    held_direct(layer, 1 + part, part).start()
                    held_direct(layer, 2 - part, part).start()
            pl.semaphore_signal(go_sem, inc=1, device_id=peer, device_id_type=MESH)

        @pl.when(helper)
        def _():
            for part in (0, 1):
                for layer in (0, 1):
                    held_direct(layer, 1 + part, part).wait_recv()
                    held_relay(layer, part).start()
                    hand_back(layer, 1 + part, part).start()
                    held_direct(layer, 2 - part, part).wait_recv()
                    hand_back(layer, 2 - part, part).start()
            for part in (0, 1):
                for layer in (0, 1):
                    held_relay(layer, part).wait_recv()
                    hand_back(layer, 3, part).start()

        start_own(1)
        own_local(1).start()

        @pl.when(late)
        def _():
            own_to_peer(1).start()

    @pl.when(even_core)
    def _():
        exchange_gain(0)
        own_to_peer(0).start()

        @pl.when(helper)
        def _():
            pl.semaphore_wait(go_sem, 1)

        start_own(0)

        @pl.when(late)
        def _():
            own_local(0).start()

    @pl.when(last)
    def _():
        pltpu.make_async_copy(head_ref, hw, local_sem.at[1]).start()

    @pl.when(jnp.logical_and(first, forward))
    def _():
        pltpu.make_async_copy(video_ref, ht, local_sem.at[1]).start()

    total = count * ROWS
    slots = video_ids_ref.shape[1]
    place = lax.broadcasted_iota(jnp.int32, (total, slots), 0)
    lane_of = lax.broadcasted_iota(jnp.int32, (total, slots), 1)
    chosen = [jnp.zeros((total, 1), jnp.int32) for _ in range(3)]
    start = jnp.int32(0)
    for b in range(video_ids_ref.shape[0]):
        length = lengths_ref[0, b]
        hit = jnp.logical_and(place == start + lane_of, lane_of < length)
        for kind, ids_ref in enumerate((video_ids_ref, action_ids_ref, target_ids_ref)):
            line = jnp.broadcast_to(ids_ref[b : b + 1, :], (total, slots))
            chosen[kind] = chosen[kind] + row_sum(jnp.where(hit, line, 0))
        start = start + length
    picked_ids[...] = jnp.broadcast_to(chosen[2], picked_ids.shape)

    @pl.when(jnp.logical_and(first, forward))
    def _():
        pltpu.make_async_copy(video_ref, ht, local_sem.at[1]).wait()
        video_hot = (chosen[0] == lax.broadcasted_iota(jnp.int32, (total, ht.shape[0]), 1)).astype(F32).astype(BF16)
        kinds = actions_ref.shape[0]
        for j in range(CUTS):
            cols = cut(j)
            rows = dot(video_hot, ht[:, cols])
            for a in range(kinds):
                rows = rows + jnp.where(chosen[1] == a, actions_ref[a : a + 1, cols].astype(F32), 0.0)
            h_in[:, :, cols] = rows.astype(BF16).reshape(count, ROWS, -1)

    block = min(512, width)

    def turn(layer, owner):
        def one(i, carry):
            cols = pl.ds(pl.multiple_of(i * block, block), block)
            wt[layer, cols, rows_of(owner)] = w[layer, rows_of(owner), cols].T
            return carry

        lax.fori_loop(0, width // block, one, 0)

    gain_peer(0).wait_recv()

    def ring(kind):
        for layer in range(2):
            direct(layer, 1, kind, 0).wait_recv()
            relay(layer, kind, 0).start()
            direct(layer, 2, kind, 1).wait_recv()
            relay(layer, kind, 1).start()

    def ring_rest(kind):
        for layer in range(2):
            direct(layer, 1, kind, 1).wait_recv()
            direct(layer, 2, kind, 0).wait_recv()

    def ring_far(kind):
        for layer in range(2):
            relay(layer, kind, 0).wait_recv()
            relay(layer, kind, 1).wait_recv()

    @pl.when(odd_core)
    def _():
        ring(0)
        own_local(1).wait()
        own_to_peer(0).wait_recv()

        @pl.when(helped)
        def _():
            ring_rest(0)
            ring_far(0)
            for layer in range(2):
                for lane in (1, 2, 3):
                    for part in (0, 1):
                        hand_back(layer, lane, part).wait_recv()

        @pl.when(jnp.logical_not(helped))
        def _():
            ring(1)
            ring_rest(0)
            ring_rest(1)

            @pl.when(late)
            def _():
                for layer in range(2):
                    to_peer(layer, 1, down).start()
                    to_peer(layer, 2, up).start()

            @pl.when(early)
            def _():
                for layer in range(2):
                    for owner in (y, down, up):
                        turn(layer, owner)

            ring_far(0)
            ring_far(1)

            @pl.when(late)
            def _():
                for layer in range(2):
                    to_peer(layer, 3, far).start()

    @pl.when(jnp.logical_and(last, forward))
    def _():
        pltpu.make_async_copy(head_ref, hw, local_sem.at[1]).wait()

    @pl.when(jnp.logical_and(late, even_core))
    def _():
        own_local(0).wait()
        turn(0, y)
        own_to_peer(1).wait_recv()
        turn(1, y)
        for lane, owner in ((1, down), (2, up), (3, far)):
            for layer in range(2):
                to_peer(layer, lane, owner).wait_recv()
                turn(layer, owner)

    @pl.when(jnp.logical_and(last, backward))
    def _():
        pltpu.make_async_copy(head_ref, hw, local_sem.at[1]).wait()
        for i in range(CUTS):
            ht[:, cut(i)] = hw[cut(i), :].T

    def sent(ref, sem):
        pltpu.make_async_copy(ref, ref, sem).wait()

    def gather_sent():
        sent(gain_ref, gain_send.at[0])

        def parts_sent(send, kind):
            for part in (0, 1):
                sent(w.at[0, 0 : halves[kind], :], send.at[2 * kind + part])

        for lane in (1, 2):
            parts_sent(w_send.at[lane], 0)

        @pl.when(jnp.logical_not(helped))
        def _():
            for lane in (1, 2):
                parts_sent(w_send.at[lane], 1)

        @pl.when(helped)
        def _():
            for part in (0, 1):
                sent(held.at[0, 0, 0], held_send.at[0, part])

        @pl.when(odd_core)
        def _():
            for layer in (0, 1):
                parts_sent(w_send.at[3 + layer], 0)

            @pl.when(jnp.logical_not(helped))
            def _():
                for layer in (0, 1):
                    parts_sent(w_send.at[3 + layer], 1)

            @pl.when(helper)
            def _():
                for part in (0, 1):
                    for i in range(1, 7):
                        sent(held.at[0, 0, 0], held_send.at[i, part])
                    for layer in (0, 1):
                        for lane in (1, 2, 3):
                            sent(held.at[0, 0, 0], back_send.at[layer, lane, part])

            @pl.when(late)
            def _():
                sent(w.at[0, 0:share, :], w_fwd_send.at[1, 0])
                for layer in range(2):
                    for lane in (1, 2, 3):
                        sent(w.at[0, 0:share, :], w_fwd_send.at[layer, lane])

        @pl.when(even_core)
        def _():
            sent(w.at[0, 0:share, :], w_fwd_send.at[0, 0])

    def h_piece(mb, j):
        cols = window(j)
        return remote(
            h_out.at[mb, :, cols], h_in.at[mb, :, cols], h_send.at[j], h_recv.at[mb, j], (s + 2, y)
        )

    def peer_copies(mb):
        refs = [h_in, h_mid, pre.at[0], pre.at[1]]
        return [
            remote(ref.at[mb], ref.at[mb], peer_send.at[i], peer_recv.at[i, mb], peer) for i, ref in enumerate(refs)
        ]

    def head_copies(mb):
        return [
            remote(ref.at[mb], ref.at[mb], peer_send.at[4 + i], peer_recv.at[4 + i, mb], peer)
            for i, ref in enumerate([h_out, dlog, stats])
        ]

    def inverse(squares):
        return lax.rsqrt(squares * (1.0 / width) + 1e-05)

    def fold(x):
        return sum(x[:, i : i + 128] for i in range(0, x.shape[1], 128))

    def forward_one(mb, carry, is_first, is_last):
        squares = jnp.zeros((ROWS, 128), F32)
        for j in range(CUTS):
            if not is_first:
                h_piece(mb, j).wait_recv()
            h = h_in[mb, :, cut(j)].astype(F32)
            squares = squares + fold(h * h)
            product = dot((h * gains[0, :, cut(j)]).astype(BF16), w[0, cut(j), :])
            if j == 0:
                acc[...] = product
            else:
                acc[...] += product
        inv = inverse(row_sum(squares))
        squares = jnp.zeros((ROWS, 128), F32)
        opening = None
        for j in range(CUTS):
            h = h_in[mb, :, cut(j)].astype(F32)
            at = acc[:, cut(j)] * inv
            pre[0, mb, :, cut(j)] = at
            result = (h + gelu(at)).astype(BF16)
            h_mid[mb, :, cut(j)] = result
            wide = result.astype(F32)
            squares = squares + fold(wide * wide)
            scaled = (wide * gains[1, :, cut(j)]).astype(BF16)
            raw[:, cut(j)] = scaled
            part = dot(scaled, w[1, cut(j), cut(0)])
            opening = part if opening is None else opening + part
        inv_mid = inverse(row_sum(squares))
        squares = jnp.zeros((ROWS, 128), F32)
        for j in range(CUTS):
            at = opening * inv_mid
            if j + 1 < CUTS:
                opening = dot(raw[...], w[1, :, cut(j + 1)])
            result = (h_mid[mb, :, cut(j)].astype(F32) + gelu(at)).astype(BF16)
            h_out[mb, :, cut(j)] = result
            if not is_last:
                h_piece(mb, j).start()
            pre[1, mb, :, cut(j)] = at
            wide = result.astype(F32)
            squares = squares + fold(wide * wide)
        for j in range(CUTS):
            normed[0, mb, :, cut(j)] = (
                h_in[mb, :, cut(j)].astype(F32) * inv * gains[0, :, cut(j)]
            ).astype(BF16)
            normed[1, mb, :, cut(j)] = (
                h_mid[mb, :, cut(j)].astype(F32) * inv_mid * gains[1, :, cut(j)]
            ).astype(BF16)

        @pl.when(late)
        def _():
            for copy in peer_copies(mb):
                copy.start()

        if is_last:
            scale = inverse(row_sum(squares))
            z = (h_out[mb].astype(F32) * scale * out_gain_ref[...]).astype(BF16)
            logits = dot(z, hw[...])
            top = jnp.max(logits, axis=1, keepdims=True)
            exponents = jnp.exp(logits - top)
            denominator = row_sum(exponents)
            target = picked_ids[pl.ds(pl.multiple_of(mb * ROWS, ROWS), ROWS), 0:1]
            one_hot = (target == lax.broadcasted_iota(jnp.int32, logits.shape, 1)).astype(F32)
            picked = row_sum(logits * one_hot)
            d = (exponents / denominator - one_hot).astype(BF16)
            dlog[mb] = d
            pull = scale * scale * (1.0 / width) * row_sum(d.astype(F32) * logits)
            stats[mb, 0] = jnp.broadcast_to(scale, stats.shape[2:])
            stats[mb, 1] = jnp.broadcast_to(pull, stats.shape[2:])
            for copy in head_copies(mb):
                copy.start()
            losses = jnp.sum(jnp.log(denominator) + top - picked, axis=0, keepdims=True)
            loss_part[...] += jnp.broadcast_to(losses, loss_part.shape)

        return carry

    def part_copy(lane, target):
        return remote(loss_part, loss_in.at[lane], part_send.at[lane], part_recv.at[lane], (odd, target))

    def loss_back():
        return remote(loss_all, loss_all, loss_send.at[0], loss_recv.at[0], (s - 2, y))

    def loss_peer():
        return remote(loss_all, loss_all, loss_send.at[1], loss_recv.at[1], peer)

    def n_copy(layer, owner, lane):
        src = normed.at[layer, :, :, pl.ds(pl.multiple_of(owner * share, share), share)]
        return remote(src, normed_out.at[y], n_send.at[layer, lane], n_recv.at[lane], (2 * k + layer, owner))

    def n_local(layer):
        src = normed.at[layer, :, :, pl.ds(pl.multiple_of(y * share, share), share)]
        return pltpu.make_async_copy(src, normed_out.at[y], local_sem.at[0])

    def n_wait(lane, owner):
        src = normed.at[0, :, :, pl.ds(0, share)]
        return remote(src, normed_out.at[owner], n_send.at[0, lane], n_recv.at[lane], peer)

    def d_copy(layer, owner, lane, mb):
        return remote(
            dpre.at[layer, mb], dpre_out.at[y, mb], d_send.at[layer, lane], d_recv.at[lane], (2 * k + layer, owner)
        )

    def send_dpre(layer, mb):
        for lane, owner in lanes:
            d_copy(layer, owner, lane, mb).start()
        here = early if layer == 1 else late

        @pl.when(here)
        def _():
            d_local(layer, mb).start()

        @pl.when(jnp.logical_not(here))
        def _():
            d_copy(layer, y, 0, mb).start()

    def d_local(layer, mb):
        return pltpu.make_async_copy(dpre.at[layer, mb], dpre_out.at[y, mb], local_sem.at[1])

    def d_whole(layer, owner, lane):
        return remote(
            dpre.at[layer], dpre_out.at[y], d_send.at[layer, lane], d_recv.at[lane], (2 * k + layer, owner)
        )

    def d_wait(lane, owner):
        return remote(dpre.at[0], dpre_out.at[owner], d_send.at[0, lane], d_recv.at[lane], peer)

    lanes = ((1, up), (2, down), (3, far))
    arrivals = ((1, down), (2, up), (3, far))

    @pl.when(forward)
    def _():
        loss_part[...] = jnp.zeros_like(loss_part)

        @pl.when(first)
        def _():
            lax.fori_loop(0, count, functools.partial(forward_one, is_first=True, is_last=False), 0)

        @pl.when(jnp.logical_and(not_first, not_last))
        def _():
            lax.fori_loop(0, count, functools.partial(forward_one, is_first=False, is_last=False), 0)

        @pl.when(last)
        def _():
            lax.fori_loop(0, count, functools.partial(forward_one, is_first=False, is_last=True), 0)

        for layer in range(2):
            for lane, owner in lanes:
                n_copy(layer, owner, lane).start()
        n_copy(0, y, 0).start()
        n_local(1).start()

        @pl.when(early)
        def _():
            for layer in range(2):
                turn(layer, far)

        @pl.when(helped)
        def _():
            for layer in range(2):
                for owner in (y, down, up):
                    turn(layer, owner)

    def g_piece(mb, j):
        cols = window(j)
        return remote(
            g_out.at[mb, :, cols], g_in.at[mb, :, cols], g_send.at[j], g_recv.at[mb, j], (back_target, y)
        )

    def prepare(mb):
        @pl.when(late)
        def _():
            for copy in peer_copies(mb):
                copy.wait_recv()

        for layer, rows in ((0, h_in), (1, h_mid)):
            squares = jnp.zeros((ROWS, 1), F32)
            for j in range(CUTS):
                h = rows[mb, :, cut(j)].astype(F32)
                squares = squares + row_sum(h * h)
                slope[layer, :, cut(j)] = gelu_slope(pre[layer, mb, :, cut(j)])
            inv_keep[layer] = jnp.broadcast_to(inverse(squares), inv_keep.shape[1:])

    def backward_one(mb, carry, is_first, is_last):
        if is_last:
            for copy in head_copies(mb):
                copy.wait_recv()
            scale, pull = stats[mb, 0, :, 0:1], stats[mb, 1, :, 0:1]
            ahead = dot(dlog[mb], ht[:, cut(0)])

        dots = jnp.zeros((ROWS, 128), F32)
        for j in range(CUTS):
            if not is_last:
                g_piece(mb, j).wait_recv()
            else:
                back = ahead * out_gain_ref[:, cut(j)]
                if j + 1 < CUTS:
                    ahead = dot(dlog[mb], ht[:, cut(j + 1)])
                g_in[mb, :, cut(j)] = (scale * back - h_out[mb, :, cut(j)].astype(F32) * pull).astype(BF16)
            d = (g_in[mb, :, cut(j)].astype(F32) * slope[1, :, cut(j)]).astype(BF16)
            dpre[1, mb, :, cut(j)] = d
            dots = dots + fold(d.astype(F32) * pre[1, mb, :, cut(j)])
            product = dot(d, wt[1, cut(j), :])
            if j == 0:
                acc[...] = product
            else:
                acc[...] += product
        if is_first:
            send_dpre(1, mb)
        inv = inv_keep[1, :, 0:1]
        pull = inv * inv * (1.0 / width) * row_sum(dots)
        dots = jnp.zeros((ROWS, 128), F32)
        opening = None
        for j in range(CUTS):
            back = acc[:, cut(j)] * gains[1, :, cut(j)]
            g = (
                g_in[mb, :, cut(j)].astype(F32) + (inv * back - h_mid[mb, :, cut(j)].astype(F32) * pull)
            ).astype(BF16).astype(F32)
            d = (g * slope[0, :, cut(j)]).astype(BF16)
            dpre[0, mb, :, cut(j)] = d
            if not is_first:
                acc[:, cut(j)] = g
                dots = dots + fold(d.astype(F32) * pre[0, mb, :, cut(j)])
                part = dot(d, wt[0, cut(j), cut(0)])
                opening = part if opening is None else opening + part
        if not is_first:
            inv = inv_keep[0, :, 0:1]
            pull = inv * inv * (1.0 / width) * row_sum(dots)
            for j in range(CUTS):
                back = opening * gains[0, :, cut(j)]
                if j + 1 < CUTS:
                    opening = dot(dpre[0, mb], wt[0, :, cut(j + 1)])
                g_out[mb, :, cut(j)] = (
                    acc[:, cut(j)] + (inv * back - h_in[mb, :, cut(j)].astype(F32) * pull)
                ).astype(BF16)
                g_piece(mb, j).start()

        if not is_last:
            send_dpre(0, mb)
        if not is_first and not is_last:
            send_dpre(1, mb)

        @pl.when(mb < count - 1)
        def _():
            prepare(mb + 1)

        return carry

    @pl.when(backward)
    def _():
        prepare(0)

        @pl.when(first)
        def _():
            lax.fori_loop(0, count, functools.partial(backward_one, is_first=True, is_last=False), 0)

        @pl.when(jnp.logical_and(not_first, not_last))
        def _():
            lax.fori_loop(0, count, functools.partial(backward_one, is_first=False, is_last=False), 0)

        @pl.when(last)
        def _():
            lax.fori_loop(0, count, functools.partial(backward_one, is_first=False, is_last=True), 0)
            for layer in range(2):
                for lane, owner in lanes:
                    d_whole(layer, owner, lane).start()
            d_whole(1, y, 0).start()
            pltpu.make_async_copy(dpre.at[0], dpre_out.at[y], local_sem.at[1]).start()


    @pl.when(odd_core)
    def _():
        @pl.when(last)
        def _():
            for lane, owner in lanes:
                part_copy(lane, owner).start()
            for lane, owner in lanes:
                part_copy(lane, owner).wait_recv()
            loss_all[...] = loss_part[...] + loss_in[1] + loss_in[2] + loss_in[3]

        @pl.when(not_last)
        def _():
            loss_back().wait_recv()

        @pl.when(not_first)
        def _():
            loss_back().start()

        loss_peer().start()

    @pl.when(even_core)
    def _():
        loss_peer().wait_recv()

    live_count = (start * lax.axis_size("dp")).astype(F32)
    loss_ref[0, 0] = loss_all[0, 0] / live_count
    for lane, owner in arrivals:
        n_wait(lane, owner).wait_recv()
        d_wait(lane, owner).wait_recv()

    gather_sent()

    @pl.when(odd_core)
    def _():
        for layer in range(2):
            for lane in (1, 2, 3):
                sent(normed.at[0, :, :, 0:share], n_send.at[layer, lane])
        sent(normed.at[0, :, :, 0:share], n_send.at[0, 0])
        n_local(1).wait()

        @pl.when(late)
        def _():
            for i, ref in enumerate([h_in, h_mid, pre.at[0], pre.at[1]]):
                sent(ref, peer_send.at[i])
            d_wait(0, y).wait_recv()

        @pl.when(not_last)
        def _():
            for j in range(CUTS):
                sent(h_out.at[:, :, cut(j)], h_send.at[j])

        @pl.when(last)
        def _():
            sent(h_out, peer_send.at[4])
            sent(dlog, peer_send.at[5])
            sent(stats, peer_send.at[6])
            for lane in (1, 2, 3):
                sent(loss_part, part_send.at[lane])

        @pl.when(not_first)
        def _():
            sent(loss_all, loss_send.at[0])

        sent(loss_all, loss_send.at[1])

    @pl.when(even_core)
    def _():
        n_wait(0, y).wait_recv()

        @pl.when(early)
        def _():
            d_wait(0, y).wait_recv()

    @pl.when(backward)
    def _():
        for layer in range(2):
            for lane in (1, 2, 3):
                sent(dpre.at[0], d_send.at[layer, lane])
        sent(dpre.at[0], local_sem.at[1])

        @pl.when(early)
        def _():
            sent(dpre.at[0], d_send.at[0, 0])

        @pl.when(late)
        def _():
            sent(dpre.at[0], d_send.at[1, 0])

        @pl.when(not_first)
        def _():
            for j in range(CUTS):
                sent(g_out.at[:, :, cut(j)], g_send.at[j])


def product_kernel(normed_ref, dpre_ref, out_ref, lefts, right, results, left_sem, right_sem, out_sem):
    parts, step = lefts.shape[0], lefts.shape[2]
    loads = [
        pltpu.make_async_copy(normed_ref.at[:, pl.ds(i * step, step)], lefts.at[i], left_sem.at[i])
        for i in range(parts)
    ]
    whole = pltpu.make_async_copy(dpre_ref, right, right_sem)
    loads[0].start()
    whole.start()
    for load in loads[1:]:
        load.start()
    stores = []
    for i in range(parts):
        loads[i].wait()
        turned = lefts[i].T
        if i == 0:
            whole.wait()
        results[i] = dot(turned, right[...])
        stores.append(
            pltpu.make_async_copy(results.at[i], out_ref.at[0, pl.ds(i * step, step), :], out_sem.at[i])
        )
        stores[-1].start()
    for store in stores:
        store.wait()


def product(normed, dpre):
    rows, share = normed.shape
    width = dpre.shape[1]
    step = min(256, share)
    parts = share // step
    hbm = pl.BlockSpec(memory_space=pl.ANY)
    return pl.pallas_call(
        product_kernel,
        name="weight_grad",
        out_shape=jax.ShapeDtypeStruct((1, share, width), F32),
        in_specs=[hbm, hbm],
        out_specs=hbm,
        scratch_shapes=[
            pltpu.VMEM((parts, rows, step), BF16),
            pltpu.VMEM((rows, width), BF16),
            pltpu.VMEM((parts, step, width), F32),
            pltpu.SemaphoreType.DMA((parts,)),
            pltpu.SemaphoreType.DMA,
            pltpu.SemaphoreType.DMA((parts,)),
        ],
        compiler_params=pltpu.CompilerParams(vmem_limit_bytes=60 * 1024 * 1024),
        cost_estimate=pl.CostEstimate(
            flops=2 * rows * share * width, bytes_accessed=6 * share * width, transcendentals=0
        ),
    )(normed, dpre)


def shards(
    video_ids,
    action_ids,
    target_ids,
    live_lengths,
    video_table,
    action_table,
    layer_gain,
    layer_weight,
    out_gain,
    head_weight,
    live_rows,
):
    width, vocab = head_weight.shape
    share = width // 4
    count = live_rows // ROWS

    vmem = pl.BlockSpec(memory_space=pltpu.VMEM)
    smem = pl.BlockSpec(memory_space=pltpu.SMEM)
    hbm = pl.BlockSpec(memory_space=pl.ANY)
    dma = pltpu.SemaphoreType.DMA
    rows = lambda kind: pltpu.VMEM((count, ROWS, width), kind)
    pair = lambda kind: pltpu.VMEM((2, count, ROWS, width), kind)
    loss, normed, dpre = pl.pallas_call(
        kernel,
        name="stack",
        out_shape=(
            jax.ShapeDtypeStruct((1, 1), F32),
            jax.ShapeDtypeStruct((4, count, ROWS, share), BF16),
            jax.ShapeDtypeStruct((4, count, ROWS, width), BF16),
        ),
        in_specs=[smem, vmem, vmem, vmem, vmem, vmem, vmem, hbm, hbm, hbm],
        out_specs=(smem, hbm, hbm),
        scratch_shapes=[
            pltpu.VMEM((2, width, width), BF16),
            pltpu.VMEM((2, width, width), BF16),
            pltpu.VMEM((width, vocab), BF16),
            pltpu.VMEM((vocab, width), BF16),
            rows(BF16),
            rows(BF16),
            rows(BF16),
            pair(F32),
            pair(BF16),
            pair(BF16),
            rows(BF16),
            rows(BF16),
            pltpu.VMEM((count, ROWS, vocab), BF16),
            pltpu.VMEM((count, 2, ROWS, 128), F32),
            pltpu.VMEM((ROWS, width), F32),
            pltpu.VMEM((ROWS, width), BF16),
            pltpu.VMEM((2, ROWS, width), F32),
            pltpu.VMEM((2, ROWS, 128), F32),
            pltpu.VMEM((2, 1, width), F32),
            pltpu.VMEM((live_rows, 128), jnp.int32),
            pltpu.VMEM((8, 128), F32),
            pltpu.VMEM((4, 8, 128), F32),
            pltpu.VMEM((8, 128), F32),
            dma((5, 4)),
            dma((2, 4, 4)),
            dma((2, 4)),
            dma((2, 4)),
            dma((2,)),
            dma((CUTS,)),
            dma((count, CUTS)),
            dma((CUTS,)),
            dma((count, CUTS)),
            dma((7,)),
            dma((7, count)),
            dma((2, 4)),
            dma((4,)),
            dma((2, 4)),
            dma((4,)),
            dma((4,)),
            dma((4,)),
            dma((2,)),
            dma((2,)),
            dma((1,)),
            dma((1,)),
            pltpu.VMEM((2, 4, 2, share // 8, width), BF16),
            dma((7, 2)),
            dma((2, 4, 2)),
            dma((2, 4, 2)),
            dma((2, 4, 2)),
            pltpu.SemaphoreType.REGULAR,
        ],
        compiler_params=pltpu.CompilerParams(
            collective_id=0, has_side_effects=True, vmem_limit_bytes=60 * 1024 * 1024
        ),
        cost_estimate=pl.CostEstimate(flops=10**10, bytes_accessed=2 * 10**7, transcendentals=0),
    )(
        live_lengths,
        video_ids,
        action_ids,
        target_ids,
        layer_gain,
        out_gain[None],
        action_table,
        video_table,
        layer_weight,
        head_weight,
    )
    grad = product(normed.reshape(4 * live_rows, share), dpre.reshape(4 * live_rows, width))
    return (loss[0, 0], grad)


def solution(mesh, live_rows=160):
    in_specs = (
        P("dp", None),
        P("dp", None),
        P("dp", None),
        P("dp", None),
        P(),
        P(),
        P("section", None),
        P("section", "dp", None),
        P(),
        P(),
    )
    out_specs = (P(), P("section", "dp", None))
    return jax.shard_map(
        functools.partial(shards, live_rows=live_rows),
        mesh=mesh,
        in_specs=in_specs,
        out_specs=out_specs,
        check_vma=False,
    )
```

```python
import functools

import jax
import jax.numpy as jnp
from jax import lax
from jax.experimental import pallas as pl
from jax.experimental.pallas import tpu as pltpu
from jax.sharding import PartitionSpec as P

MESH = pl.DeviceIdType.MESH
F32 = jnp.float32
BF16 = jnp.bfloat16
ROWS = 16
PIECES = (2, 2, 2, 2)
CUTS = len(PIECES)
PRE_SCALE = 0.7978845608028654
CUBE = 0.044715


def gelu(x):
    return 0.5 * x * (1.0 + jnp.tanh(PRE_SCALE * (x + CUBE * x * x * x)))


def gelu_slope(x):
    t = jnp.tanh(PRE_SCALE * (x + CUBE * x * x * x))
    return 0.5 * (1.0 + t) + 0.5 * x * (1.0 - t * t) * (PRE_SCALE * (1.0 + 3.0 * CUBE * x * x))


def dot(left, right):
    return jnp.dot(left, right, preferred_element_type=F32)


def row_sum(x):
    return jnp.sum(x, axis=1, keepdims=True)


def kernel(
    lengths_ref,
    video_ids_ref,
    action_ids_ref,
    target_ids_ref,
    gain_ref,
    out_gain_ref,
    actions_ref,
    video_ref,
    weight_ref,
    head_ref,
    loss_ref,
    normed_out,
    dpre_out,
    w,
    wt,
    hw,
    ht,
    h_in,
    h_mid,
    h_out,
    pre,
    normed,
    dpre,
    g_in,
    g_out,
    dlog,
    stats,
    acc,
    raw,
    slope,
    inv_keep,
    gains,
    picked_ids,
    loss_part,
    loss_in,
    loss_all,
    w_send,
    w_recv,
    w_fwd_send,
    w_fwd_recv,
    local_sem,
    h_send,
    h_recv,
    g_send,
    g_recv,
    peer_send,
    peer_recv,
    n_send,
    n_recv,
    d_send,
    d_recv,
    part_send,
    part_recv,
    loss_send,
    loss_recv,
    gain_send,
    gain_recv,
    held,
    held_send,
    held_recv,
    back_send,
    back_recv,
    go_sem,
):
    s = lax.axis_index("section")
    y = lax.axis_index("dp")
    planes = lax.axis_size("section") // 2
    k = s // 2
    core = s % 2
    turning = planes - max(1, planes * 3 // 16)
    late = k >= turning
    early = k < turning
    odd_core = core == 1
    even_core = core == 0
    forward = odd_core
    backward = jnp.logical_or(jnp.logical_and(early, odd_core), jnp.logical_and(late, even_core))
    back_target = 2 * (k - 1) + jnp.where(k - 1 < turning, 1, 0)
    first = k == 0
    last = k == planes - 1
    not_first = k > 0
    not_last = k < planes - 1

    width = w.shape[2]
    share = width // 4
    halves = (share * 3 // 8, share // 8)
    main = 2 * halves[0]
    edges = [width * sum(PIECES[:j]) // sum(PIECES) for j in range(CUTS + 1)]
    count = h_in.shape[0]
    vocab = hw.shape[1]

    up, down, far = (y + 1) % 4, (y + 3) % 4, (y + 2) % 4
    peer = (2 * k + 1 - core, y)
    odd = 2 * k + 1
    even = 2 * k

    def remote(src, dst, send, recv, device):
        return pltpu.make_async_remote_copy(
            src_ref=src, dst_ref=dst, send_sem=send, recv_sem=recv, device_id=device, device_id_type=MESH
        )

    def cut(j):
        return slice(edges[j], edges[j + 1])

    def window(j):
        return pl.ds(edges[j], edges[j + 1] - edges[j])

    barrier = pltpu.get_barrier_semaphore()
    for other in (up, down, far):
        for c in (0, 1):
            pl.semaphore_signal(barrier, inc=1, device_id=(2 * k + c, other), device_id_type=MESH)
    pl.semaphore_signal(barrier, inc=1, device_id=peer, device_id_type=MESH)

    for plane in ((k + 1) % planes, (k + planes - 1) % planes):
        for c in (0, 1):
            pl.semaphore_signal(barrier, inc=1, device_id=(2 * plane + c, y), device_id_type=MESH)

    group = planes // 4
    helped = k < group
    helper = k >= planes - group
    friend = jnp.where(helped, k + planes - group, k - planes + group)

    @pl.when(jnp.logical_or(helped, helper))
    def _():
        for c in (0, 1):
            pl.semaphore_signal(barrier, inc=1, device_id=(2 * friend + c, y), device_id_type=MESH)

    pl.semaphore_wait(barrier, 11 + jnp.where(jnp.logical_or(helped, helper), 2, 0))

    def rows_of(owner):
        return pl.ds(pl.multiple_of(owner * share, share), share)

    def piece(kind, part):
        return kind * main + part * halves[kind], halves[kind]

    def piece_of(owner, kind, part):
        offset, size = piece(kind, part)
        return pl.ds(pl.multiple_of(owner * share + offset, 16), size)

    def direct(layer, lane, kind, part):
        offset, size = piece(kind, part)
        return remote(
            weight_ref.at[0, offset : offset + size, :],
            w.at[layer, piece_of(y, kind, part), :],
            w_send.at[lane, 2 * kind + part],
            w_recv.at[layer, lane, 2 * kind + part],
            (odd, up if lane == 1 else down),
        )

    def relay(layer, kind, part):
        owner, target = (down, up) if part == 0 else (up, down)
        block = w.at[layer, piece_of(owner, kind, part), :]
        return remote(
            block, block, w_send.at[3 + layer, 2 * kind + part], w_recv.at[layer, 3, 2 * kind + part], (odd, target)
        )

    friend_odd = 2 * friend + 1

    def to_helper(layer, part):
        offset, size = piece(1, part)
        return remote(
            weight_ref.at[0, offset : offset + size, :],
            held.at[layer, y, part],
            held_send.at[0, part],
            held_recv.at[layer, 0, part],
            (friend_odd, y),
        )

    def held_direct(layer, lane, part):
        block = held.at[layer, y, part]
        return remote(
            block,
            block,
            held_send.at[1 + 2 * layer + (lane - 1), part],
            held_recv.at[layer, lane, part],
            (odd, up if lane == 1 else down),
        )

    def held_relay(layer, part):
        owner, target = (down, up) if part == 0 else (up, down)
        block = held.at[layer, owner, part]
        return remote(block, block, held_send.at[5 + layer, part], held_recv.at[layer, 3, part], (odd, target))

    owners = {1: down, 2: up, 3: far}

    def hand_back(layer, lane, part):
        return remote(
            held.at[layer, owners[lane], part],
            w.at[layer, piece_of(owners[lane], 1, part), :],
            back_send.at[layer, lane, part],
            back_recv.at[layer, lane, part],
            (friend_odd, y),
        )

    def to_peer(layer, lane, owner):
        block = w.at[layer, rows_of(owner), :]
        return remote(block, block, w_fwd_send.at[layer, lane], w_fwd_recv.at[layer, lane], peer)

    def own_to_peer(layer):
        return remote(
            weight_ref.at[0], w.at[layer, rows_of(y), :], w_fwd_send.at[layer, 0], w_fwd_recv.at[layer, 0], peer
        )

    def own_local(layer):
        return pltpu.make_async_copy(weight_ref.at[0], w.at[layer, rows_of(y), :], local_sem.at[0])

    def start_own(layer):
        @pl.when(helped)
        def _():
            to_helper(layer, 0).start()
            to_helper(layer, 1).start()

        for kind in (0, 1):

            def one_kind(kind=kind):
                direct(layer, 1, kind, 0).start()
                direct(layer, 2, kind, 1).start()
                direct(layer, 1, kind, 1).start()
                direct(layer, 2, kind, 0).start()

            if kind == 0:
                one_kind()
            else:
                pl.when(jnp.logical_not(helped))(one_kind)

    def gain_peer(layer):
        return remote(gain_ref, gains.at[layer], gain_send.at[0], gain_recv.at[0], peer)

    def exchange_gain(layer):
        gain_peer(layer).start()
        gains[layer] = gain_ref[...]

    @pl.when(odd_core)
    def _():
        exchange_gain(1)

        @pl.when(helper)
        def _():
            for part in (0, 1):
                for layer in (0, 1):
                    to_helper(layer, part).wait_recv()
                    held_direct(layer, 1 + part, part).start()
                    held_direct(layer, 2 - part, part).start()
            pl.semaphore_signal(go_sem, inc=1, device_id=peer, device_id_type=MESH)

        @pl.when(helper)
        def _():
            for part in (0, 1):
                for layer in (0, 1):
                    held_direct(layer, 1 + part, part).wait_recv()
                    held_relay(layer, part).start()
                    hand_back(layer, 1 + part, part).start()
                    held_direct(layer, 2 - part, part).wait_recv()
                    hand_back(layer, 2 - part, part).start()
            for part in (0, 1):
                for layer in (0, 1):
                    held_relay(layer, part).wait_recv()
                    hand_back(layer, 3, part).start()

        start_own(1)
        own_local(1).start()

        @pl.when(late)
        def _():
            own_to_peer(1).start()

    @pl.when(even_core)
    def _():
        exchange_gain(0)
        own_to_peer(0).start()

        @pl.when(helper)
        def _():
            pl.semaphore_wait(go_sem, 1)

        start_own(0)

        @pl.when(late)
        def _():
            own_local(0).start()

    @pl.when(last)
    def _():
        pltpu.make_async_copy(head_ref, hw, local_sem.at[1]).start()

    @pl.when(jnp.logical_and(first, forward))
    def _():
        pltpu.make_async_copy(video_ref, ht, local_sem.at[1]).start()

    total = count * ROWS
    slots = video_ids_ref.shape[1]
    place = lax.broadcasted_iota(jnp.int32, (total, slots), 0)
    lane_of = lax.broadcasted_iota(jnp.int32, (total, slots), 1)
    chosen = [jnp.zeros((total, 1), jnp.int32) for _ in range(3)]
    start = jnp.int32(0)
    for b in range(video_ids_ref.shape[0]):
        length = lengths_ref[0, b]
        hit = jnp.logical_and(place == start + lane_of, lane_of < length)
        for kind, ids_ref in enumerate((video_ids_ref, action_ids_ref, target_ids_ref)):
            line = jnp.broadcast_to(ids_ref[b : b + 1, :], (total, slots))
            chosen[kind] = chosen[kind] + row_sum(jnp.where(hit, line, 0))
        start = start + length
    picked_ids[...] = jnp.broadcast_to(chosen[2], picked_ids.shape)

    @pl.when(jnp.logical_and(first, forward))
    def _():
        pltpu.make_async_copy(video_ref, ht, local_sem.at[1]).wait()
        video_hot = (chosen[0] == lax.broadcasted_iota(jnp.int32, (total, ht.shape[0]), 1)).astype(F32).astype(BF16)
        kinds = actions_ref.shape[0]
        for j in range(CUTS):
            cols = cut(j)
            rows = dot(video_hot, ht[:, cols])
            for a in range(kinds):
                rows = rows + jnp.where(chosen[1] == a, actions_ref[a : a + 1, cols].astype(F32), 0.0)
            h_in[:, :, cols] = rows.astype(BF16).reshape(count, ROWS, -1)

    block = min(512, width)

    def turn(layer, owner):
        def one(i, carry):
            cols = pl.ds(pl.multiple_of(i * block, block), block)
            wt[layer, cols, rows_of(owner)] = w[layer, rows_of(owner), cols].T
            return carry

        lax.fori_loop(0, width // block, one, 0)

    gain_peer(0).wait_recv()

    def ring(kind):
        for layer in range(2):
            direct(layer, 1, kind, 0).wait_recv()
            relay(layer, kind, 0).start()
            direct(layer, 2, kind, 1).wait_recv()
            relay(layer, kind, 1).start()

    def ring_rest(kind):
        for layer in range(2):
            direct(layer, 1, kind, 1).wait_recv()
            direct(layer, 2, kind, 0).wait_recv()

    def ring_far(kind):
        for layer in range(2):
            relay(layer, kind, 0).wait_recv()
            relay(layer, kind, 1).wait_recv()

    @pl.when(odd_core)
    def _():
        ring(0)
        own_local(1).wait()
        own_to_peer(0).wait_recv()

        @pl.when(helped)
        def _():
            ring_rest(0)
            ring_far(0)
            for layer in range(2):
                for lane in (1, 2, 3):
                    for part in (0, 1):
                        hand_back(layer, lane, part).wait_recv()

        @pl.when(jnp.logical_not(helped))
        def _():
            ring(1)
            ring_rest(0)
            ring_rest(1)

            @pl.when(late)
            def _():
                for layer in range(2):
                    to_peer(layer, 1, down).start()
                    to_peer(layer, 2, up).start()

            @pl.when(early)
            def _():
                for layer in range(2):
                    for owner in (y, down, up):
                        turn(layer, owner)

            ring_far(0)
            ring_far(1)

            @pl.when(late)
            def _():
                for layer in range(2):
                    to_peer(layer, 3, far).start()

    @pl.when(jnp.logical_and(last, forward))
    def _():
        pltpu.make_async_copy(head_ref, hw, local_sem.at[1]).wait()

    @pl.when(jnp.logical_and(late, even_core))
    def _():
        own_local(0).wait()
        turn(0, y)
        own_to_peer(1).wait_recv()
        turn(1, y)
        for lane, owner in ((1, down), (2, up), (3, far)):
            for layer in range(2):
                to_peer(layer, lane, owner).wait_recv()
                turn(layer, owner)

    @pl.when(jnp.logical_and(last, backward))
    def _():
        pltpu.make_async_copy(head_ref, hw, local_sem.at[1]).wait()
        for i in range(CUTS):
            ht[:, cut(i)] = hw[cut(i), :].T

    def sent(ref, sem):
        pltpu.make_async_copy(ref, ref, sem).wait()

    def gather_sent():
        sent(gain_ref, gain_send.at[0])

        def parts_sent(send, kind):
            for part in (0, 1):
                sent(w.at[0, 0 : halves[kind], :], send.at[2 * kind + part])

        for lane in (1, 2):
            parts_sent(w_send.at[lane], 0)

        @pl.when(jnp.logical_not(helped))
        def _():
            for lane in (1, 2):
                parts_sent(w_send.at[lane], 1)

        @pl.when(helped)
        def _():
            for part in (0, 1):
                sent(held.at[0, 0, 0], held_send.at[0, part])

        @pl.when(odd_core)
        def _():
            for layer in (0, 1):
                parts_sent(w_send.at[3 + layer], 0)

            @pl.when(jnp.logical_not(helped))
            def _():
                for layer in (0, 1):
                    parts_sent(w_send.at[3 + layer], 1)

            @pl.when(helper)
            def _():
                for part in (0, 1):
                    for i in range(1, 7):
                        sent(held.at[0, 0, 0], held_send.at[i, part])
                    for layer in (0, 1):
                        for lane in (1, 2, 3):
                            sent(held.at[0, 0, 0], back_send.at[layer, lane, part])

            @pl.when(late)
            def _():
                sent(w.at[0, 0:share, :], w_fwd_send.at[1, 0])
                for layer in range(2):
                    for lane in (1, 2, 3):
                        sent(w.at[0, 0:share, :], w_fwd_send.at[layer, lane])

        @pl.when(even_core)
        def _():
            sent(w.at[0, 0:share, :], w_fwd_send.at[0, 0])

    def h_piece(mb, j):
        cols = window(j)
        return remote(
            h_out.at[mb, :, cols], h_in.at[mb, :, cols], h_send.at[j], h_recv.at[mb, j], (s + 2, y)
        )

    def peer_copies(mb):
        refs = [h_in, h_mid, pre.at[0], pre.at[1]]
        return [
            remote(ref.at[mb], ref.at[mb], peer_send.at[i], peer_recv.at[i, mb], peer) for i, ref in enumerate(refs)
        ]

    def head_copies(mb):
        return [
            remote(ref.at[mb], ref.at[mb], peer_send.at[4 + i], peer_recv.at[4 + i, mb], peer)
            for i, ref in enumerate([h_out, dlog, stats])
        ]

    def inverse(squares):
        return lax.rsqrt(squares * (1.0 / width) + 1e-05)

    def fold(x):
        return sum(x[:, i : i + 128] for i in range(0, x.shape[1], 128))

    def forward_one(mb, carry, is_first, is_last):
        squares = jnp.zeros((ROWS, 128), F32)
        for j in range(1 if is_first else CUTS):
            if not is_first:
                h_piece(mb, j).wait_recv()
            taken = slice(0, width) if is_first else cut(j)
            h = h_in[mb, :, taken].astype(F32)
            squares = squares + fold(h * h)
            product = dot((h * gains[0, :, taken]).astype(BF16), w[0, taken, :])
            if j == 0:
                acc[...] = product
            else:
                acc[...] += product
        inv = inverse(row_sum(squares))
        squares = jnp.zeros((ROWS, 128), F32)
        opening = None
        for j in range(CUTS):
            h = h_in[mb, :, cut(j)].astype(F32)
            at = acc[:, cut(j)] * inv
            pre[0, mb, :, cut(j)] = at
            result = (h + gelu(at)).astype(BF16)
            h_mid[mb, :, cut(j)] = result
            wide = result.astype(F32)
            squares = squares + fold(wide * wide)
            scaled = (wide * gains[1, :, cut(j)]).astype(BF16)
            raw[:, cut(j)] = scaled
            part = dot(scaled, w[1, cut(j), cut(0)])
            opening = part if opening is None else opening + part
        inv_mid = inverse(row_sum(squares))
        squares = jnp.zeros((ROWS, 128), F32)
        for j in range(CUTS):
            at = opening * inv_mid
            if j + 1 < CUTS:
                opening = dot(raw[...], w[1, :, cut(j + 1)])
            result = (h_mid[mb, :, cut(j)].astype(F32) + gelu(at)).astype(BF16)
            h_out[mb, :, cut(j)] = result
            if not is_last:
                h_piece(mb, j).start()
            pre[1, mb, :, cut(j)] = at
            wide = result.astype(F32)
            squares = squares + fold(wide * wide)
        def keep_normed():
            for j in range(CUTS):
                normed[0, mb, :, cut(j)] = (
                    h_in[mb, :, cut(j)].astype(F32) * inv * gains[0, :, cut(j)]
                ).astype(BF16)
                normed[1, mb, :, cut(j)] = (
                    h_mid[mb, :, cut(j)].astype(F32) * inv_mid * gains[1, :, cut(j)]
                ).astype(BF16)

        if not is_last:
            keep_normed()

        @pl.when(late)
        def _():
            for copy in peer_copies(mb):
                copy.start()

        if is_last:
            scale = inverse(row_sum(squares))
            z = (h_out[mb].astype(F32) * scale * out_gain_ref[...]).astype(BF16)
            logits = dot(z, hw[...])
            top = jnp.max(logits, axis=1, keepdims=True)
            exponents = jnp.exp(logits - top)
            denominator = row_sum(exponents)
            target = picked_ids[pl.ds(pl.multiple_of(mb * ROWS, ROWS), ROWS), 0:1]
            one_hot = (target == lax.broadcasted_iota(jnp.int32, logits.shape, 1)).astype(F32)
            picked = row_sum(logits * one_hot)
            d = (exponents / denominator - one_hot).astype(BF16)
            dlog[mb] = d
            pull = scale * scale * (1.0 / width) * row_sum(d.astype(F32) * logits)
            stats[mb, 0] = jnp.broadcast_to(scale, stats.shape[2:])
            stats[mb, 1] = jnp.broadcast_to(pull, stats.shape[2:])
            for copy in head_copies(mb):
                copy.start()
            losses = jnp.sum(jnp.log(denominator) + top - picked, axis=0, keepdims=True)
            loss_part[...] += jnp.broadcast_to(losses, loss_part.shape)
            keep_normed()

        return carry

    def part_copy(lane, target):
        return remote(loss_part, loss_in.at[lane], part_send.at[lane], part_recv.at[lane], (odd, target))

    def loss_back():
        return remote(loss_all, loss_all, loss_send.at[0], loss_recv.at[0], (s - 2, y))

    def loss_peer():
        return remote(loss_all, loss_all, loss_send.at[1], loss_recv.at[1], peer)

    def n_copy(layer, owner, lane):
        src = normed.at[layer, :, :, pl.ds(pl.multiple_of(owner * share, share), share)]
        return remote(src, normed_out.at[y], n_send.at[layer, lane], n_recv.at[lane], (2 * k + layer, owner))

    def n_local(layer):
        src = normed.at[layer, :, :, pl.ds(pl.multiple_of(y * share, share), share)]
        return pltpu.make_async_copy(src, normed_out.at[y], local_sem.at[0])

    def n_wait(lane, owner):
        src = normed.at[0, :, :, pl.ds(0, share)]
        return remote(src, normed_out.at[owner], n_send.at[0, lane], n_recv.at[lane], peer)

    def d_copy(layer, owner, lane, mb):
        return remote(
            dpre.at[layer, mb], dpre_out.at[y, mb], d_send.at[layer, lane], d_recv.at[lane], (2 * k + layer, owner)
        )

    def send_dpre(layer, mb):
        for lane, owner in lanes:
            d_copy(layer, owner, lane, mb).start()
        here = early if layer == 1 else late

        @pl.when(here)
        def _():
            d_local(layer, mb).start()

        @pl.when(jnp.logical_not(here))
        def _():
            d_copy(layer, y, 0, mb).start()

    def d_local(layer, mb):
        return pltpu.make_async_copy(dpre.at[layer, mb], dpre_out.at[y, mb], local_sem.at[1])

    def d_whole(layer, owner, lane):
        return remote(
            dpre.at[layer], dpre_out.at[y], d_send.at[layer, lane], d_recv.at[lane], (2 * k + layer, owner)
        )

    def d_wait(lane, owner):
        return remote(dpre.at[0], dpre_out.at[owner], d_send.at[0, lane], d_recv.at[lane], peer)

    lanes = ((1, up), (2, down), (3, far))
    arrivals = ((1, down), (2, up), (3, far))

    @pl.when(forward)
    def _():
        loss_part[...] = jnp.zeros_like(loss_part)

        @pl.when(first)
        def _():
            lax.fori_loop(0, count, functools.partial(forward_one, is_first=True, is_last=False), 0)

        @pl.when(jnp.logical_and(not_first, not_last))
        def _():
            lax.fori_loop(0, count, functools.partial(forward_one, is_first=False, is_last=False), 0)

        @pl.when(last)
        def _():
            lax.fori_loop(0, count, functools.partial(forward_one, is_first=False, is_last=True), 0)

        for layer in range(2):
            for lane, owner in lanes:
                n_copy(layer, owner, lane).start()
        n_copy(0, y, 0).start()
        n_local(1).start()

        @pl.when(early)
        def _():
            for layer in range(2):
                turn(layer, far)

        @pl.when(helped)
        def _():
            for layer in range(2):
                for owner in (y, down, up):
                    turn(layer, owner)

    def g_piece(mb, j):
        cols = window(j)
        return remote(
            g_out.at[mb, :, cols], g_in.at[mb, :, cols], g_send.at[j], g_recv.at[mb, j], (back_target, y)
        )

    def prepare(mb):
        @pl.when(late)
        def _():
            for copy in peer_copies(mb):
                copy.wait_recv()

        for layer, rows in ((0, h_in), (1, h_mid)):
            squares = jnp.zeros((ROWS, 1), F32)
            for j in range(CUTS):
                h = rows[mb, :, cut(j)].astype(F32)
                squares = squares + row_sum(h * h)
                slope[layer, :, cut(j)] = gelu_slope(pre[layer, mb, :, cut(j)])
            inv_keep[layer] = jnp.broadcast_to(inverse(squares), inv_keep.shape[1:])

    def backward_one(mb, carry, is_first, is_last):
        if is_last:
            for copy in head_copies(mb):
                copy.wait_recv()
            scale, pull = stats[mb, 0, :, 0:1], stats[mb, 1, :, 0:1]
            ahead = dot(dlog[mb], ht[:, cut(0)])

        dots = jnp.zeros((ROWS, 128), F32)
        for j in range(CUTS):
            if not is_last:
                g_piece(mb, j).wait_recv()
            else:
                back = ahead * out_gain_ref[:, cut(j)]
                if j + 1 < CUTS:
                    ahead = dot(dlog[mb], ht[:, cut(j + 1)])
                g_in[mb, :, cut(j)] = (scale * back - h_out[mb, :, cut(j)].astype(F32) * pull).astype(BF16)
            d = (g_in[mb, :, cut(j)].astype(F32) * slope[1, :, cut(j)]).astype(BF16)
            dpre[1, mb, :, cut(j)] = d
            dots = dots + fold(d.astype(F32) * pre[1, mb, :, cut(j)])
            product = dot(d, wt[1, cut(j), :])
            if j == 0:
                acc[...] = product
            else:
                acc[...] += product
        if is_first:
            send_dpre(1, mb)
        inv = inv_keep[1, :, 0:1]
        pull = inv * inv * (1.0 / width) * row_sum(dots)
        dots = jnp.zeros((ROWS, 128), F32)
        opening = None
        for j in range(CUTS):
            back = acc[:, cut(j)] * gains[1, :, cut(j)]
            g = (
                g_in[mb, :, cut(j)].astype(F32) + (inv * back - h_mid[mb, :, cut(j)].astype(F32) * pull)
            ).astype(BF16).astype(F32)
            d = (g * slope[0, :, cut(j)]).astype(BF16)
            dpre[0, mb, :, cut(j)] = d
            if not is_first:
                acc[:, cut(j)] = g
                dots = dots + fold(d.astype(F32) * pre[0, mb, :, cut(j)])
                part = dot(d, wt[0, cut(j), cut(0)])
                opening = part if opening is None else opening + part
        if not is_first:
            inv = inv_keep[0, :, 0:1]
            pull = inv * inv * (1.0 / width) * row_sum(dots)
            for j in range(CUTS):
                back = opening * gains[0, :, cut(j)]
                if j + 1 < CUTS:
                    opening = dot(dpre[0, mb], wt[0, :, cut(j + 1)])
                g_out[mb, :, cut(j)] = (
                    acc[:, cut(j)] + (inv * back - h_in[mb, :, cut(j)].astype(F32) * pull)
                ).astype(BF16)
                g_piece(mb, j).start()

        if not is_last:
            send_dpre(0, mb)
        if not is_first and not is_last:
            send_dpre(1, mb)

        @pl.when(mb < count - 1)
        def _():
            prepare(mb + 1)

        return carry

    @pl.when(backward)
    def _():
        prepare(0)

        @pl.when(first)
        def _():
            lax.fori_loop(0, count, functools.partial(backward_one, is_first=True, is_last=False), 0)

        @pl.when(jnp.logical_and(not_first, not_last))
        def _():
            lax.fori_loop(0, count, functools.partial(backward_one, is_first=False, is_last=False), 0)

        @pl.when(last)
        def _():
            lax.fori_loop(0, count, functools.partial(backward_one, is_first=False, is_last=True), 0)
            for layer in range(2):
                for lane, owner in lanes:
                    d_whole(layer, owner, lane).start()
            d_whole(1, y, 0).start()
            pltpu.make_async_copy(dpre.at[0], dpre_out.at[y], local_sem.at[1]).start()


    @pl.when(odd_core)
    def _():
        @pl.when(last)
        def _():
            for lane, owner in lanes:
                part_copy(lane, owner).start()
            for lane, owner in lanes:
                part_copy(lane, owner).wait_recv()
            loss_all[...] = loss_part[...] + loss_in[1] + loss_in[2] + loss_in[3]

        @pl.when(not_last)
        def _():
            loss_back().wait_recv()

        @pl.when(not_first)
        def _():
            loss_back().start()

        loss_peer().start()

    @pl.when(even_core)
    def _():
        loss_peer().wait_recv()

    live_count = (start * lax.axis_size("dp")).astype(F32)
    loss_ref[0, 0] = loss_all[0, 0] / live_count
    for lane, owner in arrivals:
        n_wait(lane, owner).wait_recv()
        d_wait(lane, owner).wait_recv()

    gather_sent()

    @pl.when(odd_core)
    def _():
        for layer in range(2):
            for lane in (1, 2, 3):
                sent(normed.at[0, :, :, 0:share], n_send.at[layer, lane])
        sent(normed.at[0, :, :, 0:share], n_send.at[0, 0])
        n_local(1).wait()

        @pl.when(late)
        def _():
            for i, ref in enumerate([h_in, h_mid, pre.at[0], pre.at[1]]):
                sent(ref, peer_send.at[i])
            d_wait(0, y).wait_recv()

        @pl.when(not_last)
        def _():
            for j in range(CUTS):
                sent(h_out.at[:, :, cut(j)], h_send.at[j])

        @pl.when(last)
        def _():
            sent(h_out, peer_send.at[4])
            sent(dlog, peer_send.at[5])
            sent(stats, peer_send.at[6])
            for lane in (1, 2, 3):
                sent(loss_part, part_send.at[lane])

        @pl.when(not_first)
        def _():
            sent(loss_all, loss_send.at[0])

        sent(loss_all, loss_send.at[1])

    @pl.when(even_core)
    def _():
        n_wait(0, y).wait_recv()

        @pl.when(early)
        def _():
            d_wait(0, y).wait_recv()

    @pl.when(backward)
    def _():
        for layer in range(2):
            for lane in (1, 2, 3):
                sent(dpre.at[0], d_send.at[layer, lane])
        sent(dpre.at[0], local_sem.at[1])

        @pl.when(early)
        def _():
            sent(dpre.at[0], d_send.at[0, 0])

        @pl.when(late)
        def _():
            sent(dpre.at[0], d_send.at[1, 0])

        @pl.when(not_first)
        def _():
            for j in range(CUTS):
                sent(g_out.at[:, :, cut(j)], g_send.at[j])


def product_kernel(normed_ref, dpre_ref, out_ref, lefts, right, results, left_sem, right_sem, out_sem):
    parts, step = lefts.shape[0], lefts.shape[2]
    loads = [
        pltpu.make_async_copy(normed_ref.at[:, pl.ds(i * step, step)], lefts.at[i], left_sem.at[i])
        for i in range(parts)
    ]
    whole = pltpu.make_async_copy(dpre_ref, right, right_sem)
    loads[0].start()
    whole.start()
    for load in loads[1:]:
        load.start()
    stores = []
    for i in range(parts):
        loads[i].wait()
        turned = lefts[i].T
        if i == 0:
            whole.wait()
        results[i] = dot(turned, right[...])
        stores.append(
            pltpu.make_async_copy(results.at[i], out_ref.at[0, pl.ds(i * step, step), :], out_sem.at[i])
        )
        stores[-1].start()
    for store in stores:
        store.wait()


def product(normed, dpre):
    rows, share = normed.shape
    width = dpre.shape[1]
    step = min(256, share)
    parts = share // step
    hbm = pl.BlockSpec(memory_space=pl.ANY)
    return pl.pallas_call(
        product_kernel,
        name="weight_grad",
        out_shape=jax.ShapeDtypeStruct((1, share, width), F32),
        in_specs=[hbm, hbm],
        out_specs=hbm,
        scratch_shapes=[
            pltpu.VMEM((parts, rows, step), BF16),
            pltpu.VMEM((rows, width), BF16),
            pltpu.VMEM((parts, step, width), F32),
            pltpu.SemaphoreType.DMA((parts,)),
            pltpu.SemaphoreType.DMA,
            pltpu.SemaphoreType.DMA((parts,)),
        ],
        compiler_params=pltpu.CompilerParams(vmem_limit_bytes=60 * 1024 * 1024),
        cost_estimate=pl.CostEstimate(
            flops=2 * rows * share * width, bytes_accessed=6 * share * width, transcendentals=0
        ),
    )(normed, dpre)


def shards(
    video_ids,
    action_ids,
    target_ids,
    live_lengths,
    video_table,
    action_table,
    layer_gain,
    layer_weight,
    out_gain,
    head_weight,
    live_rows,
):
    width, vocab = head_weight.shape
    share = width // 4
    count = live_rows // ROWS

    vmem = pl.BlockSpec(memory_space=pltpu.VMEM)
    smem = pl.BlockSpec(memory_space=pltpu.SMEM)
    hbm = pl.BlockSpec(memory_space=pl.ANY)
    dma = pltpu.SemaphoreType.DMA
    rows = lambda kind: pltpu.VMEM((count, ROWS, width), kind)
    pair = lambda kind: pltpu.VMEM((2, count, ROWS, width), kind)
    loss, normed, dpre = pl.pallas_call(
        kernel,
        name="stack",
        out_shape=(
            jax.ShapeDtypeStruct((1, 1), F32),
            jax.ShapeDtypeStruct((4, count, ROWS, share), BF16),
            jax.ShapeDtypeStruct((4, count, ROWS, width), BF16),
        ),
        in_specs=[smem, vmem, vmem, vmem, vmem, vmem, vmem, hbm, hbm, hbm],
        out_specs=(smem, hbm, hbm),
        scratch_shapes=[
            pltpu.VMEM((2, width, width), BF16),
            pltpu.VMEM((2, width, width), BF16),
            pltpu.VMEM((width, vocab), BF16),
            pltpu.VMEM((vocab, width), BF16),
            rows(BF16),
            rows(BF16),
            rows(BF16),
            pair(F32),
            pair(BF16),
            pair(BF16),
            rows(BF16),
            rows(BF16),
            pltpu.VMEM((count, ROWS, vocab), BF16),
            pltpu.VMEM((count, 2, ROWS, 128), F32),
            pltpu.VMEM((ROWS, width), F32),
            pltpu.VMEM((ROWS, width), BF16),
            pltpu.VMEM((2, ROWS, width), F32),
            pltpu.VMEM((2, ROWS, 128), F32),
            pltpu.VMEM((2, 1, width), F32),
            pltpu.VMEM((live_rows, 128), jnp.int32),
            pltpu.VMEM((8, 128), F32),
            pltpu.VMEM((4, 8, 128), F32),
            pltpu.VMEM((8, 128), F32),
            dma((5, 4)),
            dma((2, 4, 4)),
            dma((2, 4)),
            dma((2, 4)),
            dma((2,)),
            dma((CUTS,)),
            dma((count, CUTS)),
            dma((CUTS,)),
            dma((count, CUTS)),
            dma((7,)),
            dma((7, count)),
            dma((2, 4)),
            dma((4,)),
            dma((2, 4)),
            dma((4,)),
            dma((4,)),
            dma((4,)),
            dma((2,)),
            dma((2,)),
            dma((1,)),
            dma((1,)),
            pltpu.VMEM((2, 4, 2, share // 8, width), BF16),
            dma((7, 2)),
            dma((2, 4, 2)),
            dma((2, 4, 2)),
            dma((2, 4, 2)),
            pltpu.SemaphoreType.REGULAR,
        ],
        compiler_params=pltpu.CompilerParams(
            collective_id=0, has_side_effects=True, vmem_limit_bytes=60 * 1024 * 1024
        ),
        cost_estimate=pl.CostEstimate(flops=10**10, bytes_accessed=2 * 10**7, transcendentals=0),
    )(
        live_lengths,
        video_ids,
        action_ids,
        target_ids,
        layer_gain,
        out_gain[None],
        action_table,
        video_table,
        layer_weight,
        head_weight,
    )
    grad = product(normed.reshape(4 * live_rows, share), dpre.reshape(4 * live_rows, width))
    return (loss[0, 0], grad)


def solution(mesh, live_rows=160):
    in_specs = (
        P("dp", None),
        P("dp", None),
        P("dp", None),
        P("dp", None),
        P(),
        P(),
        P("section", None),
        P("section", "dp", None),
        P(),
        P(),
    )
    out_specs = (P(), P("section", "dp", None))
    return jax.shard_map(
        functools.partial(shards, live_rows=live_rows),
        mesh=mesh,
        in_specs=in_specs,
        out_specs=out_specs,
        check_vma=False,
    )
```
